32 devices in a mesh: expert: 8 (over z, y), tensor: 4 (over x, core).
Axes of the slice: x: 2, y: 2, z: 4, core: 2. Of those that a mesh axis runs over, the one named last changes fastest.
Arguments:
- tokens: bfloat16 [8192, 1024], P('expert'), may hold values from -6 to 6
- cotangent: bfloat16 [8192, 1024], P('expert'), may hold values from -6 to 6
- routes: int32 [8192, 8], P('expert'), may hold values from 0 to 31, all different within a row; in each aligned block of 1024 rows (0 to 1023, 1024 to 2047, ...) at most 320 rows name the same one
- norm_gains: float32 [2, 1024], P(None, 'expert'), may hold values from 0.5 to 1.5
- gains_moment: float32 [2, 1024], P(None, 'expert'), may hold values from -64 to 64
- gains_second: float32 [2, 1024], P(None, 'expert'), may hold values from 4.096 to 65.536
- query_weight: float32 [1024, 1024], P('expert', 'tensor'), may hold values from -0.1875 to 0.1875
- query_moment: float32 [1024, 1024], P('expert', 'tensor'), may hold values from -16 to 16
- query_second: float32 [1024, 1024], P('expert', 'tensor'), may hold values from 0.36864 to 5.89824
- keyval_weight: float32 [2, 1024, 512], P(None, 'expert', 'tensor'), may hold values from -0.1875 to 0.1875
- keyval_moment: float32 [2, 1024, 512], P(None, 'expert', 'tensor'), may hold values from -32 to 32
- keyval_second: float32 [2, 1024, 512], P(None, 'expert', 'tensor'), may hold values from 1.024 to 16.384
- output_weight: float32 [1024, 1024], P('tensor', 'expert'), may hold values from -0.5 to 0.5
- output_moment: float32 [1024, 1024], P('tensor', 'expert'), may hold values from -16 to 16
- output_second: float32 [1024, 1024], P('tensor', 'expert'), may hold values from 0.36864 to 5.89824
- router_weight: float32 [1024, 32], P('expert'), may hold values from -0.09375 to 0.09375
- router_moment: float32 [1024, 32], P('expert'), may hold values from -320 to 320
- router_second: float32 [1024, 32], P('expert'), may hold values from 102.4 to 1638.4
- gateup_weight: float32 [32, 2, 1024, 512], P('expert', None, None, 'tensor'), may hold values from -0.1875 to 0.1875
- gateup_moment: float32 [32, 2, 1024, 512], P('expert', None, None, 'tensor'), may hold values from -16 to 16
- gateup_second: float32 [32, 2, 1024, 512], P('expert', None, None, 'tensor'), may hold values from 0.256 to 4.096
- down_weight: float32 [32, 512, 1024], P('expert', 'tensor'), may hold values from -1 to 1
- down_moment: float32 [32, 512, 1024], P('expert', 'tensor'), may hold values from -3 to 3
- down_second: float32 [32, 512, 1024], P('expert', 'tensor'), may hold values from 0.01024 to 0.16384
Outputs:
- block_out: bfloat16 [8192, 1024], P('expert')
- input_grad: bfloat16 [8192, 1024], P('expert')
- new_gains: float32 [2, 1024], P(None, 'expert')
- new_gains_moment: float32 [2, 1024], P(None, 'expert')
- new_gains_second: float32 [2, 1024], P(None, 'expert')
- new_query: float32 [1024, 1024], P('expert', 'tensor')
- new_query_moment: float32 [1024, 1024], P('expert', 'tensor')
- new_query_second: float32 [1024, 1024], P('expert', 'tensor')
- new_keyval: float32 [2, 1024, 512], P(None, 'expert', 'tensor')
- new_keyval_moment: float32 [2, 1024, 512], P(None, 'expert', 'tensor')
- new_keyval_second: float32 [2, 1024, 512], P(None, 'expert', 'tensor')
- new_output: float32 [1024, 1024], P('tensor', 'expert')
- new_output_moment: float32 [1024, 1024], P('tensor', 'expert')
- new_output_second: float32 [1024, 1024], P('tensor', 'expert')
- new_router: float32 [1024, 32], P('expert')
- new_router_moment: float32 [1024, 32], P('expert')
- new_router_second: float32 [1024, 32], P('expert')
- new_gateup: float32 [32, 2, 1024, 512], P('expert', None, None, 'tensor')
- new_gateup_moment: float32 [32, 2, 1024, 512], P('expert', None, None, 'tensor')
- new_gateup_second: float32 [32, 2, 1024, 512], P('expert', None, None, 'tensor')
- new_down: float32 [32, 512, 1024], P('expert', 'tensor')
- new_down_moment: float32 [32, 512, 1024], P('expert', 'tensor')
- new_down_second: float32 [32, 512, 1024], P('expert', 'tensor')
The draws below stay inside these ranges and needn't reach their ends.
Inputs may be any that keep to these rules, and one draw needn't show every extreme that they name: `routes`: each row names 8 different experts. In each aligned block of 1024 rows (the rows of one device) no expert is named by more than 320 rows, a bound that some block reaches.
All inputs are finite; a program needn't handle non-finite values.
Results may differ from the reference program's by a relative error of at most 0.025.
Values may be sent and summed in bfloat16 or wider, within the bound.
No kernel may reach another device: no remote copies, remote signals or barrier semaphores. Data moves between devices by JAX's collectives and lax.ppermute only.
A program may use at most 384 MiB of HBM per device.

```python
import math
import jax
import jax.numpy as jnp
import numpy as np
from jax import lax

D = 1024
HEADS = 16
KV_HEADS = 8
HD = 64
FF = 512
EXPERTS = 32
TOPK = 8
STEP = 10
TOK_DEV = 1024
CAP = 320
TOKENS = 8192


def block_scale(key, shape, pieces, low, largest):
    def one(position, blocks):
        steps = jax.random.uniform(jax.random.fold_in(jax.random.fold_in(key, 6), position), (blocks,), jnp.float32, low / len(pieces), largest / len(pieces))
        return jnp.repeat(jnp.exp(steps), shape[position] // blocks).reshape((-1,) + (1,) * (len(shape) - position - 1))

    factor_of = one(*pieces[0])
    for cut in pieces[1:]:
        factor_of = factor_of * one(*cut)
    return factor_of


def deal_out(key, own, number, rows, count, top, bound, skew):
    order = jax.random.permutation(key, count)
    heavy_load, ordinary = shares(count, rows * top, bound, skew, True), shares(count, rows * top, bound, skew, False)
    places = jnp.arange(count)

    def named(lengths, offset_by):
        used = int((lengths > 0).sum())
        fixed = max(1, used // 4)
        moved = fixed + (places - fixed + offset_by * (used - fixed)) % max(1, count - fixed)
        return jnp.zeros((count,), jnp.int32).at[order[jnp.where(places < fixed, places, moved)]].set(jnp.asarray(lengths, jnp.int32))

    lengths = jnp.where(number % 4 == 0, named(heavy_load, number // 4), named(ordinary, number - number // 4 - 1))
    mixed = jax.random.permutation(jax.random.fold_in(own, 3), count)
    source_of, receiver = mixed[0:count // 2 * 2:2], mixed[1:count // 2 * 2:2]
    margin = jnp.minimum(lengths[source_of] - 1, bound - lengths[receiver]) // 2
    margin = jnp.where((source_of == order[0]) | (receiver == order[0]) | (lengths[receiver] == 0), 0, jnp.maximum(margin, 0))
    moved = jax.random.randint(jax.random.fold_in(own, 4), (count // 2,), 0, 1 << 20) % (margin + 1)
    lengths = lengths.at[source_of].add(-moved).at[receiver].add(moved)
    labels = jnp.searchsorted(jnp.cumsum(lengths), jnp.arange(rows * top), side="right").astype(jnp.int32)
    listing = labels.reshape(top, rows).T
    listing = listing[jax.random.permutation(jax.random.fold_in(own, 1), rows)]
    offset_by = jax.random.randint(jax.random.fold_in(own, 2), (rows, 1), 0, top)
    return jnp.take_along_axis(listing, (jnp.arange(top)[None, :] + offset_by) % top, axis=1)


def shares(number_of, total, most, skew, full):
    loads = [(1 << 20) // math.isqrt(standing ** skew) + 1 for standing in range(1, number_of + 1)]
    largest = most if full else min(most, max(-(-total // number_of), total * loads[0] // sum(loads)))
    least = 1 if total - largest >= number_of - 1 else 0
    given, surplus = [largest] + [least] * (number_of - 1), total - largest - least * (number_of - 1)
    while surplus > 0:
        candidates = [i for i in range(1, number_of) if given[i] < largest] or [i for i in range(1, number_of) if given[i] < most]
        mass, remaining = sum([loads[i] for i in candidates]), surplus
        for i in candidates:
            addition = min(most - given[i], max(1, remaining * loads[i] // mass), surplus)
            given[i] = given[i] + addition
            surplus = surplus - addition
    return np.array(given)


def normal_values(own_key, shape, scale, most, cuts=(), kind=jnp.bfloat16):
    values = jax.random.normal(own_key, shape, jnp.float32) * scale
    if len(cuts) > 0:
        values = block_scale(own_key, shape, cuts, -0.22, 0.18) * values
    return jnp.clip(values, min=-most, max=most).astype(kind)


def setup_inputs(seed: int = 0) -> dict:
    key_of = jax.random.split(jax.random.key(seed), 25)
    tokens = normal_values(key_of[0], (TOKENS, D), 1.0, 6.0, ((0, 8),))
    cotangent = normal_values(key_of[1], (TOKENS, D), 1.0, 6.0, ((0, 8),))
    routes_keys = jax.random.split(jax.random.fold_in(key_of[2], 1), TOKENS // TOK_DEV)
    routes_turns = jax.random.permutation(jax.random.fold_in(key_of[2], 3), TOKENS // TOK_DEV)
    routes = jax.vmap(lambda own, number: deal_out(jax.random.fold_in(key_of[2], 2), own, number, TOK_DEV, EXPERTS, TOPK, CAP, 1))(routes_keys, routes_turns).reshape((TOKENS, TOPK))
    norm_gains = jnp.clip(1.0 + 0.1 * jax.random.normal(key_of[3], (2, D), jnp.float32), 0.5, 1.5)
    gains_moment = normal_values(key_of[4], (2, D), (0.11 * TOKENS ** 0.5), 64.0, ((1, 8),), jnp.float32)
    gains_second = jnp.clip(jnp.exp(math.log(65.536) - 2.7725887 * jax.random.uniform(key_of[5], (2, D), jnp.float32) ** block_scale(key_of[5], (2, D), ((1, 8),), -0.2, 0.2)), 4.096, 65.536)
    query_weight = normal_values(key_of[6], (D, HEADS * HD), D ** -0.5, 0.1875, ((0, 8), (1, 4)), jnp.float32)
    query_moment = normal_values(key_of[7], (D, HEADS * HD), (0.033 * TOKENS ** 0.5), 16.0, ((0, 8), (1, 4)), jnp.float32)
    query_second = jnp.clip(jnp.exp(math.log(5.89824) - 2.7725887 * jax.random.uniform(key_of[8], (D, HEADS * HD), jnp.float32) ** block_scale(key_of[8], (D, HEADS * HD), ((0, 8), (1, 4)), -0.2, 0.2)), 0.36864, 5.89824)
    keyval_weight = normal_values(key_of[9], (2, D, KV_HEADS * HD), D ** -0.5, 0.1875, ((1, 8), (2, 4)), jnp.float32)
    keyval_moment = normal_values(key_of[10], (2, D, KV_HEADS * HD), (0.055 * TOKENS ** 0.5), 32.0, ((1, 8), (2, 4)), jnp.float32)
    keyval_second = jnp.clip(jnp.exp(math.log(16.384) - 2.7725887 * jax.random.uniform(key_of[11], (2, D, KV_HEADS * HD), jnp.float32) ** block_scale(key_of[11], (2, D, KV_HEADS * HD), ((1, 8), (2, 4)), -0.2, 0.2)), 1.024, 16.384)
    output_weight = normal_values(key_of[12], (HEADS * HD, D), (HEADS * HD // 8) ** -0.5, 0.5, ((0, 4), (1, 8)), jnp.float32)
    output_moment = normal_values(key_of[13], (HEADS * HD, D), (0.033 * TOKENS ** 0.5), 16.0, ((0, 4), (1, 8)), jnp.float32)
    output_second = jnp.clip(jnp.exp(math.log(5.89824) - 2.7725887 * jax.random.uniform(key_of[14], (HEADS * HD, D), jnp.float32) ** block_scale(key_of[14], (HEADS * HD, D), ((0, 4), (1, 8)), -0.2, 0.2)), 0.36864, 5.89824)
    router_weight = normal_values(key_of[15], (D, EXPERTS), (4 * D) ** -0.5, 0.09375, ((0, 8),), jnp.float32)
    router_moment = normal_values(key_of[16], (D, EXPERTS), (0.55 * TOKENS ** 0.5), 320.0, ((0, 8),), jnp.float32)
    router_second = jnp.clip(jnp.exp(math.log(1638.4) - 2.7725887 * jax.random.uniform(key_of[17], (D, EXPERTS), jnp.float32) ** block_scale(key_of[17], (D, EXPERTS), ((0, 8),), -0.2, 0.2)), 102.4, 1638.4)
    gateup_weight = normal_values(key_of[18], (EXPERTS, 2, D, FF), D ** -0.5, 0.1875, ((0, 8), (3, 4)), jnp.float32)
    gateup_moment = normal_values(key_of[19], (EXPERTS, 2, D, FF), (0.055 * (TOKENS * TOPK // EXPERTS) ** 0.5), 16.0, ((0, 8), (3, 4)), jnp.float32)
    gateup_second = jnp.clip(jnp.exp(math.log(4.096) - 2.7725887 * jax.random.uniform(key_of[20], (EXPERTS, 2, D, FF), jnp.float32) ** block_scale(key_of[20], (EXPERTS, 2, D, FF), ((0, 8), (3, 4)), -0.2, 0.2)), 0.256, 4.096)
    down_weight = normal_values(key_of[21], (EXPERTS, FF, D), (FF // 16) ** -0.5, 1.0, ((0, 8), (1, 4)), jnp.float32)
    down_moment = normal_values(key_of[22], (EXPERTS, FF, D), (0.011 * (TOKENS * TOPK // EXPERTS) ** 0.5), 3.0, ((0, 8), (1, 4)), jnp.float32)
    down_second = jnp.clip(jnp.exp(math.log(0.16384) - 2.7725887 * jax.random.uniform(key_of[23], (EXPERTS, FF, D), jnp.float32) ** block_scale(key_of[23], (EXPERTS, FF, D), ((0, 8), (1, 4)), -0.2, 0.2)), 0.01024, 0.16384)
    return {"tokens": tokens, "cotangent": cotangent, "routes": routes, "norm_gains": norm_gains, "gains_moment": gains_moment, "gains_second": gains_second, "query_weight": query_weight, "query_moment": query_moment, "query_second": query_second, "keyval_weight": keyval_weight, "keyval_moment": keyval_moment, "keyval_second": keyval_second, "output_weight": output_weight, "output_moment": output_moment, "output_second": output_second, "router_weight": router_weight, "router_moment": router_moment, "router_second": router_second, "gateup_weight": gateup_weight, "gateup_moment": gateup_moment, "gateup_second": gateup_second, "down_weight": down_weight, "down_moment": down_moment, "down_second": down_second}


NORM_EPS = 1e-06
BETA_ONE = 0.9
BETA_TWO = 0.999
ADAM_EPS = 1e-08
MATRIX_RATE = 0.08
GAIN_RATE = 0.6
MATRIX_DECAY = 0.1
NEG_LARGE = -1e+30
HIGH = lax.Precision.HIGHEST

@jax.custom_vjp
def low(v):
    return lax.optimization_barrier(v.astype(jnp.bfloat16)).astype(jnp.float32)

@jax.custom_vjp
def low_back(v):
    return v

def low_keep(v):
    return (low(v), None)

def low_pass(kept, grad):
    return (grad,)

def back_keep(v):
    return (v, None)

def back_low(kept, grad):
    return (low(grad),)
low.defvjp(low_keep, low_pass)
low_back.defvjp(back_keep, back_low)

def rms_norm(values, gain):
    return values * lax.rsqrt(lax.optimization_barrier(jnp.mean(values * values, axis=-1, keepdims=True)) + NORM_EPS) * gain

def rope_tables(length, head_size):
    half_size = head_size // 2
    frequency = 10000.0 ** (-(jnp.arange(half_size, dtype=jnp.float32) * 2.0) / head_size)
    angles = jnp.arange(length, dtype=jnp.float32)[:, None] * frequency[None, :]
    return (jnp.cos(angles), jnp.sin(angles))

def rotate(values, cosine_table, sine_table):
    half_size = values.shape[-1] // 2
    first_half = values[..., :half_size]
    second_half = values[..., half_size:]
    c = cosine_table[:, None, :]
    s = sine_table[:, None, :]
    return jnp.concatenate([first_half * c - second_half * s, second_half * c + first_half * s], axis=-1)

def slot_targets(routes):
    flat_ids = routes.reshape(-1)
    onehot = (flat_ids[:, None] == jnp.arange(EXPERTS, dtype=jnp.int32)[None, :]).astype(jnp.int32)
    slot_index = lax.optimization_barrier(jnp.sum(jnp.cumsum(onehot, axis=0) * onehot, axis=1)) - 1
    return flat_ids * CAP + slot_index

def sequence_forward(weights, x, routes):
    norm_gains, query_weight, keyval_weight, output_weight, router_weight, gateup_weight, down_weight = weights
    length = x.shape[0]
    groups = HEADS // KV_HEADS
    query_low = low(query_weight)
    keyval_low = low(keyval_weight)
    output_low = low(output_weight)
    router_low = low(router_weight)
    gateup_low = low(gateup_weight)
    down_low = low(down_weight)
    a = low(rms_norm(x, norm_gains[0]))
    query_pre = low_back(jnp.dot(a, query_low, precision=HIGH))
    key_pre = low_back(jnp.dot(a, keyval_low[0], precision=HIGH))
    value_pre = low_back(jnp.dot(a, keyval_low[1], precision=HIGH))
    cosine_table, sine_table = rope_tables(length, HD)
    q = low(rotate(query_pre.reshape(length, HEADS, HD), cosine_table, sine_table))
    k = low(rotate(key_pre.reshape(length, KV_HEADS, HD), cosine_table, sine_table))
    v = low(value_pre.reshape(length, KV_HEADS, HD))
    q = q.reshape(length, KV_HEADS, groups, HD)
    scores = low_back(jnp.einsum('qhgd,khd->hgqk', q, k, precision=HIGH) * HD ** (-0.5))
    causal = jnp.arange(length)[:, None] >= jnp.arange(length)[None, :]
    scores = jnp.where(causal, scores, NEG_LARGE)
    weights_attn = jax.nn.softmax(scores, axis=-1)
    mixture = jnp.einsum('hgqk,khd->qhgd', low(weights_attn), v, precision=HIGH).reshape(length, HEADS * HD)
    mixture = low(low_back(mixture))
    attention = low_back(jnp.dot(mixture, output_low, precision=HIGH))
    x_mid = x + attention
    b = low(rms_norm(x_mid, norm_gains[1]))
    logits = low_back(jnp.dot(b, router_low, precision=HIGH))
    chosen = jnp.take_along_axis(logits, routes, axis=1)
    gating = jax.nn.softmax(chosen, axis=-1)
    targets = slot_targets(routes)
    repeated = low_back(jnp.repeat(b, TOPK, axis=0))
    buffer = jnp.zeros((EXPERTS * CAP, D), jnp.float32).at[targets].set(repeated).reshape(EXPERTS, CAP, D)
    gate_pre = low_back(jnp.einsum('erd,edf->erf', buffer, gateup_low[:, 0], precision=HIGH))
    up_pre = low_back(jnp.einsum('erd,edf->erf', buffer, gateup_low[:, 1], precision=HIGH))
    activation = low(jax.nn.silu(gate_pre) * up_pre)
    expert_out = low(low_back(jnp.einsum('erf,efd->erd', activation, down_low, precision=HIGH)))
    picked = expert_out.reshape(EXPERTS * CAP, D)[targets].reshape(length, TOPK, D)
    return x_mid + lax.optimization_barrier(jnp.sum(gating[:, :, None] * picked, axis=1))

def adamw_update(weight, moment, second, gradient, rate, decay):
    moment_new = BETA_ONE * moment + (1.0 - BETA_ONE) * gradient
    second_new = BETA_TWO * second + (1.0 - BETA_TWO) * gradient * gradient
    fix_one = 1.0 - BETA_ONE ** STEP
    fix_two = 1.0 - BETA_TWO ** STEP
    update = moment_new / fix_one / (jnp.sqrt(second_new / fix_two) + ADAM_EPS)
    return (weight - rate * (update + decay * weight), moment_new, second_new)

def reference(tokens, cotangent, routes, norm_gains, gains_moment, gains_second, query_weight, query_moment, query_second, keyval_weight, keyval_moment, keyval_second, output_weight, output_moment, output_second, router_weight, router_moment, router_second, gateup_weight, gateup_moment, gateup_second, down_weight, down_moment, down_second):
    params = (norm_gains, query_weight, keyval_weight, output_weight, router_weight, gateup_weight, down_weight)
    sequences = tokens.shape[0] // TOK_DEV
    inputs = tokens.astype(jnp.float32).reshape(sequences, TOK_DEV, D)
    route_blocks = routes.reshape(sequences, TOK_DEV, TOPK)

    def forward(weights, inputs):

        def one_sequence(sequence_pair):
            return sequence_forward(weights, sequence_pair[0], sequence_pair[1])
        return lax.map(jax.checkpoint(one_sequence), (inputs, route_blocks))
    outputs, pullback = jax.vjp(forward, params, inputs)
    gradients, input_grad = pullback(cotangent.astype(jnp.float32).reshape(sequences, TOK_DEV, D))
    block_out = outputs.reshape(-1, D).astype(jnp.bfloat16)
    input_grad = input_grad.reshape(-1, D).astype(jnp.bfloat16)
    gains_grad, query_grad, keyval_grad, output_grad, router_grad, gateup_grad, down_grad = gradients
    new_gains = adamw_update(norm_gains, gains_moment, gains_second, gains_grad, GAIN_RATE, 0.0)
    new_query = adamw_update(query_weight, query_moment, query_second, query_grad, MATRIX_RATE, MATRIX_DECAY)
    new_keyval = adamw_update(keyval_weight, keyval_moment, keyval_second, keyval_grad, MATRIX_RATE, MATRIX_DECAY)
    new_output = adamw_update(output_weight, output_moment, output_second, output_grad, MATRIX_RATE, MATRIX_DECAY)
    new_router = adamw_update(router_weight, router_moment, router_second, router_grad, MATRIX_RATE, MATRIX_DECAY)
    new_gateup = adamw_update(gateup_weight, gateup_moment, gateup_second, gateup_grad, MATRIX_RATE, MATRIX_DECAY)
    new_down = adamw_update(down_weight, down_moment, down_second, down_grad, MATRIX_RATE, MATRIX_DECAY)
    return (block_out, input_grad, new_gains[0], new_gains[1], new_gains[2], new_query[0], new_query[1], new_query[2], new_keyval[0], new_keyval[1], new_keyval[2], new_output[0], new_output[1], new_output[2], new_router[0], new_router[1], new_router[2], new_gateup[0], new_gateup[1], new_gateup[2], new_down[0], new_down[1], new_down[2])
```

```python
import functools

import jax
import jax.numpy as jnp
from jax import lax
from jax.experimental import pallas as pl
from jax.experimental.pallas import tpu as pltpu
from jax.sharding import PartitionSpec as P

HEADS = 16
KV_HEADS = 8
HD = 64
EXPERTS = 32
STEP = 10
PAD = 128

NORM_EPS = 1e-06
BETA_ONE = 0.9
BETA_TWO = 0.999
ADAM_EPS = 1e-08
MATRIX_RATE = 0.08
GAIN_RATE = 0.6
MATRIX_DECAY = 0.1
NEG_LARGE = -1e30
BF = jnp.bfloat16
F32 = jnp.float32


def dot(left, right, dims):
    return lax.dot_general(left, right, (dims, ((), ())), preferred_element_type=F32)


def normalize(values):
    inverse = lax.rsqrt(jnp.mean(values * values, axis=-1, keepdims=True) + NORM_EPS)
    return (values * inverse, inverse)


def norm_backward(grad_unit, unit, inverse):
    return inverse * (grad_unit - unit * jnp.mean(grad_unit * unit, axis=-1, keepdims=True))


def rope_tables(length, head_size):
    half_size = head_size // 2
    frequency = 10000.0 ** (-(jnp.arange(half_size, dtype=F32) * 2.0) / head_size)
    angles = jnp.arange(length, dtype=F32)[:, None] * frequency[None, :]
    return (jnp.cos(angles), jnp.sin(angles))


def rotate(values, cosine_table, sine_table):
    half_size = values.shape[-1] // 2
    first_half = values[..., :half_size]
    second_half = values[..., half_size:]
    c = cosine_table[:, None, :]
    s = sine_table[:, None, :]
    return jnp.concatenate(
        [first_half * c - second_half * s, second_half * c + first_half * s], axis=-1
    )


def unrotate(values, cosine_table, sine_table):
    return rotate(values, cosine_table, -sine_table)


def adamw_update(weight, moment, second, gradient, rate, decay):
    moment_new = BETA_ONE * moment + (1.0 - BETA_ONE) * gradient
    second_new = BETA_TWO * second + (1.0 - BETA_TWO) * gradient * gradient
    fix_one = 1.0 - BETA_ONE**STEP
    fix_two = 1.0 - BETA_TWO**STEP
    update = moment_new / fix_one / (jnp.sqrt(second_new / fix_two) + ADAM_EPS)
    return (weight - rate * (update + decay * weight), moment_new, second_new)


def split_pieces(values, count):
    pieces = []
    for _ in range(count):
        high = lax.reduce_precision(values, 8, 7)
        pieces.append(high.astype(BF))
        values = values - high
    return pieces


def ring_order(size):
    return list(range(0, size, 2)) + list(range(1, size, 2))[::-1]


def ring_perm(size, step):
    order = ring_order(size)
    return [(order[i], order[(i + step) % size]) for i in range(size)]


def ring_index(size, offset):
    me = lax.axis_index("expert")
    place = jnp.where(me % 2 == 0, me // 2, size - 1 - me // 2)
    place = (place + offset) % size
    return jnp.where(place < (size + 1) // 2, 2 * place, 2 * (size - 1 - place) + 1)


def ring_gather(block, size):
    blocks = {0: block}
    ahead = behind = block
    for hop in range(1, size // 2 + 1):
        ahead = lax.ppermute(ahead, "expert", ring_perm(size, 1))
        blocks[-hop] = ahead
        if hop <= (size - 1) // 2:
            behind = lax.ppermute(behind, "expert", ring_perm(size, -1))
            blocks[hop] = behind
    return blocks


def ring_reduce(part, size):
    down = up = None
    for hop in range(size // 2, 0, -1):
        mine = part(-hop).astype(F32)
        total = mine if down is None else down.astype(F32) + mine
        down = lax.ppermute(total.astype(BF), "expert", ring_perm(size, -1))
        side = hop - 1 if size % 2 == 0 else hop
        if side > 0:
            mine = part(side).astype(F32)
            total = mine if up is None else up.astype(F32) + mine
            up = lax.ppermute(total.astype(BF), "expert", ring_perm(size, 1))
    total = part(0).astype(F32) + down.astype(F32)
    return total if up is None else total + up.astype(F32)


def tensor_perm(size, along, core):
    chips = size // 2
    return [(t, ((t // 2 + along) % chips) * 2 + ((t % 2) ^ core)) for t in range(size)]


def tensor_gather(shard, size):
    own = [shard] + [
        lax.ppermute(shard, "tensor", tensor_perm(size, -step, 0)) for step in range(1, size // 2)
    ]
    other = [lax.ppermute(piece, "tensor", tensor_perm(size, 0, 1)) for piece in own]
    return own + other


def tensor_reduce(parts, size):
    chips = size // 2
    sums = []
    for step in range(chips):
        came = lax.ppermute(parts[chips + step], "tensor", tensor_perm(size, 0, 1))
        sums.append(parts[step].astype(F32) + came.astype(F32))
    total = sums[0]
    for step in range(1, chips):
        came = lax.ppermute(sums[step].astype(BF), "tensor", tensor_perm(size, step, 0))
        total = total + came.astype(F32)
    return total


def tensor_sum(values, size):
    values = values + lax.ppermute(values, "tensor", tensor_perm(size, 0, 1))
    moved = [
        lax.ppermute(values, "tensor", tensor_perm(size, step, 0)) for step in range(1, size // 2)
    ]
    return sum(moved, values)


def expert_kernel(
    first_ref,
    one_ref,
    two_ref,
    dy_one_ref,
    dy_two_ref,
    gateup_ref,
    down_ref,
    grads_ref,
    scaled_ref,
    y_one_ref,
    y_two_ref,
    back_one_ref,
    back_two_ref,
    rows_ref,
    dy_ref,
    y_acc,
    back_acc,
    tail_acc,
):
    expert = pl.program_id(0)
    count = pl.num_programs(0)
    rows, width = dy_one_ref.shape

    @pl.when(expert == 0)
    def _():
        rows_ref[:rows] = one_ref[...]
        rows_ref[rows:] = two_ref[...]
        dy_ref[:rows] = dy_one_ref[...]
        dy_ref[rows:] = dy_two_ref[...]
        y_acc[...] = jnp.zeros_like(y_acc)
        back_acc[...] = jnp.zeros_like(back_acc)
        tail_acc[...] = jnp.zeros_like(tail_acc)

    b = rows_ref[:, :width]
    dy = dy_ref[...]
    gate_w = gateup_ref[0, 0]
    up_w = gateup_ref[0, 1]
    down_w = down_ref[0]
    gate_pre = dot(b, gate_w, ((1,), (0,)))
    up_pre = dot(b, up_w, ((1,), (0,)))
    sig = jax.nn.sigmoid(gate_pre)
    silu = gate_pre * sig
    act = (silu * up_pre).astype(BF).astype(F32)
    grad_act = dot(dy, down_w, ((1,), (1,)))
    grad_gating = jnp.sum(act * grad_act, axis=1, keepdims=True)
    column = first_ref[0] + expert
    lane = lax.broadcasted_iota(jnp.int32, (2 * rows, PAD), 1)
    chosen = (lane == column) | (lane == column + EXPERTS)
    tail = rows_ref[:, width:].astype(F32)
    gating = jnp.sum(jnp.where(chosen, tail, 0.0), axis=1, keepdims=True)
    tail_acc[...] += jnp.where(chosen, grad_gating, 0.0)
    grad_act = grad_act * gating
    grad_gate = (grad_act * up_pre * (sig * (1.0 + gate_pre * (1.0 - sig)))).astype(BF)
    grad_up = (grad_act * silu).astype(BF)
    scaled = (act * gating).astype(BF)
    grads_ref[0, 0] = grad_gate
    grads_ref[1, 0] = grad_up
    scaled_ref[0] = scaled
    back_acc[...] += dot(grad_gate, gate_w, ((1,), (1,))) + dot(grad_up, up_w, ((1,), (1,)))
    y_acc[...] += dot(scaled, down_w, ((1,), (0,)))

    @pl.when(expert == count - 1)
    def _():
        y = y_acc[...].astype(BF)
        y_one_ref[...] = y[:rows]
        y_two_ref[...] = y[rows:]
        back = back_acc[...].astype(BF)
        total = tail_acc[...]
        high = total.astype(BF)
        low = (total - high.astype(F32)).astype(BF)
        ends = jnp.where(lane < EXPERTS, high.astype(F32), low.astype(F32)).astype(BF)
        back_one_ref[:, :width] = back[:rows]
        back_one_ref[:, width:] = ends[:rows]
        back_two_ref[:, :width] = back[rows:]
        back_two_ref[:, width:] = ends[rows:]


def expert_blocks(first, one, two, dy_one, dy_two, gateup, down):
    experts, _, width, hidden = gateup.shape
    rows = one.shape[0]
    message = one.shape[1]
    whole = lambda e, s: (0, 0)
    block = pl.BlockSpec((rows, message), whole)
    plain = pl.BlockSpec((rows, width), whole)
    return pl.pallas_call(
        expert_kernel,
        grid_spec=pltpu.PrefetchScalarGridSpec(
            num_scalar_prefetch=1,
            grid=(experts,),
            in_specs=[
                block,
                block,
                plain,
                plain,
                pl.BlockSpec((1, 2, width, hidden), lambda e, s: (e, 0, 0, 0)),
                pl.BlockSpec((1, hidden, width), lambda e, s: (e, 0, 0)),
            ],
            out_specs=[
                pl.BlockSpec((2, 1, 2 * rows, hidden), lambda e, s: (0, e, 0, 0)),
                pl.BlockSpec((1, 2 * rows, hidden), lambda e, s: (e, 0, 0)),
                plain,
                plain,
                block,
                block,
            ],
            scratch_shapes=[
                pltpu.VMEM((2 * rows, message), BF),
                pltpu.VMEM((2 * rows, width), BF),
                pltpu.VMEM((2 * rows, width), F32),
                pltpu.VMEM((2 * rows, width), F32),
                pltpu.VMEM((2 * rows, PAD), F32),
            ],
        ),
        out_shape=[
            jax.ShapeDtypeStruct((2, experts, 2 * rows, hidden), BF),
            jax.ShapeDtypeStruct((experts, 2 * rows, hidden), BF),
            jax.ShapeDtypeStruct((rows, width), BF),
            jax.ShapeDtypeStruct((rows, width), BF),
            jax.ShapeDtypeStruct((rows, message), BF),
            jax.ShapeDtypeStruct((rows, message), BF),
        ],
        compiler_params=pltpu.CompilerParams(vmem_limit_bytes=48 * 1024 * 1024),
        name="expert_blocks",
    )(first, one, two, dy_one, dy_two, gateup, down)


def gateup_grad_kernel(pairs, *refs):
    out_ref = refs[-1]
    total = None
    for pair in range(pairs):
        grads = refs[2 * pairs + pair][0, 0]
        rows = grads.shape[0] // 2
        for half in range(2):
            term = dot(refs[2 * pair + half][...], grads[half * rows : (half + 1) * rows], ((0,), (0,)))
            total = term if total is None else total + term
    out_ref[0, 0] = total.astype(BF)


def gateup_grad(inputs, grads):
    pairs = len(grads)
    _, experts, both, hidden = grads[0].shape
    rows = both // 2
    width = inputs[0].shape[1] - PAD
    return pl.pallas_call(
        functools.partial(gateup_grad_kernel, pairs),
        grid=(experts, 2),
        in_specs=[pl.BlockSpec((rows, width), lambda e, k: (0, 0))] * (2 * pairs)
        + [pl.BlockSpec((1, 1, both, hidden), lambda e, k: (k, e, 0, 0))] * pairs,
        out_specs=pl.BlockSpec((1, 1, width, hidden), lambda e, k: (e, k, 0, 0)),
        out_shape=jax.ShapeDtypeStruct((experts, 2, width, hidden), BF),
        compiler_params=pltpu.CompilerParams(vmem_limit_bytes=56 * 1024 * 1024),
        name="gateup_grad",
    )(*inputs, *grads)


def down_grad_kernel(pairs, *refs):
    out_ref = refs[-1]
    total = None
    for pair in range(pairs):
        scaled = refs[2 * pairs + pair][0]
        rows = scaled.shape[0] // 2
        for half in range(2):
            term = dot(scaled[half * rows : (half + 1) * rows], refs[2 * pair + half][...], ((0,), (0,)))
            total = term if total is None else total + term
    out_ref[0] = total.astype(BF)


def down_grad(outputs, scaled):
    pairs = len(scaled)
    experts, both, hidden = scaled[0].shape
    rows, width = outputs[0].shape
    return pl.pallas_call(
        functools.partial(down_grad_kernel, pairs),
        grid=(experts,),
        in_specs=[pl.BlockSpec((rows, width), lambda e: (0, 0))] * (2 * pairs)
        + [pl.BlockSpec((1, both, hidden), lambda e: (e, 0, 0))] * pairs,
        out_specs=pl.BlockSpec((1, hidden, width), lambda e: (e, 0, 0)),
        out_shape=jax.ShapeDtypeStruct((experts, hidden, width), BF),
        compiler_params=pltpu.CompilerParams(vmem_limit_bytes=56 * 1024 * 1024),
        name="down_grad",
    )(*outputs, *scaled)


def attention_forward(query_rot, key_rot, value_rot):
    length, local_groups, group_size, _ = query_rot.shape
    block_rows = min(512, length)
    mixture_parts = []
    lse_parts = []
    for begin in range(0, length, block_rows):
        end = begin + block_rows
        scores = jnp.einsum(
            "qhgd,khd->hgqk", query_rot[begin:end], key_rot[:end], preferred_element_type=F32
        ) * HD ** (-0.5)
        causal = (begin + jnp.arange(block_rows))[:, None] >= jnp.arange(end)[None, :]
        scores = jnp.where(causal, scores, NEG_LARGE)
        row_peak = jnp.max(scores, axis=-1, keepdims=True)
        exponent = jnp.exp(scores - row_peak)
        row_total = jnp.sum(exponent, axis=-1, keepdims=True)
        lse_parts.append(row_peak + jnp.log(row_total))
        weights_block = (exponent / row_total).astype(BF)
        mixture_parts.append(
            jnp.einsum("hgqk,khd->qhgd", weights_block, value_rot[:end], preferred_element_type=F32)
        )
    mixture = jnp.concatenate(mixture_parts, axis=0).reshape(length, -1).astype(BF)
    return mixture, lse_parts


def attention_backward(query_rot, key_rot, value_rot, lse_parts, grad_mixture):
    length, local_groups, group_size, _ = query_rot.shape
    block_rows = min(512, length)
    score_scale = HD ** (-0.5)
    grad_key = jnp.zeros((length, local_groups, HD), F32)
    grad_value = jnp.zeros((length, local_groups, HD), F32)
    grad_query_parts = []
    for index, begin in enumerate(range(0, length, block_rows)):
        end = begin + block_rows
        query_block = query_rot[begin:end]
        key_block = key_rot[:end]
        grad_block = grad_mixture[begin:end]
        scores = (
            jnp.einsum("qhgd,khd->hgqk", query_block, key_block, preferred_element_type=F32)
            * score_scale
        )
        causal = (begin + jnp.arange(block_rows))[:, None] >= jnp.arange(end)[None, :]
        weights_block = jnp.where(causal, jnp.exp(scores - lse_parts[index]), 0.0)
        grad_weights = jnp.einsum(
            "qhgd,khd->hgqk", grad_block, value_rot[:end], preferred_element_type=F32
        )
        row_delta = jnp.sum(weights_block * grad_weights, axis=-1, keepdims=True)
        grad_scores = (weights_block * (grad_weights - row_delta)).astype(BF)
        grad_query_parts.append(
            jnp.einsum("hgqk,khd->qhgd", grad_scores, key_block, preferred_element_type=F32)
            * score_scale
        )
        grad_key = grad_key.at[:end].add(
            jnp.einsum("hgqk,qhgd->khd", grad_scores, query_block, preferred_element_type=F32)
            * score_scale
        )
        grad_value = grad_value.at[:end].add(
            jnp.einsum(
                "hgqk,qhgd->khd", weights_block.astype(BF), grad_block, preferred_element_type=F32
            )
        )
    return jnp.concatenate(grad_query_parts, axis=0), grad_key, grad_value


def body(
    ring,
    tensors,
    tokens,
    cotangent,
    routes,
    norm_gains,
    gains_moment,
    gains_second,
    query_weight,
    query_moment,
    query_second,
    keyval_weight,
    keyval_moment,
    keyval_second,
    output_weight,
    output_moment,
    output_second,
    router_weight,
    router_moment,
    router_second,
    gateup_weight,
    gateup_moment,
    gateup_second,
    down_weight,
    down_moment,
    down_second,
):
    length, width = tokens.shape
    rows = length // tensors
    experts = gateup_weight.shape[0]
    shard = gateup_weight.shape[3]
    lane_t = lax.axis_index("tensor")
    own_rows = lambda array: lax.dynamic_slice_in_dim(array, lane_t * rows, rows, axis=0)

    q_cols = query_weight.shape[1]
    k_cols = keyval_weight.shape[2]
    o_cols = output_weight.shape[0]
    heads_cols = q_cols + 2 * k_cols
    gain_pieces = split_pieces(norm_gains.T, 3)
    packed = jnp.concatenate(
        [
            query_weight.astype(BF),
            keyval_weight[0].astype(BF),
            keyval_weight[1].astype(BF),
            output_weight.T.astype(BF),
            router_weight.astype(BF),
        ]
        + gain_pieces,
        axis=1,
    )
    packed = lax.all_gather(packed, "expert", axis=0, tiled=True)
    attn_low = packed[:, : heads_cols + o_cols]
    qkv_low = packed[:, :heads_cols]
    router_low = packed[:, heads_cols + o_cols : heads_cols + o_cols + EXPERTS]
    gains_at = heads_cols + o_cols + EXPERTS
    gains_all = (
        packed[:, gains_at : gains_at + 2].astype(F32)
        + packed[:, gains_at + 2 : gains_at + 4].astype(F32)
        + packed[:, gains_at + 4 : gains_at + 6].astype(F32)
    ).T

    gateup_low = jnp.concatenate(tensor_gather(gateup_weight.astype(BF), tensors), axis=3)
    down_low = jnp.concatenate(tensor_gather(down_weight.astype(BF), tensors), axis=1)
    dy_own = own_rows(cotangent)
    dy_blocks = ring_gather(dy_own, ring)
    attn_all = lax.all_gather(attn_low, "tensor")

    x = tokens.astype(F32)
    unit_one, inverse_one = normalize(x)
    a = (unit_one * gains_all[0]).astype(BF)
    pre = jnp.dot(a, qkv_low, preferred_element_type=F32)
    local_heads = q_cols // HD
    local_groups = k_cols // HD
    group_size = local_heads // local_groups
    cosine_table, sine_table = rope_tables(length, HD)
    query_rot = rotate(
        pre[:, :q_cols].reshape(length, local_heads, HD), cosine_table, sine_table
    ).astype(BF)
    query_rot = query_rot.reshape(length, local_groups, group_size, HD)
    key_rot = rotate(
        pre[:, q_cols : q_cols + k_cols].reshape(length, local_groups, HD), cosine_table, sine_table
    ).astype(BF)
    value_rot = pre[:, q_cols + k_cols :].astype(BF).reshape(length, local_groups, HD)
    mixture, lse_parts = attention_forward(query_rot, key_rot, value_rot)

    mixture_rows = lax.all_to_all(
        mixture.reshape(tensors, rows, o_cols), "tensor", split_axis=0, concat_axis=0, tiled=True
    )
    attention = sum(
        dot(mixture_rows[t], attn_all[t, :, heads_cols:], ((1,), (1,))) for t in range(tensors)
    )
    x_mid = own_rows(x) + attention
    unit_two, inverse_two = normalize(x_mid)
    b = (unit_two * gains_all[1]).astype(BF)
    logits = jnp.dot(b, router_low, preferred_element_type=F32)
    own_routes = own_rows(routes)
    routed = jnp.any(
        own_routes[:, :, None] == jnp.arange(EXPERTS, dtype=jnp.int32)[None, None, :], axis=1
    )
    masked = jnp.where(routed, logits, NEG_LARGE)
    exponent = jnp.where(routed, jnp.exp(masked - jnp.max(masked, axis=1, keepdims=True)), 0.0)
    gating = exponent / jnp.sum(exponent, axis=1, keepdims=True)
    message = jnp.concatenate(
        [b] + split_pieces(gating, 2) + [jnp.zeros((rows, PAD - 2 * EXPERTS), BF)], axis=1
    )
    blocks = ring_gather(message, ring)

    first = (lax.axis_index("expert") * experts).astype(jnp.int32).reshape(1)
    back = {}
    forth = {}
    grads = []
    scaled = []
    order = []
    for k in range(ring // 2):
        one = -(ring // 2 - k)
        two = ring // 2 - 1 - k
        order += [one, two]
        result = expert_blocks(
            first, blocks[one], blocks[two], dy_blocks[one], dy_blocks[two], gateup_low, down_low
        )
        grads.append(result[0])
        scaled.append(result[1])
        forth[one], forth[two] = result[2], result[3]
        back[one], back[two] = result[4], result[5]
    returned = ring_reduce(lambda offset: back[offset], ring)
    moe_sum = ring_reduce(lambda offset: forth[offset], ring)
    block_out = lax.all_gather(
        (x_mid + moe_sum).astype(BF), "tensor", axis=0, tiled=True
    )
    gateup_grads = gateup_grad([blocks[o] for o in order], grads)
    down_grads = down_grad([dy_blocks[o] for o in order], scaled)
    gateup_sum = tensor_reduce(
        [gateup_grads[..., j * shard : (j + 1) * shard] for j in range(tensors)], tensors
    )
    down_sum = tensor_reduce(
        [down_grads[:, j * shard : (j + 1) * shard] for j in range(tensors)], tensors
    )
    new_gateup = adamw_update(
        gateup_weight, gateup_moment, gateup_second, gateup_sum, MATRIX_RATE, MATRIX_DECAY
    )
    new_down = adamw_update(
        down_weight, down_moment, down_second, down_sum, MATRIX_RATE, MATRIX_DECAY
    )

    grad_gating = (
        returned[:, width : width + EXPERTS] + returned[:, width + EXPERTS : width + 2 * EXPERTS]
    )
    grad_logits = (
        gating * (grad_gating - jnp.sum(gating * grad_gating, axis=1, keepdims=True))
    ).astype(BF)
    grad_b = dot(grad_logits, router_low, ((1,), (1,))) + returned[:, :width]
    grad_mid = dy_own.astype(F32) + norm_backward(grad_b * gains_all[1], unit_two, inverse_two)
    grad_attention = grad_mid.astype(BF)
    grad_mixture = jnp.stack(
        [dot(grad_attention, attn_all[t, :, heads_cols:], ((1,), (0,))).astype(BF) for t in range(tensors)]
    )
    grad_mixture = lax.all_to_all(
        grad_mixture, "tensor", split_axis=0, concat_axis=0, tiled=True
    ).reshape(length, local_groups, group_size, HD)

    small = jnp.concatenate(
        [
            dot(b, grad_logits, ((0,), (0,))),
            jnp.sum(grad_b * unit_two, axis=0)[:, None],
        ],
        axis=1,
    )
    small = tensor_sum(small, tensors)
    grad_attention_all = lax.all_gather(grad_attention, "tensor", axis=0, tiled=True)
    early = jnp.concatenate(
        [dot(grad_attention_all, mixture, ((0,), (0,))), small], axis=1
    ).astype(BF)
    piece = width // ring
    cut = lambda array: lambda offset: lax.dynamic_slice_in_dim(
        array, ring_index(ring, offset) * piece, piece, axis=0
    )
    early_sum = ring_reduce(cut(early), ring)
    output_sum = early_sum[:, :o_cols].T
    router_sum = early_sum[:, o_cols : o_cols + EXPERTS]
    gain_two_sum = early_sum[:, o_cols + EXPERTS]

    grad_query, grad_key, grad_value = attention_backward(
        query_rot, key_rot, value_rot, lse_parts, grad_mixture
    )
    grad_query_low = (
        unrotate(grad_query.reshape(length, local_heads, HD), cosine_table, sine_table)
        .astype(BF)
        .reshape(length, q_cols)
    )
    grad_key_low = unrotate(grad_key, cosine_table, sine_table).astype(BF).reshape(length, k_cols)
    grad_value_low = grad_value.astype(BF).reshape(length, k_cols)
    grad_pre = jnp.concatenate([grad_query_low, grad_key_low, grad_value_low], axis=1)
    grad_pre_rows = lax.all_to_all(
        grad_pre.reshape(tensors, rows, heads_cols), "tensor", split_axis=0, concat_axis=0, tiled=True
    )
    late = dot(a, grad_pre, ((0,), (0,)))
    gain_one = jnp.sum(late * qkv_low.astype(F32), axis=1) / gains_all[0]
    gain_one = tensor_sum(gain_one[:, None], tensors)
    late = jnp.concatenate([late, gain_one], axis=1).astype(BF)
    late_sum = ring_reduce(cut(late), ring)
    grad_a = sum(
        dot(grad_pre_rows[t], attn_all[t, :, :heads_cols], ((1,), (1,))) for t in range(tensors)
    )
    input_grad = (
        grad_mid
        + norm_backward(grad_a * gains_all[0], own_rows(unit_one), own_rows(inverse_one))
    ).astype(BF)
    input_grad = lax.all_gather(input_grad, "tensor", axis=0, tiled=True)

    query_sum = late_sum[:, :q_cols]
    keyval_sum = jnp.stack(
        [late_sum[:, q_cols : q_cols + k_cols], late_sum[:, q_cols + k_cols : heads_cols]]
    )
    gains_sum = jnp.stack([late_sum[:, heads_cols], gain_two_sum])
    new_gains = adamw_update(norm_gains, gains_moment, gains_second, gains_sum, GAIN_RATE, 0.0)
    new_query = adamw_update(
        query_weight, query_moment, query_second, query_sum, MATRIX_RATE, MATRIX_DECAY
    )
    new_keyval = adamw_update(
        keyval_weight, keyval_moment, keyval_second, keyval_sum, MATRIX_RATE, MATRIX_DECAY
    )
    new_output = adamw_update(
        output_weight, output_moment, output_second, output_sum, MATRIX_RATE, MATRIX_DECAY
    )
    new_router = adamw_update(
        router_weight, router_moment, router_second, router_sum, MATRIX_RATE, MATRIX_DECAY
    )
    return (
        (block_out, input_grad)
        + tuple(new_gains)
        + tuple(new_query)
        + tuple(new_keyval)
        + tuple(new_output)
        + tuple(new_router)
        + tuple(new_gateup)
        + tuple(new_down)
    )


def solution(mesh):
    rows = P("expert", None)
    gains = P(None, "expert")
    query = P("expert", "tensor")
    keyval = P(None, "expert", "tensor")
    output = P("tensor", "expert")
    gateup = P("expert", None, None, "tensor")
    down = P("expert", "tensor", None)
    weights = tuple(
        spec for spec in (gains, query, keyval, output, rows, gateup, down) for _ in range(3)
    )
    return jax.shard_map(
        functools.partial(body, mesh.shape["expert"], mesh.shape["tensor"]),
        mesh=mesh,
        in_specs=(rows, rows, rows) + weights,
        out_specs=(rows, rows) + weights,
        check_vma=False,
    )
```

```python
import functools

import jax
import jax.numpy as jnp
from jax import lax
from jax.experimental import pallas as pl
from jax.experimental.pallas import tpu as pltpu
from jax.sharding import PartitionSpec as P

HEADS = 16
KV_HEADS = 8
HD = 64
EXPERTS = 32
STEP = 10
PAD = 128

NORM_EPS = 1e-06
BETA_ONE = 0.9
BETA_TWO = 0.999
ADAM_EPS = 1e-08
MATRIX_RATE = 0.08
GAIN_RATE = 0.6
MATRIX_DECAY = 0.1
NEG_LARGE = -1e30
BF = jnp.bfloat16
F32 = jnp.float32


def dot(left, right, dims):
    return lax.dot_general(left, right, (dims, ((), ())), preferred_element_type=F32)


def normalize(values):
    inverse = lax.rsqrt(jnp.mean(values * values, axis=-1, keepdims=True) + NORM_EPS)
    return (values * inverse, inverse)


def norm_backward(grad_unit, unit, inverse):
    return inverse * (grad_unit - unit * jnp.mean(grad_unit * unit, axis=-1, keepdims=True))


def rope_tables(length, head_size):
    half_size = head_size // 2
    frequency = 10000.0 ** (-(jnp.arange(half_size, dtype=F32) * 2.0) / head_size)
    angles = jnp.arange(length, dtype=F32)[:, None] * frequency[None, :]
    return (jnp.cos(angles), jnp.sin(angles))


def adamw_update(weight, moment, second, gradient, rate, decay):
    moment_new = BETA_ONE * moment + (1.0 - BETA_ONE) * gradient
    second_new = BETA_TWO * second + (1.0 - BETA_TWO) * gradient * gradient
    fix_one = 1.0 - BETA_ONE**STEP
    fix_two = 1.0 - BETA_TWO**STEP
    update = moment_new / fix_one / (jnp.sqrt(second_new / fix_two) + ADAM_EPS)
    return (weight - rate * (update + decay * weight), moment_new, second_new)


def split_pieces(values, count):
    pieces = []
    for _ in range(count):
        high = lax.reduce_precision(values, 8, 7)
        pieces.append(high.astype(BF))
        values = values - high
    return pieces


def ring_order(size):
    return list(range(0, size, 2)) + list(range(1, size, 2))[::-1]


def ring_perm(size, step):
    order = ring_order(size)
    return [(order[i], order[(i + step) % size]) for i in range(size)]


def ring_index(size, offset):
    me = lax.axis_index("expert")
    place = jnp.where(me % 2 == 0, me // 2, size - 1 - me // 2)
    place = (place + offset) % size
    return jnp.where(place < (size + 1) // 2, 2 * place, 2 * (size - 1 - place) + 1)


def ring_gather(block, size):
    blocks = {0: block}
    ahead = behind = block
    for hop in range(1, size // 2 + 1):
        ahead = lax.ppermute(ahead, "expert", ring_perm(size, 1))
        blocks[-hop] = ahead
        if hop <= (size - 1) // 2:
            behind = lax.ppermute(behind, "expert", ring_perm(size, -1))
            blocks[hop] = behind
    return blocks


def ring_reduce(part, size):
    down = up = None
    messages = []
    for hop in range(size // 2, 0, -1):
        mine = part(-hop)
        total = mine if down is None else (down.astype(F32) + mine.astype(F32)).astype(BF)
        messages.append(total)
        down = lax.ppermute(total, "expert", ring_perm(size, -1))
        side = hop - 1
        if side > 0:
            mine = part(side)
            total = mine if up is None else (up.astype(F32) + mine.astype(F32)).astype(BF)
            up = lax.ppermute(total, "expert", ring_perm(size, 1))
    return [part(0), down] + ([] if up is None else [up]), messages


def tensor_perm(size, along, core):
    chips = size // 2
    return [(t, ((t // 2 + along) % chips) * 2 + ((t % 2) ^ core)) for t in range(size)]


def tensor_gather(shard, size):
    own = [shard] + [
        lax.ppermute(shard, "tensor", tensor_perm(size, -step, 0)) for step in range(1, size // 2)
    ]
    other = [lax.ppermute(piece, "tensor", tensor_perm(size, 0, 1)) for piece in own]
    return own + other


def tensor_reduce(parts, size):
    chips = size // 2
    result = []
    for step in reversed(range(chips)):
        came = lax.ppermute(parts[chips + step], "tensor", tensor_perm(size, 0, 1))
        if step == 0:
            result += [parts[0], came]
        else:
            total = (parts[step].astype(F32) + came.astype(F32)).astype(BF)
            result.append(lax.ppermute(total, "tensor", tensor_perm(size, step, 0)))
    return result


def tensor_sum(values, size):
    values = values + lax.ppermute(values, "tensor", tensor_perm(size, 0, 1))
    moved = [
        lax.ppermute(values, "tensor", tensor_perm(size, step, 0)) for step in range(1, size // 2)
    ]
    return sum(moved, values)


def place_kernel(blocks, cuts, *refs):
    index_ref = refs[0]
    outs = refs[len(refs) - len(cuts) :]
    for block in range(blocks):
        source = refs[1 + block]
        size = source.shape[0]
        start = pl.multiple_of(index_ref[block] * size, size)
        for (low, high), out in zip(cuts, outs):
            out[pl.ds(start, size), :] = source[:, low:high]


def place(blocks, index, cuts=None, after=()):
    size, columns = blocks[0].shape
    cuts = cuts or [(0, columns)]
    count = len(blocks)
    vmem = pl.BlockSpec(memory_space=pltpu.VMEM)
    out = pl.pallas_call(
        functools.partial(place_kernel, count, cuts),
        in_specs=[pl.BlockSpec(memory_space=pltpu.SMEM)]
        + [vmem] * count
        + [pl.BlockSpec(memory_space=pl.ANY)] * len(after),
        out_specs=[vmem] * len(cuts),
        out_shape=[
            jax.ShapeDtypeStruct((count * size, high - low), blocks[0].dtype) for low, high in cuts
        ],
        compiler_params=pltpu.CompilerParams(vmem_limit_bytes=32 * 1024 * 1024),
        name="place",
    )(index, *blocks, *after)
    return out if len(cuts) > 1 else out[0]


def tensor_index(size):
    me = lax.axis_index("tensor")
    chips = size // 2
    chip, core = me // 2, me % 2
    own = [((chip + step) % chips) * 2 + core for step in range(chips)]
    other = [((chip + step) % chips) * 2 + (1 - core) for step in range(chips)]
    return jnp.stack(own + other).astype(jnp.int32)


def expert_kernel(count, afters, *refs):
    first_ref = refs[0]
    message_refs = refs[1 : 1 + count]
    cotangent_refs = refs[1 + count : 1 + 2 * count]
    gate_ref, up_ref, down_ref = refs[1 + 2 * count : 4 + 2 * count]
    outs = refs[4 + 2 * count + afters :]
    grads_ref, scaled_ref = outs[:2]
    y_refs = outs[2 : 2 + count]
    back_refs = outs[2 + count : 2 + 2 * count]
    rows_ref, dy_ref, y_acc, back_acc, tail_acc = outs[2 + 2 * count :]
    expert = pl.program_id(0)
    rows, width = cotangent_refs[0].shape

    @pl.when(expert == 0)
    def _():
        for i in range(count):
            rows_ref[i * rows : (i + 1) * rows] = message_refs[i][...]
            dy_ref[i * rows : (i + 1) * rows] = cotangent_refs[i][...]
        y_acc[...] = jnp.zeros_like(y_acc)
        back_acc[...] = jnp.zeros_like(back_acc)
        tail_acc[...] = jnp.zeros_like(tail_acc)

    gate_w = gate_ref[0]
    up_w = up_ref[0]
    down_w = down_ref[0]
    column = first_ref[0] + expert
    for i in range(count):
        part = slice(i * rows, (i + 1) * rows)
        b = rows_ref[part, :width]
        dy = dy_ref[part]
        gate_pre = dot(b, gate_w, ((1,), (0,)))
        up_pre = dot(b, up_w, ((1,), (0,)))
        sig = jax.nn.sigmoid(gate_pre)
        silu = gate_pre * sig
        act = (silu * up_pre).astype(BF).astype(F32)
        grad_act = dot(dy, down_w, ((1,), (1,)))
        grad_gating = jnp.sum(act * grad_act, axis=1, keepdims=True)
        lane = lax.broadcasted_iota(jnp.int32, (rows, PAD), 1)
        chosen = (lane == column) | (lane == column + EXPERTS)
        tail = rows_ref[part, width:].astype(F32)
        gating = jnp.sum(jnp.where(chosen, tail, 0.0), axis=1, keepdims=True)
        tail_acc[part] += jnp.where(chosen, grad_gating, 0.0)
        grad_act = grad_act * gating
        grad_gate = (grad_act * up_pre * (sig * (1.0 + gate_pre * (1.0 - sig)))).astype(BF)
        grad_up = (grad_act * silu).astype(BF)
        scaled = (act * gating).astype(BF)
        grads_ref[0, 0, part] = grad_gate
        grads_ref[1, 0, part] = grad_up
        scaled_ref[0, part] = scaled
        back_acc[part] += dot(grad_gate, gate_w, ((1,), (1,))) + dot(grad_up, up_w, ((1,), (1,)))
        y_acc[part] += dot(scaled, down_w, ((1,), (0,)))

    @pl.when(expert == pl.num_programs(0) - 1)
    def _():
        lane = lax.broadcasted_iota(jnp.int32, (rows, PAD), 1)
        for i in range(count):
            part = slice(i * rows, (i + 1) * rows)
            y_refs[i][...] = y_acc[part].astype(BF)
            total = tail_acc[part]
            high = total.astype(BF).astype(F32)
            back_refs[i][:, :width] = back_acc[part].astype(BF)
            back_refs[i][:, width:] = jnp.where(lane < EXPERTS, high, total - high).astype(BF)


def expert_blocks(first, messages, owners, cotangents, gate, up, down, after):
    experts, width, hidden = gate.shape
    rows, message = messages[0].shape
    count = len(messages)
    block = pl.BlockSpec((rows, message), lambda e, s: (0, 0))
    plain = pl.BlockSpec((rows, width), lambda e, s: (0, 0))
    owned = [pl.BlockSpec((rows, width), lambda e, s, i=i: (s[1 + i], 0)) for i in range(count)]
    shape = jax.ShapeDtypeStruct
    out = pl.pallas_call(
        functools.partial(expert_kernel, count, len(after)),
        grid_spec=pltpu.PrefetchScalarGridSpec(
            num_scalar_prefetch=1,
            grid=(experts,),
            in_specs=[block] * count
            + owned
            + [pl.BlockSpec((1, width, hidden), lambda e, s: (e, 0, 0))] * 2
            + [pl.BlockSpec((1, hidden, width), lambda e, s: (e, 0, 0))]
            + [pl.BlockSpec(memory_space=pl.ANY)] * len(after),
            out_specs=[
                pl.BlockSpec((2, 1, count * rows, hidden), lambda e, s: (0, e, 0, 0)),
                pl.BlockSpec((1, count * rows, hidden), lambda e, s: (e, 0, 0)),
            ]
            + [plain] * count
            + [block] * count,
            scratch_shapes=[
                pltpu.VMEM((count * rows, message), BF),
                pltpu.VMEM((count * rows, width), BF),
                pltpu.VMEM((count * rows, width), F32),
                pltpu.VMEM((count * rows, width), F32),
                pltpu.VMEM((count * rows, PAD), F32),
            ],
        ),
        out_shape=[
            shape((2, experts, count * rows, hidden), BF),
            shape((experts, count * rows, hidden), BF),
        ]
        + [shape((rows, width), BF)] * count
        + [shape((rows, message), BF)] * count,
        compiler_params=pltpu.CompilerParams(vmem_limit_bytes=48 * 1024 * 1024),
        cost_estimate=pl.CostEstimate(
            flops=12 * count * rows * experts * width * hidden,
            bytes_accessed=6 * experts * width * hidden,
            transcendentals=count * rows * experts * hidden,
        ),
        name="expert_blocks",
    )(jnp.stack([first] + owners), *messages, *cotangents, gate, up, down, *after)
    return out[0], out[1], out[2 : 2 + count], out[2 + count :]


def weight_grad_kernel(spots, swap, shards, afters, *refs):
    blocks = len(spots)
    outs = refs[len(refs) - shards :]
    total = None
    for block, (call, part, rows) in enumerate(spots):
        grads_ref = refs[1 + blocks + call]
        lead = (0,) * (len(grads_ref.shape) - 2)
        grads = grads_ref[lead + (slice(part * rows, (part + 1) * rows),)]
        pair = (grads, refs[1 + block][...]) if swap else (refs[1 + block][...], grads)
        term = dot(*pair, ((0,), (0,)))
        total = term if total is None else total + term
    total = total.astype(BF)
    size = total.shape[0 if swap else 1] // shards
    for i, out in enumerate(outs):
        cut = slice(i * size, (i + 1) * size)
        out[0] = total[cut] if swap else total[:, cut]


def weight_grad(inputs, owners, spots, grads, pick, swap, shards, after):
    lead = grads[0].ndim == 4
    experts, _, hidden = grads[0].shape[-3:]
    rows = spots[0][2]
    width = inputs[0].shape[1] - (PAD if lead else 0)
    blocks = len(inputs)
    shape = (hidden // shards, width) if swap else (width, hidden // shards)
    in_specs = [pl.BlockSpec((rows, width), lambda e, s, i=i: (s[i], 0)) for i in range(blocks)]
    for array in grads:
        if lead:
            in_specs.append(pl.BlockSpec((1, 1) + array.shape[2:], lambda e, s: (pick, e, 0, 0)))
        else:
            in_specs.append(pl.BlockSpec((1,) + array.shape[1:], lambda e, s: (e, 0, 0)))
    in_specs += [pl.BlockSpec(memory_space=pl.ANY)] * len(after)
    return pl.pallas_call(
        functools.partial(weight_grad_kernel, spots, swap, shards, len(after)),
        grid_spec=pltpu.PrefetchScalarGridSpec(
            num_scalar_prefetch=1,
            grid=(experts,),
            in_specs=in_specs,
            out_specs=[pl.BlockSpec((1,) + shape, lambda e, s: (e, 0, 0))] * shards,
        ),
        out_shape=[jax.ShapeDtypeStruct((experts,) + shape, BF)] * shards,
        compiler_params=pltpu.CompilerParams(vmem_limit_bytes=56 * 1024 * 1024),
        cost_estimate=pl.CostEstimate(
            flops=2 * blocks * rows * experts * width * hidden,
            bytes_accessed=4 * blocks * rows * width,
            transcendentals=0,
        ),
        name="weight_grad",
    )(owners, *inputs, *grads, *after)


def adamw_kernel(kinds, parts, *refs):
    weight_ref, moment_ref, second_ref = refs[:3]
    outs = refs[len(refs) - 3 :]
    for kind in range(kinds):
        gradient = refs[3 + kind * parts][0].astype(F32)
        for i in range(1, parts):
            gradient += refs[3 + kind * parts + i][0].astype(F32)
        new = adamw_update(
            weight_ref[0, kind],
            moment_ref[0, kind],
            second_ref[0, kind],
            gradient,
            MATRIX_RATE,
            MATRIX_DECAY,
        )
        for out, value in zip(outs, new):
            out[0, kind] = value


def adamw_blocks(weight, moment, second, gradients):
    experts, kinds, high, wide = weight.shape
    parts = len(gradients[0])
    whole = pl.BlockSpec((1, kinds, high, wide), lambda e: (e, 0, 0, 0))
    return pl.pallas_call(
        functools.partial(adamw_kernel, kinds, parts),
        grid=(experts,),
        in_specs=[whole] * 3 + [pl.BlockSpec((1, high, wide), lambda e: (e, 0, 0))] * (kinds * parts),
        out_specs=[whole] * 3,
        out_shape=[jax.ShapeDtypeStruct(weight.shape, F32)] * 3,
        compiler_params=pltpu.CompilerParams(vmem_limit_bytes=48 * 1024 * 1024),
        cost_estimate=pl.CostEstimate(
            flops=20 * weight.size, bytes_accessed=28 * weight.size, transcendentals=weight.size
        ),
        name="adamw",
    )(weight, moment, second, *[part for kind in gradients for part in kind])


def call_whole(kernel, out_shape, operands, name, scalars=None, specs=None, scratch=(), cost=0):
    specs = specs or {}
    scalars = jnp.zeros((1,), jnp.int32) if scalars is None else scalars
    return pl.pallas_call(
        kernel,
        grid_spec=pltpu.PrefetchScalarGridSpec(
            num_scalar_prefetch=1,
            grid=(1,),
            in_specs=[
                specs.get(i, pl.BlockSpec(array.shape, lambda g, s, n=array.ndim: (0,) * n))
                for i, array in enumerate(operands)
            ],
            out_specs=[
                pl.BlockSpec(shape.shape, lambda g, s, n=len(shape.shape): (0,) * n)
                for shape in out_shape
            ],
            scratch_shapes=list(scratch),
        ),
        out_shape=out_shape,
        compiler_params=pltpu.CompilerParams(vmem_limit_bytes=56 * 1024 * 1024),
        cost_estimate=pl.CostEstimate(flops=cost, bytes_accessed=1 << 22, transcendentals=0),
        name=name,
    )(scalars, *operands)


def swap_halves(chunk):
    columns = chunk.shape[1]
    lane = lax.broadcasted_iota(jnp.int32, chunk.shape, 1)
    return jnp.where(
        lane % HD < HD // 2,
        pltpu.roll(chunk, columns - HD // 2, axis=1),
        pltpu.roll(chunk, HD // 2, axis=1),
    )


def turn(chunk, cosine, sine, begin, end):
    if begin >= end:
        return chunk
    turned = chunk * cosine + swap_halves(chunk) * sine
    if begin + chunk.shape[1] <= end:
        return turned
    lane = lax.broadcasted_iota(jnp.int32, chunk.shape, 1)
    return jnp.where(lane + begin < end, turned, chunk)


def soft(query, key, begin):
    scores = dot(query, key, ((1,), (1,))) * HD ** (-0.5)
    row = lax.broadcasted_iota(jnp.int32, scores.shape, 0) + begin
    scores = jnp.where(row >= lax.broadcasted_iota(jnp.int32, scores.shape, 1), scores, NEG_LARGE)
    exponent = jnp.exp(scores - jnp.max(scores, axis=1, keepdims=True))
    return exponent * (1.0 / jnp.sum(exponent, axis=1, keepdims=True))


def front_kernel(q_cols, k_cols, s_ref, x_ref, gains_ref, qkv_ref, cos_ref, sin_ref, a_ref, rot_ref, mix_ref):
    length = x_ref.shape[0]
    step = min(256, length)
    for begin in range(0, length, step):
        part = slice(begin, begin + step)
        x = x_ref[part].astype(F32)
        a = (normalize(x)[0] * gains_ref[0:1]).astype(BF)
        a_ref[part] = a
        pre = dot(a, qkv_ref[...], ((1,), (0,)))
        for low in range(0, pre.shape[1], 128):
            rot_ref[part, low : low + 128] = turn(
                pre[:, low : low + 128], cos_ref[part], sin_ref[part], low, q_cols + k_cols
            ).astype(BF)
    heads = q_cols // HD
    share = q_cols // k_cols
    for head in range(heads):
        at = head * HD
        key_at = q_cols + head // share * HD
        value_at = key_at + k_cols
        for begin in range(0, length, step):
            end = begin + step
            weights = soft(rot_ref[begin:end, at : at + HD], rot_ref[:end, key_at : key_at + HD], begin)
            mix_ref[begin:end, at : at + HD] = dot(
                weights.astype(BF), rot_ref[:end, value_at : value_at + HD], ((1,), (0,))
            ).astype(BF)


def attention_back_kernel(q_cols, k_cols, s_ref, rot_ref, grad_ref, cos_ref, sin_ref, out_ref, acc_ref):
    length = rot_ref.shape[0]
    step = min(256, length)
    acc_ref[...] = jnp.zeros_like(acc_ref)
    heads = q_cols // HD
    share = q_cols // k_cols
    scale = HD ** (-0.5)
    for head in range(heads):
        at = head * HD
        key_at = q_cols + head // share * HD
        value_at = key_at + k_cols
        for begin in range(0, length, step):
            end = begin + step
            query = rot_ref[begin:end, at : at + HD]
            key = rot_ref[:end, key_at : key_at + HD]
            grad = grad_ref[begin:end, at : at + HD]
            weights = soft(query, key, begin)
            grad_weights = dot(grad, rot_ref[:end, value_at : value_at + HD], ((1,), (1,)))
            delta = jnp.sum(weights * grad_weights, axis=1, keepdims=True)
            grad_scores = (weights * (grad_weights - delta)).astype(BF)
            acc_ref[begin:end, at : at + HD] = dot(grad_scores, key, ((1,), (0,))) * scale
            acc_ref[:end, key_at : key_at + HD] += dot(grad_scores, query, ((0,), (0,))) * scale
            acc_ref[:end, value_at : value_at + HD] += dot(weights.astype(BF), grad, ((0,), (0,)))
    for begin in range(0, length, step):
        part = slice(begin, begin + step)
        for low in range(0, out_ref.shape[1], 128):
            out_ref[part, low : low + 128] = turn(
                acc_ref[part, low : low + 128], cos_ref[part], -sin_ref[part], low, q_cols + k_cols
            ).astype(BF)


def middle_kernel(s_ref, mix_ref, out_ref, x_ref, routes_ref, gains_ref, rest_ref, message_ref, mid_ref):
    rows, width = x_ref.shape
    mid = x_ref[...].astype(F32)
    for t in range(mix_ref.shape[0]):
        mid += dot(mix_ref[t], out_ref[t], ((1,), (1,)))
    mid_ref[...] = mid
    b = (normalize(mid)[0] * gains_ref[1:2]).astype(BF)
    message_ref[:, :width] = b
    logits = dot(b, rest_ref[...], ((1,), (0,)))
    lane = lax.broadcasted_iota(jnp.int32, (rows, PAD), 1)
    routed = lane < 0
    for k in range(routes_ref.shape[1]):
        routed |= lane == routes_ref[:, k : k + 1]
    logits = jnp.where(routed, logits, NEG_LARGE)
    exponent = jnp.where(routed, jnp.exp(logits - jnp.max(logits, axis=1, keepdims=True)), 0.0)
    gating = exponent / jnp.sum(exponent, axis=1, keepdims=True)
    high = gating.astype(BF).astype(F32)
    low = pltpu.roll(gating - high, EXPERTS, axis=1)
    message_ref[:, width:] = jnp.where(lane < EXPERTS, high, low).astype(BF)


def join_tail(tail):
    lane = lax.broadcasted_iota(jnp.int32, tail.shape, 1)
    return jnp.where(lane < EXPERTS, tail + pltpu.roll(tail, PAD - EXPERTS, axis=1), 0.0)


def middle_back_kernel(parts, s_ref, *refs):
    sums = refs[:parts]
    mid_ref, message_ref, dy_ref, gains_ref, rest_ref, out_ref = refs[parts : parts + 6]
    grad_mid_ref, attention_ref, mix_ref, tail_ref = refs[parts + 6 :]
    rows, width = mid_ref.shape
    total = sums[0][...].astype(F32)
    for ref in sums[1:]:
        total += ref[...].astype(F32)
    gating = join_tail(message_ref[:, width:].astype(F32))
    grad_gating = join_tail(total[:, width:])
    grad_logits = gating * (grad_gating - jnp.sum(gating * grad_gating, axis=1, keepdims=True))
    grad_logits = grad_logits.astype(BF)
    grad_b = total[:, :width] + dot(grad_logits, rest_ref[...], ((1,), (1,)))
    unit, inverse = normalize(mid_ref[...])
    grad_mid = dy_ref[...].astype(F32) + norm_backward(grad_b * gains_ref[1:2], unit, inverse)
    grad_mid_ref[...] = grad_mid
    attention = grad_mid.astype(BF)
    attention_ref[...] = attention
    for t in range(out_ref.shape[0]):
        mix_ref[t] = dot(attention, out_ref[t], ((1,), (0,))).astype(BF)
    lane = lax.broadcasted_iota(jnp.int32, (rows, PAD), 1)
    ones = jnp.where(lane == EXPERTS, 1.0, 0.0).astype(BF)
    tail_ref[...] = (
        dot(message_ref[:, :width], grad_logits, ((0,), (0,)))
        + dot((grad_b * unit).astype(BF), ones, ((0,), (0,)))
    ).astype(BF)


def pack_kernel(
    s_ref, a_ref, grad_ref, attention_ref, mix_ref, qkv_ref, rest_ref, tail_ref, main_ref, tail_out_ref
):
    late = dot(a_ref[...], grad_ref[...], ((0,), (0,)))
    columns = late.shape[1]
    main_ref[:, :columns] = late.astype(BF)
    main_ref[:, columns:] = dot(attention_ref[...], mix_ref[...], ((0,), (0,))).astype(BF)
    rest = rest_ref[...].astype(F32)
    lane = lax.broadcasted_iota(jnp.int32, rest.shape, 1)
    piece = (lane == EXPERTS) | (lane == EXPERTS + 2) | (lane == EXPERTS + 4)
    gain = jnp.sum(jnp.where(piece, rest, 0.0), axis=1, keepdims=True)
    gain_grad = jnp.sum(late * qkv_ref[...].astype(F32), axis=1, keepdims=True) / gain
    tail = tail_ref[...].astype(F32)
    tail_out_ref[...] = jnp.where(lane == EXPERTS + 1, gain_grad, tail).astype(BF)


def final_kernel(s_ref, rows_ref, qkv_ref, grad_mid_ref, x_ref, gains_ref, out_ref):
    grad_a = dot(rows_ref[0], qkv_ref[0], ((1,), (1,)))
    for t in range(1, rows_ref.shape[0]):
        grad_a += dot(rows_ref[t], qkv_ref[t], ((1,), (1,)))
    unit, inverse = normalize(x_ref[...].astype(F32))
    out_ref[...] = (
        grad_mid_ref[...] + norm_backward(grad_a * gains_ref[0:1], unit, inverse)
    ).astype(BF)


def body(
    ring,
    tensors,
    tokens,
    cotangent,
    routes,
    norm_gains,
    gains_moment,
    gains_second,
    query_weight,
    query_moment,
    query_second,
    keyval_weight,
    keyval_moment,
    keyval_second,
    output_weight,
    output_moment,
    output_second,
    router_weight,
    router_moment,
    router_second,
    gateup_weight,
    gateup_moment,
    gateup_second,
    down_weight,
    down_moment,
    down_second,
):
    length, width = tokens.shape
    rows = length // tensors
    experts = gateup_weight.shape[0]
    shape = jax.ShapeDtypeStruct
    lane_t = lax.axis_index("tensor").astype(jnp.int32).reshape(1)
    own_block = pl.BlockSpec((rows, width), lambda g, s: (s[0], 0))
    chips = tensors // 2

    gate_pieces = tensor_gather(gateup_weight[:, 0].astype(BF), tensors)
    up_pieces = tensor_gather(gateup_weight[:, 1].astype(BF), tensors)
    down_pieces = tensor_gather(down_weight.astype(BF), tensors)
    gate_low = jnp.concatenate(gate_pieces, axis=2)
    up_low = jnp.concatenate(up_pieces, axis=2)
    down_low = jnp.concatenate(down_pieces, axis=1)

    q_cols = query_weight.shape[1]
    k_cols = keyval_weight.shape[2]
    o_cols = output_weight.shape[0]
    heads_cols = q_cols + 2 * k_cols
    packed = jnp.concatenate(
        [
            query_weight.astype(BF),
            keyval_weight[0].astype(BF),
            keyval_weight[1].astype(BF),
            output_weight.T.astype(BF),
            router_weight.astype(BF),
        ]
        + split_pieces(norm_gains.T, 3)
        + [jnp.zeros((query_weight.shape[0], PAD - EXPERTS - 6), BF)],
        axis=1,
    )
    packed_blocks = ring_gather(packed, ring)
    offsets = sorted(packed_blocks)
    qkv_low, out_low, rest = place(
        [packed_blocks[o] for o in offsets],
        jnp.stack([ring_index(ring, o) for o in offsets]).astype(jnp.int32),
        cuts=[
            (0, heads_cols),
            (heads_cols, heads_cols + o_cols),
            (heads_cols + o_cols, heads_cols + o_cols + PAD),
        ],
        after=gate_pieces[1:chips] + up_pieces[1:chips],
    )
    gains_all = (
        rest[:, EXPERTS : EXPERTS + 2].astype(F32)
        + rest[:, EXPERTS + 2 : EXPERTS + 4].astype(F32)
        + rest[:, EXPERTS + 4 : EXPERTS + 6].astype(F32)
    ).T
    one_spot = jnp.zeros((1,), jnp.int32)
    dy_own = lax.dynamic_slice_in_dim(cotangent, lane_t[0] * rows, rows, axis=0)
    dy_all = lax.all_gather(
        place([dy_own], one_spot, after=[qkv_low]), "expert", axis=0, tiled=True
    )

    cosine_table, sine_table = rope_tables(length, HD)
    cosine_table = jnp.concatenate([cosine_table] * 4, axis=1)
    sine_table = jnp.concatenate([-sine_table, sine_table] * 2, axis=1)
    a, rotated, mixture = call_whole(
        functools.partial(front_kernel, q_cols, k_cols),
        [shape((length, width), BF), shape((length, heads_cols), BF), shape((length, q_cols), BF)],
        [tokens, gains_all, qkv_low, cosine_table, sine_table],
        "attention_forward",
        cost=10**10,
    )

    mixture_rows = lax.all_to_all(
        mixture.reshape(tensors, rows, o_cols), "tensor", split_axis=0, concat_axis=0, tiled=True
    )
    owners_t = tensor_index(tensors)
    out_all = place(
        tensor_gather(out_low, tensors), owners_t, after=[mixture_rows] + down_pieces[1:chips]
    ).reshape(tensors, width, o_cols)
    message, x_mid = call_whole(
        middle_kernel,
        [shape((rows, width + PAD), BF), shape((rows, width), F32)],
        [mixture_rows, out_all, tokens, routes, gains_all, rest],
        "middle",
        scalars=lane_t,
        specs={2: own_block, 3: pl.BlockSpec((rows, routes.shape[1]), lambda g, s: (s[0], 0))},
        cost=10**9,
    )
    blocks = ring_gather(message, ring)

    half = ring // 2
    first = (lax.axis_index("expert") * experts).astype(jnp.int32)
    calls = [[0]] + [[-k, k] for k in range(1, half - 1)] + [[-half, half - 1], [1 - half]]
    back = {}
    forth = {}
    grads = []
    scaled = []
    order = []
    spots = []
    after = []
    for number, call in enumerate(calls):
        owners = [ring_index(ring, o).astype(jnp.int32) for o in call]
        result = expert_blocks(
            first,
            [blocks[o] for o in call],
            owners,
            [dy_all] * len(call),
            gate_low,
            up_low,
            down_low,
            after,
        )
        grads.append(result[0])
        scaled.append(result[1])
        after = [result[1]]
        for part, o in enumerate(call):
            forth[o], back[o] = result[2][part], result[3][part]
            order.append(o)
            spots.append((number, part, rows))
    returned, sent = ring_reduce(lambda offset: back[offset], ring)

    still = jnp.zeros((ring,), jnp.int32)
    whose = jnp.stack([ring_index(ring, o) for o in order]).astype(jnp.int32)
    messages = [blocks[o] for o in order]
    hop = lambda number: [sent[min(number, half - 1)]]
    gate_grads = weight_grad(messages, still, spots, grads, 0, False, tensors, hop(1))
    up_grads = weight_grad(messages, still, spots, grads, 1, False, tensors, hop(2))
    down_grads = weight_grad([dy_all] * ring, whose, spots, scaled, 0, True, tensors, hop(3))

    moe_sum = lax.psum_scatter(
        place([forth[o] for o in order], whose, after=[returned[1]]),
        "expert",
        scatter_dimension=0,
        tiled=True,
    )
    block_out = place(tensor_gather((x_mid + moe_sum.astype(F32)).astype(BF), tensors), owners_t)

    grad_mid, grad_attention, grad_mixture, tail = call_whole(
        functools.partial(middle_back_kernel, len(returned)),
        [
            shape((rows, width), F32),
            shape((rows, width), BF),
            shape((tensors, rows, o_cols), BF),
            shape((width, PAD), BF),
        ],
        returned + [x_mid, message, cotangent, gains_all, rest, out_all],
        "middle_backward",
        scalars=lane_t,
        specs={len(returned) + 2: own_block},
        cost=10**9,
    )
    grad_mixture = lax.all_to_all(
        grad_mixture, "tensor", split_axis=0, concat_axis=0, tiled=True
    ).reshape(length, o_cols)
    grad_attention_all = place(tensor_gather(grad_attention, tensors), owners_t)
    (grad_pre,) = call_whole(
        functools.partial(attention_back_kernel, q_cols, k_cols),
        [shape((length, heads_cols), BF)],
        [rotated, grad_mixture, cosine_table, sine_table],
        "attention_backward",
        scratch=[pltpu.VMEM((length, heads_cols), F32)],
        cost=2 * 10**10,
    )
    grad_pre_rows = lax.all_to_all(
        grad_pre.reshape(tensors, rows, heads_cols), "tensor", split_axis=0, concat_axis=0, tiled=True
    )
    main, tail = call_whole(
        pack_kernel,
        [shape((width, heads_cols + o_cols), BF), shape((width, PAD), BF)],
        [a, grad_pre, grad_attention_all, mixture, qkv_low, rest, tail],
        "pack",
        cost=4 * 10**9,
    )
    tail = tensor_sum(tail, tensors)
    piece = width // ring

    def own_piece(offset):
        start = ring_index(ring, offset) * piece
        return jnp.concatenate(
            [lax.dynamic_slice_in_dim(array, start, piece, axis=0) for array in (main, tail)], axis=1
        )

    summed = sum(part.astype(F32) for part in ring_reduce(own_piece, ring)[0])
    qkv_all = lax.all_gather(place([qkv_low], one_spot, after=[scaled[1]]), "tensor")
    (input_grad,) = call_whole(
        final_kernel,
        [shape((rows, width), BF)],
        [grad_pre_rows, qkv_all, grad_mid, tokens, gains_all],
        "input_gradient",
        scalars=lane_t,
        specs={3: own_block},
        cost=2 * 10**9,
    )
    input_grad = place(tensor_gather(input_grad, tensors), owners_t)

    new_gateup = adamw_blocks(
        gateup_weight,
        gateup_moment,
        gateup_second,
        [tensor_reduce(gate_grads, tensors), tensor_reduce(up_grads, tensors)],
    )
    new_down = [
        array[:, 0]
        for array in adamw_blocks(
            down_weight[:, None],
            down_moment[:, None],
            down_second[:, None],
            [tensor_reduce(down_grads, tensors)],
        )
    ]
    query_sum = summed[:, :q_cols]
    keyval_sum = jnp.stack([summed[:, q_cols : q_cols + k_cols], summed[:, q_cols + k_cols : heads_cols]])
    output_sum = summed[:, heads_cols : heads_cols + o_cols].T
    ends = summed[:, heads_cols + o_cols :]
    router_sum = ends[:, :EXPERTS]
    gains_sum = jnp.stack([ends[:, EXPERTS + 1], ends[:, EXPERTS]])
    new_gains = adamw_update(norm_gains, gains_moment, gains_second, gains_sum, GAIN_RATE, 0.0)
    new_query = adamw_update(
        query_weight, query_moment, query_second, query_sum, MATRIX_RATE, MATRIX_DECAY
    )
    new_keyval = adamw_update(
        keyval_weight, keyval_moment, keyval_second, keyval_sum, MATRIX_RATE, MATRIX_DECAY
    )
    new_output = adamw_update(
        output_weight, output_moment, output_second, output_sum, MATRIX_RATE, MATRIX_DECAY
    )
    new_router = adamw_update(
        router_weight, router_moment, router_second, router_sum, MATRIX_RATE, MATRIX_DECAY
    )
    return (
        (block_out, input_grad)
        + tuple(new_gains)
        + tuple(new_query)
        + tuple(new_keyval)
        + tuple(new_output)
        + tuple(new_router)
        + tuple(new_gateup)
        + tuple(new_down)
    )


def solution(mesh):
    rows = P("expert", None)
    gains = P(None, "expert")
    query = P("expert", "tensor")
    keyval = P(None, "expert", "tensor")
    output = P("tensor", "expert")
    gateup = P("expert", None, None, "tensor")
    down = P("expert", "tensor", None)
    weights = tuple(
        spec for spec in (gains, query, keyval, output, rows, gateup, down) for _ in range(3)
    )
    return jax.shard_map(
        functools.partial(body, mesh.shape["expert"], mesh.shape["tensor"]),
        mesh=mesh,
        in_specs=(rows, rows, rows) + weights,
        out_specs=(rows, rows) + weights,
        check_vma=False,
    )
```

```python
import functools

import jax
import jax.numpy as jnp
from jax import lax
from jax.experimental import pallas as pl
from jax.experimental.pallas import tpu as pltpu
from jax.sharding import PartitionSpec as P

HEADS = 16
KV_HEADS = 8
HD = 64
EXPERTS = 32
STEP = 10
PAD = 128

NORM_EPS = 1e-06
BETA_ONE = 0.9
BETA_TWO = 0.999
ADAM_EPS = 1e-08
MATRIX_RATE = 0.08
GAIN_RATE = 0.6
MATRIX_DECAY = 0.1
NEG_LARGE = -1e30
BF = jnp.bfloat16
F32 = jnp.float32


def dot(left, right, dims):
    return lax.dot_general(left, right, (dims, ((), ())), preferred_element_type=F32)


def normalize(values):
    inverse = lax.rsqrt(jnp.mean(values * values, axis=-1, keepdims=True) + NORM_EPS)
    return (values * inverse, inverse)


def norm_backward(grad_unit, unit, inverse):
    return inverse * (grad_unit - unit * jnp.mean(grad_unit * unit, axis=-1, keepdims=True))


def rope_tables(length, head_size):
    half_size = head_size // 2
    frequency = 10000.0 ** (-(jnp.arange(half_size, dtype=F32) * 2.0) / head_size)
    angles = jnp.arange(length, dtype=F32)[:, None] * frequency[None, :]
    return (jnp.cos(angles), jnp.sin(angles))


def adamw_update(weight, moment, second, gradient, rate, decay):
    moment_new = BETA_ONE * moment + (1.0 - BETA_ONE) * gradient
    second_new = BETA_TWO * second + (1.0 - BETA_TWO) * gradient * gradient
    fix_one = 1.0 - BETA_ONE**STEP
    fix_two = 1.0 - BETA_TWO**STEP
    update = moment_new / fix_one / (jnp.sqrt(second_new / fix_two) + ADAM_EPS)
    return (weight - rate * (update + decay * weight), moment_new, second_new)


def split_pieces(values, count):
    pieces = []
    for _ in range(count):
        high = lax.reduce_precision(values, 8, 7)
        pieces.append(high.astype(BF))
        values = values - high
    return pieces


def ring_order(size):
    return list(range(0, size, 2)) + list(range(1, size, 2))[::-1]


def ring_perm(size, step):
    order = ring_order(size)
    return [(order[i], order[(i + step) % size]) for i in range(size)]


def ring_index(size, offset):
    me = lax.axis_index("expert")
    place = jnp.where(me % 2 == 0, me // 2, size - 1 - me // 2)
    place = (place + offset) % size
    return jnp.where(place < (size + 1) // 2, 2 * place, 2 * (size - 1 - place) + 1)


def ring_gather(block, size):
    blocks = {0: block}
    ahead = behind = block
    for hop in range(1, size // 2 + 1):
        ahead = lax.ppermute(ahead, "expert", ring_perm(size, 1))
        blocks[-hop] = ahead
        if hop <= (size - 1) // 2:
            behind = lax.ppermute(behind, "expert", ring_perm(size, -1))
            blocks[hop] = behind
    return blocks


def ring_reduce(part, size, beside=None):
    down = up = None
    after = []
    for hop in range(size // 2, 0, -1):
        side = hop - 1
        if down is None:
            messages = [part(-hop), part(side)]
        else:
            pairs = [(down, part(-hop))] + ([(up, part(side))] if side > 0 else [])
            messages = add_pairs(pairs, after)
            after = beside(hop, messages) if beside else []
        down = lax.ppermute(messages[0], "expert", ring_perm(size, -1))
        if side > 0:
            up = lax.ppermute(messages[1], "expert", ring_perm(size, 1))
    return [part(0), down, up], after


def tensor_perm(size, along, core):
    chips = size // 2
    return [(t, ((t // 2 + along) % chips) * 2 + ((t % 2) ^ core)) for t in range(size)]


def tensor_gather(shard, size, after=()):
    own = [shard] + [
        lax.ppermute(shard, "tensor", tensor_perm(size, -step, 0)) for step in range(1, size // 2)
    ]
    ready = [hold(piece, after) for piece in own] if after else own
    other = [lax.ppermute(piece, "tensor", tensor_perm(size, 0, 1)) for piece in ready]
    return own + other


def tensor_reduce(parts, size):
    chips = size // 2
    result = []
    for step in reversed(range(chips)):
        came = lax.ppermute(parts[chips + step], "tensor", tensor_perm(size, 0, 1))
        if step == 0:
            result += [parts[0], came]
        else:
            total = (parts[step].astype(F32) + came.astype(F32)).astype(BF)
            result.append(lax.ppermute(total, "tensor", tensor_perm(size, step, 0)))
    return result


def tensor_sum(values, size):
    values = values + lax.ppermute(values, "tensor", tensor_perm(size, 0, 1))
    moved = [
        lax.ppermute(values, "tensor", tensor_perm(size, step, 0)) for step in range(1, size // 2)
    ]
    return sum(moved, values)


def place_kernel(blocks, cuts, *refs):
    index_ref = refs[0]
    outs = refs[len(refs) - len(cuts) :]
    for block in range(blocks):
        source = refs[1 + block]
        size = source.shape[0]
        start = pl.multiple_of(index_ref[block] * size, size)
        for (low, high), out in zip(cuts, outs):
            out[pl.ds(start, size), :] = source[:, low:high]


def place(blocks, index, cuts=None, after=()):
    size, columns = blocks[0].shape
    cuts = cuts or [(0, columns)]
    count = len(blocks)
    vmem = pl.BlockSpec(memory_space=pltpu.VMEM)
    out = pl.pallas_call(
        functools.partial(place_kernel, count, cuts),
        in_specs=[pl.BlockSpec(memory_space=pltpu.SMEM)]
        + [vmem] * count
        + [pl.BlockSpec(memory_space=pl.ANY)] * len(after),
        out_specs=[vmem] * len(cuts),
        out_shape=[
            jax.ShapeDtypeStruct((count * size, high - low), blocks[0].dtype) for low, high in cuts
        ],
        compiler_params=pltpu.CompilerParams(vmem_limit_bytes=32 * 1024 * 1024),
        name="place",
    )(index, *blocks, *after)
    return out if len(cuts) > 1 else out[0]


def hold(array, after):
    flat = array.reshape(-1, array.shape[-1])
    return place([flat], jnp.zeros((1,), jnp.int32), after=after).reshape(array.shape)


def cut_kernel(blocks, s_ref, main_ref, tail_ref, *refs):
    outs = refs[len(refs) - blocks :]
    for i, out in enumerate(outs):
        size = out.shape[0]
        part = pl.ds(pl.multiple_of(s_ref[i] * size, size), size)
        out[:, : main_ref.shape[1]] = main_ref[part, :]
        out[:, main_ref.shape[1] :] = tail_ref[part, :]


def cut(main, tail, index, after):
    count = index.shape[0]
    vmem = pl.BlockSpec(memory_space=pltpu.VMEM)
    block = (main.shape[0] // count, main.shape[1] + tail.shape[1])
    return pl.pallas_call(
        functools.partial(cut_kernel, count),
        in_specs=[pl.BlockSpec(memory_space=pltpu.SMEM), vmem, vmem]
        + [pl.BlockSpec(memory_space=pl.ANY)] * len(after),
        out_specs=[vmem] * count,
        out_shape=[jax.ShapeDtypeStruct(block, main.dtype)] * count,
        compiler_params=pltpu.CompilerParams(vmem_limit_bytes=32 * 1024 * 1024),
        name="cut",
    )(index, main, tail, *after)


def add_kernel(count, *refs):
    outs = refs[len(refs) - count :]
    for i, out in enumerate(outs):
        out[...] = (refs[2 * i][...].astype(F32) + refs[2 * i + 1][...].astype(F32)).astype(BF)


def add_pairs(pairs, after):
    vmem = pl.BlockSpec(memory_space=pltpu.VMEM)
    return pl.pallas_call(
        functools.partial(add_kernel, len(pairs)),
        in_specs=[vmem] * (2 * len(pairs)) + [pl.BlockSpec(memory_space=pl.ANY)] * len(after),
        out_specs=[vmem] * len(pairs),
        out_shape=[jax.ShapeDtypeStruct(pair[0].shape, BF) for pair in pairs],
        compiler_params=pltpu.CompilerParams(vmem_limit_bytes=32 * 1024 * 1024),
        name="add_pairs",
    )(*[array for pair in pairs for array in pair], *after)


def tensor_index(size):
    me = lax.axis_index("tensor")
    chips = size // 2
    chip, core = me // 2, me % 2
    own = [((chip + step) % chips) * 2 + core for step in range(chips)]
    other = [((chip + step) % chips) * 2 + (1 - core) for step in range(chips)]
    return jnp.stack(own + other).astype(jnp.int32)


def expert_kernel(count, afters, *refs):
    first_ref = refs[0]
    message_refs = refs[1 : 1 + count]
    cotangent_refs = refs[1 + count : 1 + 2 * count]
    gate_ref, up_ref, down_ref = refs[1 + 2 * count : 4 + 2 * count]
    outs = refs[4 + 2 * count + afters :]
    grads_ref, scaled_ref = outs[:2]
    y_refs = outs[2 : 2 + count]
    back_refs = outs[2 + count : 2 + 2 * count]
    rows_ref, dy_ref, y_acc, back_acc, tail_acc = outs[2 + 2 * count :]
    expert = pl.program_id(0)
    rows, width = cotangent_refs[0].shape

    @pl.when(expert == 0)
    def _():
        for i in range(count):
            rows_ref[i * rows : (i + 1) * rows] = message_refs[i][...]
            dy_ref[i * rows : (i + 1) * rows] = cotangent_refs[i][...]
        y_acc[...] = jnp.zeros_like(y_acc)
        back_acc[...] = jnp.zeros_like(back_acc)
        tail_acc[...] = jnp.zeros_like(tail_acc)

    gate_w = gate_ref[0]
    up_w = up_ref[0]
    down_w = down_ref[0]
    column = first_ref[0] + expert
    for i in range(count):
        part = slice(i * rows, (i + 1) * rows)
        b = rows_ref[part, :width]
        dy = dy_ref[part]
        gate_pre = dot(b, gate_w, ((1,), (0,)))
        up_pre = dot(b, up_w, ((1,), (0,)))
        sig = jax.nn.sigmoid(gate_pre)
        silu = gate_pre * sig
        act = (silu * up_pre).astype(BF).astype(F32)
        grad_act = dot(dy, down_w, ((1,), (1,)))
        grad_gating = jnp.sum(act * grad_act, axis=1, keepdims=True)
        lane = lax.broadcasted_iota(jnp.int32, (rows, PAD), 1)
        chosen = (lane == column) | (lane == column + EXPERTS)
        tail = rows_ref[part, width:].astype(F32)
        gating = jnp.sum(jnp.where(chosen, tail, 0.0), axis=1, keepdims=True)
        tail_acc[part] += jnp.where(chosen, grad_gating, 0.0)
        grad_act = grad_act * gating
        grad_gate = (grad_act * up_pre * (sig * (1.0 + gate_pre * (1.0 - sig)))).astype(BF)
        grad_up = (grad_act * silu).astype(BF)
        scaled = (act * gating).astype(BF)
        grads_ref[0, 0, part] = grad_gate
        grads_ref[1, 0, part] = grad_up
        scaled_ref[0, part] = scaled
        back_acc[part] += dot(grad_gate, gate_w, ((1,), (1,))) + dot(grad_up, up_w, ((1,), (1,)))
        y_acc[part] += dot(scaled, down_w, ((1,), (0,)))

    @pl.when(expert == pl.num_programs(0) - 1)
    def _():
        lane = lax.broadcasted_iota(jnp.int32, (rows, PAD), 1)
        for i in range(count):
            part = slice(i * rows, (i + 1) * rows)
            y_refs[i][...] = y_acc[part].astype(BF)
            total = tail_acc[part]
            high = total.astype(BF).astype(F32)
            back_refs[i][:, :width] = back_acc[part].astype(BF)
            back_refs[i][:, width:] = jnp.where(lane < EXPERTS, high, total - high).astype(BF)


def expert_blocks(first, messages, owners, cotangents, gate, up, down, after):
    experts, width, hidden = gate.shape
    rows, message = messages[0].shape
    count = len(messages)
    block = pl.BlockSpec((rows, message), lambda e, s: (0, 0))
    plain = pl.BlockSpec((rows, width), lambda e, s: (0, 0))
    owned = [pl.BlockSpec((rows, width), lambda e, s, i=i: (s[1 + i], 0)) for i in range(count)]
    shape = jax.ShapeDtypeStruct
    out = pl.pallas_call(
        functools.partial(expert_kernel, count, len(after)),
        grid_spec=pltpu.PrefetchScalarGridSpec(
            num_scalar_prefetch=1,
            grid=(experts,),
            in_specs=[block] * count
            + owned
            + [pl.BlockSpec((1, width, hidden), lambda e, s: (e, 0, 0))] * 2
            + [pl.BlockSpec((1, hidden, width), lambda e, s: (e, 0, 0))]
            + [pl.BlockSpec(memory_space=pl.ANY)] * len(after),
            out_specs=[
                pl.BlockSpec((2, 1, count * rows, hidden), lambda e, s: (0, e, 0, 0)),
                pl.BlockSpec((1, count * rows, hidden), lambda e, s: (e, 0, 0)),
            ]
            + [plain] * count
            + [block] * count,
            scratch_shapes=[
                pltpu.VMEM((count * rows, message), BF),
                pltpu.VMEM((count * rows, width), BF),
                pltpu.VMEM((count * rows, width), F32),
                pltpu.VMEM((count * rows, width), F32),
                pltpu.VMEM((count * rows, PAD), F32),
            ],
        ),
        out_shape=[
            shape((2, experts, count * rows, hidden), BF),
            shape((experts, count * rows, hidden), BF),
        ]
        + [shape((rows, width), BF)] * count
        + [shape((rows, message), BF)] * count,
        compiler_params=pltpu.CompilerParams(vmem_limit_bytes=60 * 1024 * 1024),
        cost_estimate=pl.CostEstimate(
            flops=12 * count * rows * experts * width * hidden,
            bytes_accessed=6 * experts * width * hidden,
            transcendentals=count * rows * experts * hidden,
        ),
        name="expert_blocks",
    )(jnp.stack([first] + owners), *messages, *cotangents, gate, up, down, *after)
    return out[0], out[1], out[2 : 2 + count], out[2 + count :]


def weight_grad_kernel(spots, swap, shards, afters, *refs):
    blocks = len(spots)
    outs = refs[len(refs) - shards :]
    total = None
    for block, (call, part, rows) in enumerate(spots):
        grads_ref = refs[1 + blocks + call]
        lead = (0,) * (len(grads_ref.shape) - 2)
        grads = grads_ref[lead + (slice(part * rows, (part + 1) * rows),)]
        pair = (grads, refs[1 + block][...]) if swap else (refs[1 + block][...], grads)
        term = dot(*pair, ((0,), (0,)))
        total = term if total is None else total + term
    total = total.astype(BF)
    size = total.shape[0 if swap else 1] // shards
    for i, out in enumerate(outs):
        cut = slice(i * size, (i + 1) * size)
        out[0] = total[cut] if swap else total[:, cut]


def weight_grad(inputs, owners, spots, grads, pick, swap, shards, after):
    lead = grads[0].ndim == 4
    experts, _, hidden = grads[0].shape[-3:]
    rows = spots[0][2]
    width = inputs[0].shape[1] - (PAD if lead else 0)
    blocks = len(inputs)
    shape = (hidden // shards, width) if swap else (width, hidden // shards)
    in_specs = [pl.BlockSpec((rows, width), lambda e, s, i=i: (s[i], 0)) for i in range(blocks)]
    for array in grads:
        if lead:
            in_specs.append(pl.BlockSpec((1, 1) + array.shape[2:], lambda e, s: (pick, e, 0, 0)))
        else:
            in_specs.append(pl.BlockSpec((1,) + array.shape[1:], lambda e, s: (e, 0, 0)))
    in_specs += [pl.BlockSpec(memory_space=pl.ANY)] * len(after)
    return pl.pallas_call(
        functools.partial(weight_grad_kernel, spots, swap, shards, len(after)),
        grid_spec=pltpu.PrefetchScalarGridSpec(
            num_scalar_prefetch=1,
            grid=(experts,),
            in_specs=in_specs,
            out_specs=[pl.BlockSpec((1,) + shape, lambda e, s: (e, 0, 0))] * shards,
        ),
        out_shape=[jax.ShapeDtypeStruct((experts,) + shape, BF)] * shards,
        compiler_params=pltpu.CompilerParams(vmem_limit_bytes=60 * 1024 * 1024),
        cost_estimate=pl.CostEstimate(
            flops=2 * blocks * rows * experts * width * hidden,
            bytes_accessed=4 * blocks * rows * width,
            transcendentals=0,
        ),
        name="weight_grad",
    )(owners, *inputs, *grads, *after)


def adamw_kernel(kinds, parts, *refs):
    weight_ref, moment_ref, second_ref = refs[:3]
    outs = refs[len(refs) - 3 :]
    for kind in range(kinds):
        gradient = refs[3 + kind * parts][0].astype(F32)
        for i in range(1, parts):
            gradient += refs[3 + kind * parts + i][0].astype(F32)
        new = adamw_update(
            weight_ref[0, kind],
            moment_ref[0, kind],
            second_ref[0, kind],
            gradient,
            MATRIX_RATE,
            MATRIX_DECAY,
        )
        for out, value in zip(outs, new):
            out[0, kind] = value


def adamw_blocks(weight, moment, second, gradients):
    experts, kinds, high, wide = weight.shape
    parts = len(gradients[0])
    whole = pl.BlockSpec((1, kinds, high, wide), lambda e: (e, 0, 0, 0))
    return pl.pallas_call(
        functools.partial(adamw_kernel, kinds, parts),
        grid=(experts,),
        in_specs=[whole] * 3 + [pl.BlockSpec((1, high, wide), lambda e: (e, 0, 0))] * (kinds * parts),
        out_specs=[whole] * 3,
        out_shape=[jax.ShapeDtypeStruct(weight.shape, F32)] * 3,
        compiler_params=pltpu.CompilerParams(vmem_limit_bytes=60 * 1024 * 1024),
        cost_estimate=pl.CostEstimate(
            flops=20 * weight.size, bytes_accessed=28 * weight.size, transcendentals=weight.size
        ),
        name="adamw",
    )(weight, moment, second, *[part for kind in gradients for part in kind])


def adamw_rest_kernel(q_cols, k_cols, s_ref, *refs):
    total = refs[0][...].astype(F32) + refs[1][...].astype(F32) + refs[2][...].astype(F32)
    arrays, outs = refs[3:18], refs[18:]
    gains, query, keyval, output, router = (arrays[i : i + 3] for i in range(0, 15, 3))
    new_gains, new_query, new_keyval, new_output, new_router = (
        outs[i : i + 3] for i in range(0, 15, 3)
    )

    def update(refs, outs, where, gradient, rate, decay):
        new = adamw_update(*[ref[where] for ref in refs], gradient, rate, decay)
        for out, value in zip(outs, new):
            out[where] = value

    heads_cols = q_cols + 2 * k_cols
    o_cols = output[0].shape[0]
    every = (slice(None), slice(None))
    update(query, new_query, every, total[:, :q_cols], MATRIX_RATE, MATRIX_DECAY)
    for kind in range(2):
        low = q_cols + kind * k_cols
        update(
            keyval, new_keyval, (kind,) + every, total[:, low : low + k_cols], MATRIX_RATE, MATRIX_DECAY
        )
    turned = total[:, heads_cols : heads_cols + o_cols].T
    update(output, new_output, every, turned, MATRIX_RATE, MATRIX_DECAY)
    ends = total[:, heads_cols + o_cols :]
    update(router, new_router, every, ends[:, :EXPERTS], MATRIX_RATE, MATRIX_DECAY)
    turned = ends.T
    for kind in range(2):
        at = EXPERTS + 1 - kind
        where = (slice(kind, kind + 1), slice(None))
        update(gains, new_gains, where, turned[at : at + 1], GAIN_RATE, 0.0)


def adamw_rest(q_cols, k_cols, parts, groups):
    arrays = [array for group in groups for array in group]
    return call_whole(
        functools.partial(adamw_rest_kernel, q_cols, k_cols),
        [jax.ShapeDtypeStruct(array.shape, F32) for array in arrays],
        parts + arrays,
        "adamw_rest",
        cost=10**8,
    )


def call_whole(kernel, out_shape, operands, name, scalars=None, specs=None, scratch=(), cost=0):
    specs = specs or {}
    scalars = jnp.zeros((1,), jnp.int32) if scalars is None else scalars
    return pl.pallas_call(
        kernel,
        grid_spec=pltpu.PrefetchScalarGridSpec(
            num_scalar_prefetch=1,
            grid=(1,),
            in_specs=[
                specs.get(i, pl.BlockSpec(array.shape, lambda g, s, n=array.ndim: (0,) * n))
                for i, array in enumerate(operands)
            ],
            out_specs=[
                pl.BlockSpec(shape.shape, lambda g, s, n=len(shape.shape): (0,) * n)
                for shape in out_shape
            ],
            scratch_shapes=list(scratch),
        ),
        out_shape=out_shape,
        compiler_params=pltpu.CompilerParams(vmem_limit_bytes=56 * 1024 * 1024),
        cost_estimate=pl.CostEstimate(flops=cost, bytes_accessed=1 << 22, transcendentals=0),
        name=name,
    )(scalars, *operands)


def swap_halves(chunk):
    columns = chunk.shape[1]
    lane = lax.broadcasted_iota(jnp.int32, chunk.shape, 1)
    return jnp.where(
        lane % HD < HD // 2,
        pltpu.roll(chunk, columns - HD // 2, axis=1),
        pltpu.roll(chunk, HD // 2, axis=1),
    )


def turn(chunk, cosine, sine, begin, end):
    if begin >= end:
        return chunk
    turned = chunk * cosine + swap_halves(chunk) * sine
    if begin + chunk.shape[1] <= end:
        return turned
    lane = lax.broadcasted_iota(jnp.int32, chunk.shape, 1)
    return jnp.where(lane + begin < end, turned, chunk)


def soft(query, key, begin):
    scores = dot(query, key, ((1,), (1,))) * HD ** (-0.5)
    row = lax.broadcasted_iota(jnp.int32, scores.shape, 0) + begin
    scores = jnp.where(row >= lax.broadcasted_iota(jnp.int32, scores.shape, 1), scores, NEG_LARGE)
    exponent = jnp.exp(scores - jnp.max(scores, axis=1, keepdims=True))
    return exponent * (1.0 / jnp.sum(exponent, axis=1, keepdims=True))


def front_kernel(q_cols, k_cols, s_ref, x_ref, gains_ref, qkv_ref, cos_ref, sin_ref, a_ref, rot_ref, mix_ref):
    length = x_ref.shape[0]
    step = min(256, length)
    for begin in range(0, length, step):
        part = slice(begin, begin + step)
        x = x_ref[part].astype(F32)
        a = (normalize(x)[0] * gains_ref[0:1]).astype(BF)
        a_ref[part] = a
        pre = dot(a, qkv_ref[...], ((1,), (0,)))
        for low in range(0, pre.shape[1], 128):
            rot_ref[part, low : low + 128] = turn(
                pre[:, low : low + 128], cos_ref[part], sin_ref[part], low, q_cols + k_cols
            ).astype(BF)
    heads = q_cols // HD
    share = q_cols // k_cols
    for head in range(heads):
        at = head * HD
        key_at = q_cols + head // share * HD
        value_at = key_at + k_cols
        for begin in range(0, length, step):
            end = begin + step
            weights = soft(rot_ref[begin:end, at : at + HD], rot_ref[:end, key_at : key_at + HD], begin)
            mix_ref[begin:end, at : at + HD] = dot(
                weights.astype(BF), rot_ref[:end, value_at : value_at + HD], ((1,), (0,))
            ).astype(BF)


def attention_back_kernel(q_cols, k_cols, s_ref, rot_ref, grad_ref, cos_ref, sin_ref, out_ref, acc_ref):
    length = rot_ref.shape[0]
    step = min(256, length)
    acc_ref[...] = jnp.zeros_like(acc_ref)
    heads = q_cols // HD
    share = q_cols // k_cols
    scale = HD ** (-0.5)
    for head in range(heads):
        at = head * HD
        key_at = q_cols + head // share * HD
        value_at = key_at + k_cols
        for begin in range(0, length, step):
            end = begin + step
            query = rot_ref[begin:end, at : at + HD]
            key = rot_ref[:end, key_at : key_at + HD]
            grad = grad_ref[begin:end, at : at + HD]
            weights = soft(query, key, begin)
            grad_weights = dot(grad, rot_ref[:end, value_at : value_at + HD], ((1,), (1,)))
            delta = jnp.sum(weights * grad_weights, axis=1, keepdims=True)
            grad_scores = (weights * (grad_weights - delta)).astype(BF)
            acc_ref[begin:end, at : at + HD] = dot(grad_scores, key, ((1,), (0,))) * scale
            acc_ref[:end, key_at : key_at + HD] += dot(grad_scores, query, ((0,), (0,))) * scale
            acc_ref[:end, value_at : value_at + HD] += dot(weights.astype(BF), grad, ((0,), (0,)))
    for begin in range(0, length, step):
        part = slice(begin, begin + step)
        for low in range(0, out_ref.shape[1], 128):
            out_ref[part, low : low + 128] = turn(
                acc_ref[part, low : low + 128], cos_ref[part], -sin_ref[part], low, q_cols + k_cols
            ).astype(BF)


def middle_kernel(s_ref, mix_ref, out_ref, x_ref, routes_ref, gains_ref, rest_ref, message_ref, mid_ref):
    rows, width = x_ref.shape
    mid = x_ref[...].astype(F32)
    for t in range(mix_ref.shape[0]):
        mid += dot(mix_ref[t], out_ref[t], ((1,), (1,)))
    mid_ref[...] = mid
    b = (normalize(mid)[0] * gains_ref[1:2]).astype(BF)
    message_ref[:, :width] = b
    logits = dot(b, rest_ref[...], ((1,), (0,)))
    lane = lax.broadcasted_iota(jnp.int32, (rows, PAD), 1)
    routed = lane < 0
    for k in range(routes_ref.shape[1]):
        routed |= lane == routes_ref[:, k : k + 1]
    logits = jnp.where(routed, logits, NEG_LARGE)
    exponent = jnp.where(routed, jnp.exp(logits - jnp.max(logits, axis=1, keepdims=True)), 0.0)
    gating = exponent / jnp.sum(exponent, axis=1, keepdims=True)
    high = gating.astype(BF).astype(F32)
    low = pltpu.roll(gating - high, EXPERTS, axis=1)
    message_ref[:, width:] = jnp.where(lane < EXPERTS, high, low).astype(BF)


def join_tail(tail):
    lane = lax.broadcasted_iota(jnp.int32, tail.shape, 1)
    return jnp.where(lane < EXPERTS, tail + pltpu.roll(tail, PAD - EXPERTS, axis=1), 0.0)


def middle_back_kernel(parts, s_ref, *refs):
    sums = refs[:parts]
    mid_ref, message_ref, dy_ref, gains_ref, rest_ref, out_ref = refs[parts : parts + 6]
    grad_mid_ref, attention_ref, mix_ref, tail_ref = refs[len(refs) - 4 :]
    rows, width = mid_ref.shape
    total = sums[0][...].astype(F32)
    for ref in sums[1:]:
        total += ref[...].astype(F32)
    gating = join_tail(message_ref[:, width:].astype(F32))
    grad_gating = join_tail(total[:, width:])
    grad_logits = gating * (grad_gating - jnp.sum(gating * grad_gating, axis=1, keepdims=True))
    grad_logits = grad_logits.astype(BF)
    grad_b = total[:, :width] + dot(grad_logits, rest_ref[...], ((1,), (1,)))
    unit, inverse = normalize(mid_ref[...])
    grad_mid = dy_ref[...].astype(F32) + norm_backward(grad_b * gains_ref[1:2], unit, inverse)
    grad_mid_ref[...] = grad_mid
    attention = grad_mid.astype(BF)
    attention_ref[...] = attention
    for t in range(out_ref.shape[0]):
        mix_ref[t] = dot(attention, out_ref[t], ((1,), (0,))).astype(BF)
    lane = lax.broadcasted_iota(jnp.int32, (rows, PAD), 1)
    ones = jnp.where(lane == EXPERTS, 1.0, 0.0).astype(BF)
    tail_ref[...] = (
        dot(message_ref[:, :width], grad_logits, ((0,), (0,)))
        + dot((grad_b * unit).astype(BF), ones, ((0,), (0,)))
    ).astype(BF)


def pack_kernel(
    s_ref, a_ref, grad_ref, attention_ref, mix_ref, qkv_ref, rest_ref, tail_ref, main_ref, tail_out_ref
):
    late = dot(a_ref[...], grad_ref[...], ((0,), (0,)))
    columns = late.shape[1]
    main_ref[:, :columns] = late.astype(BF)
    main_ref[:, columns:] = dot(attention_ref[...], mix_ref[...], ((0,), (0,))).astype(BF)
    rest = rest_ref[...].astype(F32)
    lane = lax.broadcasted_iota(jnp.int32, rest.shape, 1)
    piece = (lane == EXPERTS) | (lane == EXPERTS + 2) | (lane == EXPERTS + 4)
    gain = jnp.sum(jnp.where(piece, rest, 0.0), axis=1, keepdims=True)
    gain_grad = jnp.sum(late * qkv_ref[...].astype(F32), axis=1, keepdims=True) / gain
    tail = tail_ref[...].astype(F32)
    tail_out_ref[...] = jnp.where(lane == EXPERTS + 1, gain_grad, tail).astype(BF)


def final_kernel(s_ref, rows_ref, qkv_ref, grad_mid_ref, x_ref, gains_ref, out_ref):
    grad_a = dot(rows_ref[0], qkv_ref[0], ((1,), (1,)))
    for t in range(1, rows_ref.shape[0]):
        grad_a += dot(rows_ref[t], qkv_ref[t], ((1,), (1,)))
    unit, inverse = normalize(x_ref[...].astype(F32))
    out_ref[...] = (
        grad_mid_ref[...] + norm_backward(grad_a * gains_ref[0:1], unit, inverse)
    ).astype(BF)


def body(
    ring,
    tensors,
    tokens,
    cotangent,
    routes,
    norm_gains,
    gains_moment,
    gains_second,
    query_weight,
    query_moment,
    query_second,
    keyval_weight,
    keyval_moment,
    keyval_second,
    output_weight,
    output_moment,
    output_second,
    router_weight,
    router_moment,
    router_second,
    gateup_weight,
    gateup_moment,
    gateup_second,
    down_weight,
    down_moment,
    down_second,
):
    length, width = tokens.shape
    rows = length // tensors
    experts = gateup_weight.shape[0]
    shape = jax.ShapeDtypeStruct
    lane_t = lax.axis_index("tensor").astype(jnp.int32).reshape(1)
    own_block = pl.BlockSpec((rows, width), lambda g, s: (s[0], 0))
    chips = tensors // 2

    gate_pieces = tensor_gather(gateup_weight[:, 0].astype(BF), tensors)
    up_pieces = tensor_gather(gateup_weight[:, 1].astype(BF), tensors)
    gate_low = jnp.concatenate(gate_pieces, axis=2)
    up_low = jnp.concatenate(up_pieces, axis=2)

    q_cols = query_weight.shape[1]
    k_cols = keyval_weight.shape[2]
    o_cols = output_weight.shape[0]
    heads_cols = q_cols + 2 * k_cols
    packed = jnp.concatenate(
        [
            query_weight.astype(BF),
            keyval_weight[0].astype(BF),
            keyval_weight[1].astype(BF),
            output_weight.T.astype(BF),
            router_weight.astype(BF),
        ]
        + split_pieces(norm_gains.T, 3)
        + [jnp.zeros((query_weight.shape[0], PAD - EXPERTS - 6), BF)],
        axis=1,
    )
    packed_blocks = ring_gather(packed, ring)
    offsets = sorted(packed_blocks)
    cosine_table, sine_table = rope_tables(length, HD)
    cosine_table = jnp.concatenate([cosine_table] * 4, axis=1)
    sine_table = jnp.concatenate([-sine_table, sine_table] * 2, axis=1)
    down_bf = down_weight.astype(BF)
    qkv_low, out_low, rest = place(
        [packed_blocks[o] for o in offsets],
        jnp.stack([ring_index(ring, o) for o in offsets]).astype(jnp.int32),
        cuts=[
            (0, heads_cols),
            (heads_cols, heads_cols + o_cols),
            (heads_cols + o_cols, heads_cols + o_cols + PAD),
        ],
        after=gate_pieces[1:chips] + up_pieces[1:chips] + [cosine_table, sine_table, down_bf],
    )
    gains_all = (
        rest[:, EXPERTS : EXPERTS + 2].astype(F32)
        + rest[:, EXPERTS + 2 : EXPERTS + 4].astype(F32)
        + rest[:, EXPERTS + 4 : EXPERTS + 6].astype(F32)
    ).T
    dy_own = lax.dynamic_slice_in_dim(cotangent, lane_t[0] * rows, rows, axis=0)
    dy_all = lax.all_gather(
        hold(dy_own, [packed_blocks[-(ring // 4)]]), "expert", axis=0, tiled=True
    )
    a, rotated, mixture = call_whole(
        functools.partial(front_kernel, q_cols, k_cols),
        [shape((length, width), BF), shape((length, heads_cols), BF), shape((length, q_cols), BF)],
        [tokens, gains_all, qkv_low, cosine_table, sine_table],
        "attention_forward",
        cost=10**10,
    )

    mixture_rows = lax.all_to_all(
        mixture.reshape(tensors, rows, o_cols), "tensor", split_axis=0, concat_axis=0, tiled=True
    )
    owners_t = tensor_index(tensors)
    out_pieces = tensor_gather(out_low, tensors, after=[mixture])
    out_all = place(out_pieces, owners_t, after=[mixture_rows]).reshape(tensors, width, o_cols)
    down_pieces = tensor_gather(hold(down_bf, out_pieces[1:chips]), tensors)
    down_low = jnp.concatenate(down_pieces, axis=1)
    message, x_mid = call_whole(
        middle_kernel,
        [shape((rows, width + PAD), BF), shape((rows, width), F32)],
        [mixture_rows, out_all, tokens, routes, gains_all, rest],
        "middle",
        scalars=lane_t,
        specs={2: own_block, 3: pl.BlockSpec((rows, routes.shape[1]), lambda g, s: (s[0], 0))},
        cost=10**9,
    )
    blocks = ring_gather(message, ring)

    half = ring // 2
    first = (lax.axis_index("expert") * experts).astype(jnp.int32)
    calls = [[0]] + [[-k, k] for k in range(1, half - 1)] + [[-half, half - 1], [1 - half]]
    back = {}
    forth = {}
    grads = []
    scaled = []
    order = []
    spots = []
    after = []
    for number, call in enumerate(calls):
        owners = [ring_index(ring, o).astype(jnp.int32) * min(abs(o), 1) for o in call]
        result = expert_blocks(
            first,
            [blocks[o] for o in call],
            owners,
            [dy_own if o == 0 else dy_all for o in call],
            gate_low,
            up_low,
            down_low,
            after,
        )
        grads.append(result[0])
        scaled.append(result[1])
        after = [result[1]]
        for part, o in enumerate(call):
            forth[o], back[o] = result[2][part], result[3][part]
            order.append(o)
            spots.append((number, part, rows))

    still = jnp.zeros((ring,), jnp.int32)
    whose = jnp.stack([ring_index(ring, o) for o in order]).astype(jnp.int32)
    messages = [blocks[o] for o in order]
    weights = {}

    def beside(hop, sent):
        kind = max(hop - 1, 0)
        if hop > 3 or kind in weights:
            return []
        if kind == 0:
            weights[0] = weight_grad([dy_all] * ring, whose, spots, scaled, 0, True, tensors, sent[:1])
        else:
            weights[kind] = weight_grad(
                messages, still, spots, grads, kind - 1, False, tensors, sent[:1]
            )
        if hop == 2:
            sums = place([forth[o] for o in order], whose, after=sent[:1])
            weights["sum"] = lax.psum_scatter(sums, "expert", scatter_dimension=0, tiled=True)
        return [weights[kind][0]]

    returned, after = ring_reduce(lambda offset: back[offset], ring, beside)
    up_grads, gate_grads, down_grads = weights[2], weights[1], weights[0]
    moe_sum = weights["sum"]
    block_out = place(tensor_gather((x_mid + moe_sum.astype(F32)).astype(BF), tensors), owners_t)

    grad_mid, grad_attention, grad_mixture, tail = call_whole(
        functools.partial(middle_back_kernel, len(returned)),
        [
            shape((rows, width), F32),
            shape((rows, width), BF),
            shape((tensors, rows, o_cols), BF),
            shape((width, PAD), BF),
        ],
        returned + [x_mid, message, cotangent, gains_all, rest, out_all] + after,
        "middle_backward",
        scalars=lane_t,
        specs={
            len(returned) + 2: own_block,
            len(returned) + 6: pl.BlockSpec(memory_space=pl.ANY),
        },
        cost=10**9,
    )
    grad_mixture = lax.all_to_all(
        grad_mixture, "tensor", split_axis=0, concat_axis=0, tiled=True
    ).reshape(length, o_cols)
    grad_attention_all = place(tensor_gather(grad_attention, tensors), owners_t)
    (grad_pre,) = call_whole(
        functools.partial(attention_back_kernel, q_cols, k_cols),
        [shape((length, heads_cols), BF)],
        [rotated, grad_mixture, cosine_table, sine_table],
        "attention_backward",
        scratch=[pltpu.VMEM((length, heads_cols), F32)],
        cost=2 * 10**10,
    )
    grad_pre_rows = lax.all_to_all(
        grad_pre.reshape(tensors, rows, heads_cols), "tensor", split_axis=0, concat_axis=0, tiled=True
    )
    main, tail = call_whole(
        pack_kernel,
        [shape((width, heads_cols + o_cols), BF), shape((width, PAD), BF)],
        [a, grad_pre, grad_attention_all, mixture, qkv_low, rest, tail],
        "pack",
        cost=4 * 10**9,
    )
    tail = tensor_sum(tail, tensors)
    qkv_all = lax.all_gather(hold(qkv_low, [scaled[1]]), "tensor")
    (input_grad,) = call_whole(
        final_kernel,
        [shape((rows, width), BF)],
        [grad_pre_rows, qkv_all, grad_mid, tokens, gains_all],
        "input_gradient",
        scalars=lane_t,
        specs={3: own_block},
        cost=2 * 10**9,
    )
    pieces = cut(
        main,
        tail,
        jnp.stack([ring_index(ring, o) for o in offsets]).astype(jnp.int32),
        [input_grad],
    )
    pieces = dict(zip(offsets, pieces))
    summed, _ = ring_reduce(lambda offset: pieces[offset], ring)
    input_grad = place(tensor_gather(input_grad, tensors), owners_t)
    new_rest = adamw_rest(
        q_cols,
        k_cols,
        summed,
        [
            [norm_gains, gains_moment, gains_second],
            [query_weight, query_moment, query_second],
            [keyval_weight, keyval_moment, keyval_second],
            [output_weight, output_moment, output_second],
            [router_weight, router_moment, router_second],
        ],
    )

    new_gateup = adamw_blocks(
        gateup_weight,
        gateup_moment,
        gateup_second,
        [tensor_reduce(gate_grads, tensors), tensor_reduce(up_grads, tensors)],
    )
    new_down = [
        array[:, 0]
        for array in adamw_blocks(
            down_weight[:, None],
            down_moment[:, None],
            down_second[:, None],
            [tensor_reduce(down_grads, tensors)],
        )
    ]
    return (block_out, input_grad) + tuple(new_rest) + tuple(new_gateup) + tuple(new_down)


def solution(mesh):
    rows = P("expert", None)
    gains = P(None, "expert")
    query = P("expert", "tensor")
    keyval = P(None, "expert", "tensor")
    output = P("tensor", "expert")
    gateup = P("expert", None, None, "tensor")
    down = P("expert", "tensor", None)
    weights = tuple(
        spec for spec in (gains, query, keyval, output, rows, gateup, down) for _ in range(3)
    )
    return jax.shard_map(
        functools.partial(body, mesh.shape["expert"], mesh.shape["tensor"]),
        mesh=mesh,
        in_specs=(rows, rows, rows) + weights,
        out_specs=(rows, rows) + weights,
        check_vma=False,
    )
```

```python
import functools

import jax
import jax.numpy as jnp
from jax import lax
from jax.experimental import pallas as pl
from jax.experimental.pallas import tpu as pltpu
from jax.sharding import PartitionSpec as P

HEADS = 16
KV_HEADS = 8
HD = 64
EXPERTS = 32
STEP = 10
PAD = 128

NORM_EPS = 1e-06
BETA_ONE = 0.9
BETA_TWO = 0.999
ADAM_EPS = 1e-08
MATRIX_RATE = 0.08
GAIN_RATE = 0.6
MATRIX_DECAY = 0.1
NEG_LARGE = -1e30
BF = jnp.bfloat16
F32 = jnp.float32


def dot(left, right, dims):
    return lax.dot_general(left, right, (dims, ((), ())), preferred_element_type=F32)


def normalize(values):
    inverse = lax.rsqrt(jnp.mean(values * values, axis=-1, keepdims=True) + NORM_EPS)
    return (values * inverse, inverse)


def norm_backward(grad_unit, unit, inverse):
    return inverse * (grad_unit - unit * jnp.mean(grad_unit * unit, axis=-1, keepdims=True))


def rope_tables(length, head_size):
    half_size = head_size // 2
    frequency = 10000.0 ** (-(jnp.arange(half_size, dtype=F32) * 2.0) / head_size)
    angles = jnp.arange(length, dtype=F32)[:, None] * frequency[None, :]
    return (jnp.cos(angles), jnp.sin(angles))


def adamw_update(weight, moment, second, gradient, rate, decay):
    moment_new = BETA_ONE * moment + (1.0 - BETA_ONE) * gradient
    second_new = BETA_TWO * second + (1.0 - BETA_TWO) * gradient * gradient
    fix_one = 1.0 - BETA_ONE**STEP
    fix_two = 1.0 - BETA_TWO**STEP
    update = moment_new / fix_one / (jnp.sqrt(second_new / fix_two) + ADAM_EPS)
    return (weight - rate * (update + decay * weight), moment_new, second_new)


def split_pieces(values, count):
    pieces = []
    for _ in range(count):
        high = lax.reduce_precision(values, 8, 7)
        pieces.append(high.astype(BF))
        values = values - high
    return pieces


def ring_order(size):
    return list(range(0, size, 2)) + list(range(1, size, 2))[::-1]


def ring_perm(size, step):
    order = ring_order(size)
    return [(order[i], order[(i + step) % size]) for i in range(size)]


def ring_index(size, offset):
    me = lax.axis_index("expert")
    place = jnp.where(me % 2 == 0, me // 2, size - 1 - me // 2)
    place = (place + offset) % size
    return jnp.where(place < (size + 1) // 2, 2 * place, 2 * (size - 1 - place) + 1)


def ring_gather(block, size):
    blocks = {0: block}
    ahead = behind = block
    for hop in range(1, size // 2 + 1):
        ahead = lax.ppermute(ahead, "expert", ring_perm(size, 1))
        blocks[-hop] = ahead
        if hop <= (size - 1) // 2:
            behind = lax.ppermute(behind, "expert", ring_perm(size, -1))
            blocks[hop] = behind
    return blocks


def ring_reduce(part, size, beside=None):
    down = up = None
    after = []
    for hop in range(size // 2, 0, -1):
        side = hop - 1
        if down is None:
            messages = [part(-hop), part(side)]
        else:
            pairs = [(down, part(-hop))] + ([(up, part(side))] if side > 0 else [])
            messages = add_pairs(pairs, after)
            after = beside(hop, messages) if beside else []
        down = lax.ppermute(messages[0], "expert", ring_perm(size, -1))
        if side > 0:
            up = lax.ppermute(messages[1], "expert", ring_perm(size, 1))
    return [part(0), down, up], after


def tensor_perm(size, along, core):
    chips = size // 2
    return [(t, ((t // 2 + along) % chips) * 2 + ((t % 2) ^ core)) for t in range(size)]


def tensor_gather(shard, size, after=()):
    own = [shard] + [
        lax.ppermute(shard, "tensor", tensor_perm(size, -step, 0)) for step in range(1, size // 2)
    ]
    ready = [hold(piece, after) for piece in own] if after else own
    other = [lax.ppermute(piece, "tensor", tensor_perm(size, 0, 1)) for piece in ready]
    return own + other


def core_sums(parts, size):
    chips = size // 2
    came = [lax.ppermute(part, "tensor", tensor_perm(size, 0, 1)) for part in parts[chips:]]
    return [parts[0], came[0]] + [
        (part.astype(F32) + other.astype(F32)).astype(BF)
        for part, other in zip(parts[1:chips], came[1:])
    ]


def chip_sums(sums, size):
    return sums[:2] + [
        lax.ppermute(total, "tensor", tensor_perm(size, step + 1, 0))
        for step, total in enumerate(sums[2:])
    ]


def tensor_sum(values, size):
    values = values + lax.ppermute(values, "tensor", tensor_perm(size, 0, 1))
    moved = [
        lax.ppermute(values, "tensor", tensor_perm(size, step, 0)) for step in range(1, size // 2)
    ]
    return sum(moved, values)


def place_kernel(blocks, cuts, *refs):
    index_ref = refs[0]
    outs = refs[len(refs) - len(cuts) :]
    for block in range(blocks):
        source = refs[1 + block]
        size = source.shape[0]
        start = pl.multiple_of(index_ref[block] * size, size)
        for (low, high), out in zip(cuts, outs):
            out[pl.ds(start, size), :] = source[:, low:high]


def place(blocks, index, cuts=None, after=()):
    size, columns = blocks[0].shape
    cuts = cuts or [(0, columns)]
    count = len(blocks)
    vmem = pl.BlockSpec(memory_space=pltpu.VMEM)
    out = pl.pallas_call(
        functools.partial(place_kernel, count, cuts),
        in_specs=[pl.BlockSpec(memory_space=pltpu.SMEM)]
        + [vmem] * count
        + [pl.BlockSpec(memory_space=pl.ANY)] * len(after),
        out_specs=[vmem] * len(cuts),
        out_shape=[
            jax.ShapeDtypeStruct((count * size, high - low), blocks[0].dtype) for low, high in cuts
        ],
        compiler_params=pltpu.CompilerParams(vmem_limit_bytes=32 * 1024 * 1024),
        name="place",
    )(index, *blocks, *after)
    return out if len(cuts) > 1 else out[0]


def place_far_kernel(blocks, *refs):
    index_ref, out_ref, sems = refs[0], refs[-2], refs[-1]
    copies = []
    for block in range(blocks):
        size = refs[1 + block].shape[0]
        start = pl.multiple_of(index_ref[block] * size, size)
        copies.append(
            pltpu.make_async_copy(refs[1 + block], out_ref.at[pl.ds(start, size)], sems.at[block])
        )
        copies[-1].start()
    for copy in copies:
        copy.wait()


def place_far(blocks, index, after=()):
    size, columns = blocks[0].shape
    count = len(blocks)
    return pl.pallas_call(
        functools.partial(place_far_kernel, count),
        in_specs=[pl.BlockSpec(memory_space=pltpu.SMEM)]
        + [pl.BlockSpec(memory_space=pl.ANY)] * (count + len(after)),
        out_specs=pl.BlockSpec(memory_space=pl.ANY),
        out_shape=jax.ShapeDtypeStruct((count * size, columns), blocks[0].dtype),
        scratch_shapes=[pltpu.SemaphoreType.DMA((count,))],
        name="place_far",
    )(index, *blocks, *after)


def hold(array, after):
    flat = array.reshape(-1, array.shape[-1])
    return place([flat], jnp.zeros((1,), jnp.int32), after=after).reshape(array.shape)


def cut_kernel(blocks, s_ref, main_ref, tail_ref, *refs):
    outs = refs[len(refs) - blocks :]
    for i, out in enumerate(outs):
        size = out.shape[0]
        part = pl.ds(pl.multiple_of(s_ref[i] * size, size), size)
        out[:, : main_ref.shape[1]] = main_ref[part, :]
        out[:, main_ref.shape[1] :] = tail_ref[part, :]


def cut(main, tail, index, after):
    count = index.shape[0]
    vmem = pl.BlockSpec(memory_space=pltpu.VMEM)
    block = (main.shape[0] // count, main.shape[1] + tail.shape[1])
    return pl.pallas_call(
        functools.partial(cut_kernel, count),
        in_specs=[pl.BlockSpec(memory_space=pltpu.SMEM), vmem, vmem]
        + [pl.BlockSpec(memory_space=pl.ANY)] * len(after),
        out_specs=[vmem] * count,
        out_shape=[jax.ShapeDtypeStruct(block, main.dtype)] * count,
        compiler_params=pltpu.CompilerParams(vmem_limit_bytes=32 * 1024 * 1024),
        name="cut",
    )(index, main, tail, *after)


def add_kernel(count, *refs):
    outs = refs[len(refs) - count :]
    for i, out in enumerate(outs):
        out[...] = (refs[2 * i][...].astype(F32) + refs[2 * i + 1][...].astype(F32)).astype(BF)


def add_pairs(pairs, after):
    vmem = pl.BlockSpec(memory_space=pltpu.VMEM)
    return pl.pallas_call(
        functools.partial(add_kernel, len(pairs)),
        in_specs=[vmem] * (2 * len(pairs)) + [pl.BlockSpec(memory_space=pl.ANY)] * len(after),
        out_specs=[vmem] * len(pairs),
        out_shape=[jax.ShapeDtypeStruct(pair[0].shape, BF) for pair in pairs],
        compiler_params=pltpu.CompilerParams(vmem_limit_bytes=32 * 1024 * 1024),
        name="add_pairs",
    )(*[array for pair in pairs for array in pair], *after)


def tensor_index(size):
    me = lax.axis_index("tensor")
    chips = size // 2
    chip, core = me // 2, me % 2
    own = [((chip + step) % chips) * 2 + core for step in range(chips)]
    other = [((chip + step) % chips) * 2 + (1 - core) for step in range(chips)]
    return jnp.stack(own + other).astype(jnp.int32)


def expert_kernel(count, afters, *refs):
    first_ref = refs[0]
    message_refs = refs[1 : 1 + count]
    cotangent_refs = refs[1 + count : 1 + 2 * count]
    gate_ref, up_ref, down_ref = refs[1 + 2 * count : 4 + 2 * count]
    outs = refs[4 + 2 * count + afters :]
    grads_ref, scaled_ref = outs[:2]
    y_refs = outs[2 : 2 + count]
    back_refs = outs[2 + count : 2 + 2 * count]
    rows_ref, dy_ref, y_acc, back_acc, tail_acc = outs[2 + 2 * count :]
    expert = pl.program_id(0)
    rows, width = cotangent_refs[0].shape

    @pl.when(expert == 0)
    def _():
        for i in range(count):
            rows_ref[i * rows : (i + 1) * rows] = message_refs[i][...]
            dy_ref[i * rows : (i + 1) * rows] = cotangent_refs[i][...]
        y_acc[...] = jnp.zeros_like(y_acc)
        back_acc[...] = jnp.zeros_like(back_acc)
        tail_acc[...] = jnp.zeros_like(tail_acc)

    gate_w = gate_ref[0]
    up_w = up_ref[0]
    down_w = down_ref[0]
    column = first_ref[0] + expert
    b = rows_ref[:, :width]
    gate_pre = dot(b, gate_w, ((1,), (0,)))
    up_pre = dot(b, up_w, ((1,), (0,)))
    grad_act = dot(dy_ref[...], down_w, ((1,), (1,)))
    sig = 0.5 * jnp.tanh(0.5 * gate_pre) + 0.5
    silu = gate_pre * sig
    act = (silu * up_pre).astype(BF).astype(F32)
    grad_gating = jnp.sum(act * grad_act, axis=1, keepdims=True)
    lane = lax.broadcasted_iota(jnp.int32, (count * rows, PAD), 1)
    chosen = (lane == column) | (lane == column + EXPERTS)
    tail = rows_ref[:, width:].astype(F32)
    gating = jnp.sum(jnp.where(chosen, tail, 0.0), axis=1, keepdims=True)
    tail_acc[...] += jnp.where(chosen, grad_gating, 0.0)
    grad_act = grad_act * gating
    grad_gate = (grad_act * up_pre * (sig + silu * (1.0 - sig))).astype(BF)
    grad_up = (grad_act * silu).astype(BF)
    scaled = (act * gating).astype(BF)
    grads_ref[0, 0] = grad_gate
    grads_ref[1, 0] = grad_up
    scaled_ref[0] = scaled
    back_acc[...] += dot(grad_gate, gate_w, ((1,), (1,))) + dot(grad_up, up_w, ((1,), (1,)))
    y_acc[...] += dot(scaled, down_w, ((1,), (0,)))

    @pl.when(expert == pl.num_programs(0) - 1)
    def _():
        lane = lax.broadcasted_iota(jnp.int32, (rows, PAD), 1)
        for i in range(count):
            part = slice(i * rows, (i + 1) * rows)
            y_refs[i][...] = y_acc[part].astype(BF)
            total = tail_acc[part]
            high = total.astype(BF).astype(F32)
            back_refs[i][:, :width] = back_acc[part].astype(BF)
            back_refs[i][:, width:] = jnp.where(lane < EXPERTS, high, total - high).astype(BF)


def expert_blocks(first, messages, owners, cotangents, gate, up, down, after):
    experts, width, hidden = gate.shape
    rows, message = messages[0].shape
    count = len(messages)
    block = pl.BlockSpec((rows, message), lambda e, s: (0, 0))
    plain = pl.BlockSpec((rows, width), lambda e, s: (0, 0))
    owned = [pl.BlockSpec((rows, width), lambda e, s, i=i: (s[1 + i], 0)) for i in range(count)]
    shape = jax.ShapeDtypeStruct
    out = pl.pallas_call(
        functools.partial(expert_kernel, count, len(after)),
        grid_spec=pltpu.PrefetchScalarGridSpec(
            num_scalar_prefetch=1,
            grid=(experts,),
            in_specs=[block] * count
            + owned
            + [pl.BlockSpec((1, width, hidden), lambda e, s: (e, 0, 0))] * 2
            + [pl.BlockSpec((1, hidden, width), lambda e, s: (e, 0, 0))]
            + [pl.BlockSpec(memory_space=pl.ANY)] * len(after),
            out_specs=[
                pl.BlockSpec((2, 1, count * rows, hidden), lambda e, s: (0, e, 0, 0)),
                pl.BlockSpec((1, count * rows, hidden), lambda e, s: (e, 0, 0)),
            ]
            + [plain] * count
            + [block] * count,
            scratch_shapes=[
                pltpu.VMEM((count * rows, message), BF),
                pltpu.VMEM((count * rows, width), BF),
                pltpu.VMEM((count * rows, width), F32),
                pltpu.VMEM((count * rows, width), F32),
                pltpu.VMEM((count * rows, PAD), F32),
            ],
        ),
        out_shape=[
            shape((2, experts, count * rows, hidden), BF),
            shape((experts, count * rows, hidden), BF),
        ]
        + [shape((rows, width), BF)] * count
        + [shape((rows, message), BF)] * count,
        compiler_params=pltpu.CompilerParams(vmem_limit_bytes=60 * 1024 * 1024),
        cost_estimate=pl.CostEstimate(
            flops=12 * count * rows * experts * width * hidden,
            bytes_accessed=6 * experts * width * hidden,
            transcendentals=count * rows * experts * hidden,
        ),
        name="expert_blocks",
    )(jnp.stack([first] + owners), *messages, *cotangents, gate, up, down, *after)
    return out[0], out[1], out[2 : 2 + count], out[2 + count :]


def weight_grad_kernel(spots, swap, shards, afters, *refs):
    blocks = len(spots)
    outs = refs[len(refs) - shards :]
    total = None
    for block, (call, part, rows) in enumerate(spots):
        grads_ref = refs[1 + blocks + call]
        lead = (0,) * (len(grads_ref.shape) - 2)
        grads = grads_ref[lead + (slice(part * rows, (part + 1) * rows),)]
        pair = (grads, refs[1 + block][...]) if swap else (refs[1 + block][...], grads)
        term = dot(*pair, ((0,), (0,)))
        total = term if total is None else total + term
    total = total.astype(BF)
    size = total.shape[0 if swap else 1] // shards
    for i, out in enumerate(outs):
        cut = slice(i * size, (i + 1) * size)
        out[0] = total[cut] if swap else total[:, cut]


def weight_grad(inputs, owners, spots, grads, pick, swap, shards, after):
    lead = grads[0].ndim == 4
    experts, _, hidden = grads[0].shape[-3:]
    rows = spots[0][2]
    width = inputs[0].shape[1] - (PAD if lead else 0)
    blocks = len(inputs)
    shape = (hidden // shards, width) if swap else (width, hidden // shards)
    in_specs = [pl.BlockSpec((rows, width), lambda e, s, i=i: (s[i], 0)) for i in range(blocks)]
    for array in grads:
        if lead:
            in_specs.append(pl.BlockSpec((1, 1) + array.shape[2:], lambda e, s: (pick, e, 0, 0)))
        else:
            in_specs.append(pl.BlockSpec((1,) + array.shape[1:], lambda e, s: (e, 0, 0)))
    in_specs += [pl.BlockSpec(memory_space=pl.ANY)] * len(after)
    return pl.pallas_call(
        functools.partial(weight_grad_kernel, spots, swap, shards, len(after)),
        grid_spec=pltpu.PrefetchScalarGridSpec(
            num_scalar_prefetch=1,
            grid=(experts,),
            in_specs=in_specs,
            out_specs=[pl.BlockSpec((1,) + shape, lambda e, s: (e, 0, 0))] * shards,
        ),
        out_shape=[jax.ShapeDtypeStruct((experts,) + shape, BF)] * shards,
        compiler_params=pltpu.CompilerParams(vmem_limit_bytes=60 * 1024 * 1024),
        cost_estimate=pl.CostEstimate(
            flops=2 * blocks * rows * experts * width * hidden,
            bytes_accessed=4 * blocks * rows * width,
            transcendentals=0,
        ),
        name="weight_grad",
    )(owners, *inputs, *grads, *after)


def adamw_kernel(kinds, parts, *refs):
    weight_ref, moment_ref, second_ref = refs[:3]
    outs = refs[len(refs) - 3 :]
    for kind in range(kinds):
        gradient = refs[3 + kind * parts][0].astype(F32)
        for i in range(1, parts):
            gradient += refs[3 + kind * parts + i][0].astype(F32)
        new = adamw_update(
            weight_ref[0, kind],
            moment_ref[0, kind],
            second_ref[0, kind],
            gradient,
            MATRIX_RATE,
            MATRIX_DECAY,
        )
        for out, value in zip(outs, new):
            out[0, kind] = value


def adamw_blocks(weight, moment, second, gradients):
    experts, kinds, high, wide = weight.shape
    parts = len(gradients[0])
    whole = pl.BlockSpec((1, kinds, high, wide), lambda e: (e, 0, 0, 0))
    return pl.pallas_call(
        functools.partial(adamw_kernel, kinds, parts),
        grid=(experts,),
        in_specs=[whole] * 3 + [pl.BlockSpec((1, high, wide), lambda e: (e, 0, 0))] * (kinds * parts),
        out_specs=[whole] * 3,
        out_shape=[jax.ShapeDtypeStruct(weight.shape, F32)] * 3,
        compiler_params=pltpu.CompilerParams(vmem_limit_bytes=60 * 1024 * 1024),
        cost_estimate=pl.CostEstimate(
            flops=20 * weight.size, bytes_accessed=28 * weight.size, transcendentals=weight.size
        ),
        name="adamw",
    )(weight, moment, second, *[part for kind in gradients for part in kind])


def adamw_rest_kernel(q_cols, k_cols, s_ref, *refs):
    total = refs[0][...].astype(F32) + refs[1][...].astype(F32) + refs[2][...].astype(F32)
    arrays, outs = refs[3:18], refs[18:]
    gains, query, keyval, output, router = (arrays[i : i + 3] for i in range(0, 15, 3))
    new_gains, new_query, new_keyval, new_output, new_router = (
        outs[i : i + 3] for i in range(0, 15, 3)
    )

    def update(refs, outs, where, gradient, rate, decay):
        new = adamw_update(*[ref[where] for ref in refs], gradient, rate, decay)
        for out, value in zip(outs, new):
            out[where] = value

    heads_cols = q_cols + 2 * k_cols
    o_cols = output[0].shape[0]
    every = (slice(None), slice(None))
    update(query, new_query, every, total[:, :q_cols], MATRIX_RATE, MATRIX_DECAY)
    for kind in range(2):
        low = q_cols + kind * k_cols
        update(
            keyval, new_keyval, (kind,) + every, total[:, low : low + k_cols], MATRIX_RATE, MATRIX_DECAY
        )
    turned = total[:, heads_cols : heads_cols + o_cols].T
    update(output, new_output, every, turned, MATRIX_RATE, MATRIX_DECAY)
    ends = total[:, heads_cols + o_cols :]
    update(router, new_router, every, ends[:, :EXPERTS], MATRIX_RATE, MATRIX_DECAY)
    turned = ends.T
    for kind in range(2):
        at = EXPERTS + 1 - kind
        where = (slice(kind, kind + 1), slice(None))
        update(gains, new_gains, where, turned[at : at + 1], GAIN_RATE, 0.0)


def adamw_rest(q_cols, k_cols, parts, groups):
    arrays = [array for group in groups for array in group]
    return call_whole(
        functools.partial(adamw_rest_kernel, q_cols, k_cols),
        [jax.ShapeDtypeStruct(array.shape, F32) for array in arrays],
        parts + arrays,
        "adamw_rest",
        cost=10**8,
    )


def call_whole(kernel, out_shape, operands, name, scalars=None, specs=None, scratch=(), cost=0):
    specs = specs or {}
    scalars = jnp.zeros((1,), jnp.int32) if scalars is None else scalars
    return pl.pallas_call(
        kernel,
        grid_spec=pltpu.PrefetchScalarGridSpec(
            num_scalar_prefetch=1,
            grid=(1,),
            in_specs=[
                specs.get(i, pl.BlockSpec(array.shape, lambda g, s, n=array.ndim: (0,) * n))
                for i, array in enumerate(operands)
            ],
            out_specs=[
                pl.BlockSpec(shape.shape, lambda g, s, n=len(shape.shape): (0,) * n)
                for shape in out_shape
            ],
            scratch_shapes=list(scratch),
        ),
        out_shape=out_shape,
        compiler_params=pltpu.CompilerParams(vmem_limit_bytes=60 * 1024 * 1024),
        cost_estimate=pl.CostEstimate(flops=cost, bytes_accessed=1 << 22, transcendentals=0),
        name=name,
    )(scalars, *operands)


def swap_halves(chunk):
    columns = chunk.shape[1]
    lane = lax.broadcasted_iota(jnp.int32, chunk.shape, 1)
    return jnp.where(
        lane % HD < HD // 2,
        pltpu.roll(chunk, columns - HD // 2, axis=1),
        pltpu.roll(chunk, HD // 2, axis=1),
    )


def turn(chunk, cosine, sine, begin, end):
    if begin >= end:
        return chunk
    turned = chunk * cosine + swap_halves(chunk) * sine
    if begin + chunk.shape[1] <= end:
        return turned
    lane = lax.broadcasted_iota(jnp.int32, chunk.shape, 1)
    return jnp.where(lane + begin < end, turned, chunk)


def soft(query, key, begin):
    scores = dot(query, key, ((1,), (1,))) * HD ** (-0.5)
    row = lax.broadcasted_iota(jnp.int32, scores.shape, 0) + begin
    scores = jnp.where(row >= lax.broadcasted_iota(jnp.int32, scores.shape, 1), scores, NEG_LARGE)
    exponent = jnp.exp(scores - jnp.max(scores, axis=1, keepdims=True))
    return exponent * (1.0 / jnp.sum(exponent, axis=1, keepdims=True))


def front_kernel(q_cols, k_cols, s_ref, x_ref, gains_ref, qkv_ref, cos_ref, sin_ref, a_ref, rot_ref, mix_ref):
    length = x_ref.shape[0]
    step = min(256, length)
    for begin in range(0, length, step):
        part = slice(begin, begin + step)
        x = x_ref[part].astype(F32)
        a = (normalize(x)[0] * gains_ref[0:1]).astype(BF)
        a_ref[part] = a
        pre = dot(a, qkv_ref[...], ((1,), (0,)))
        for low in range(0, pre.shape[1], 128):
            rot_ref[part, low : low + 128] = turn(
                pre[:, low : low + 128], cos_ref[part], sin_ref[part], low, q_cols + k_cols
            ).astype(BF)
    heads = q_cols // HD
    share = q_cols // k_cols
    for head in range(heads):
        at = head * HD
        key_at = q_cols + head // share * HD
        value_at = key_at + k_cols
        for begin in range(0, length, step):
            end = begin + step
            weights = soft(rot_ref[begin:end, at : at + HD], rot_ref[:end, key_at : key_at + HD], begin)
            mix_ref[begin:end, at : at + HD] = dot(
                weights.astype(BF), rot_ref[:end, value_at : value_at + HD], ((1,), (0,))
            ).astype(BF)


def attention_back_kernel(
    q_cols, k_cols, s_ref, rot_ref, grad_ref, cos_ref, sin_ref, after_ref, out_ref, acc_ref
):
    length = rot_ref.shape[0]
    step = min(256, length)
    acc_ref[...] = jnp.zeros_like(acc_ref)
    heads = q_cols // HD
    share = q_cols // k_cols
    scale = HD ** (-0.5)
    for head in range(heads):
        at = head * HD
        key_at = q_cols + head // share * HD
        value_at = key_at + k_cols
        for begin in range(0, length, step):
            end = begin + step
            query = rot_ref[begin:end, at : at + HD]
            key = rot_ref[:end, key_at : key_at + HD]
            grad = grad_ref[begin:end, at : at + HD]
            weights = soft(query, key, begin)
            grad_weights = dot(grad, rot_ref[:end, value_at : value_at + HD], ((1,), (1,)))
            delta = jnp.sum(weights * grad_weights, axis=1, keepdims=True)
            grad_scores = (weights * (grad_weights - delta)).astype(BF)
            acc_ref[begin:end, at : at + HD] = dot(grad_scores, key, ((1,), (0,))) * scale
            acc_ref[:end, key_at : key_at + HD] += dot(grad_scores, query, ((0,), (0,))) * scale
            acc_ref[:end, value_at : value_at + HD] += dot(weights.astype(BF), grad, ((0,), (0,)))
    for begin in range(0, length, step):
        part = slice(begin, begin + step)
        for low in range(0, out_ref.shape[1], 128):
            out_ref[part, low : low + 128] = turn(
                acc_ref[part, low : low + 128], cos_ref[part], -sin_ref[part], low, q_cols + k_cols
            ).astype(BF)


def middle_kernel(s_ref, mix_ref, out_ref, x_ref, routes_ref, gains_ref, rest_ref, message_ref, mid_ref):
    rows, width = x_ref.shape
    mid = x_ref[...].astype(F32)
    for t in range(mix_ref.shape[0]):
        mid += dot(mix_ref[t], out_ref[t], ((1,), (1,)))
    mid_ref[...] = mid
    b = (normalize(mid)[0] * gains_ref[1:2]).astype(BF)
    message_ref[:, :width] = b
    logits = dot(b, rest_ref[...], ((1,), (0,)))
    lane = lax.broadcasted_iota(jnp.int32, (rows, PAD), 1)
    routed = lane < 0
    for k in range(routes_ref.shape[1]):
        routed |= lane == routes_ref[:, k : k + 1]
    logits = jnp.where(routed, logits, NEG_LARGE)
    exponent = jnp.where(routed, jnp.exp(logits - jnp.max(logits, axis=1, keepdims=True)), 0.0)
    gating = exponent / jnp.sum(exponent, axis=1, keepdims=True)
    high = gating.astype(BF).astype(F32)
    low = pltpu.roll(gating - high, EXPERTS, axis=1)
    message_ref[:, width:] = jnp.where(lane < EXPERTS, high, low).astype(BF)


def join_tail(tail):
    lane = lax.broadcasted_iota(jnp.int32, tail.shape, 1)
    return jnp.where(lane < EXPERTS, tail + pltpu.roll(tail, PAD - EXPERTS, axis=1), 0.0)


def middle_back_kernel(parts, s_ref, *refs):
    sums = refs[:parts]
    mid_ref, message_ref, dy_ref, gains_ref, rest_ref, out_ref = refs[parts : parts + 6]
    grad_mid_ref, attention_ref, mix_ref, tail_ref = refs[len(refs) - 4 :]
    rows, width = mid_ref.shape
    total = sums[0][...].astype(F32)
    for ref in sums[1:]:
        total += ref[...].astype(F32)
    gating = join_tail(message_ref[:, width:].astype(F32))
    grad_gating = join_tail(total[:, width:])
    grad_logits = gating * (grad_gating - jnp.sum(gating * grad_gating, axis=1, keepdims=True))
    grad_logits = grad_logits.astype(BF)
    grad_b = total[:, :width] + dot(grad_logits, rest_ref[...], ((1,), (1,)))
    unit, inverse = normalize(mid_ref[...])
    grad_mid = dy_ref[...].astype(F32) + norm_backward(grad_b * gains_ref[1:2], unit, inverse)
    grad_mid_ref[...] = grad_mid
    attention = grad_mid.astype(BF)
    attention_ref[...] = attention
    for t in range(out_ref.shape[0]):
        mix_ref[t] = dot(attention, out_ref[t], ((1,), (0,))).astype(BF)
    lane = lax.broadcasted_iota(jnp.int32, (rows, PAD), 1)
    ones = jnp.where(lane == EXPERTS, 1.0, 0.0).astype(BF)
    tail_ref[...] = (
        dot(message_ref[:, :width], grad_logits, ((0,), (0,)))
        + dot((grad_b * unit).astype(BF), ones, ((0,), (0,)))
    ).astype(BF)


def pack_kernel(
    s_ref, a_ref, grad_ref, attention_ref, mix_ref, qkv_ref, rest_ref, tail_ref, main_ref, tail_out_ref
):
    late = dot(a_ref[...], grad_ref[...], ((0,), (0,)))
    columns = late.shape[1]
    main_ref[:, :columns] = late.astype(BF)
    main_ref[:, columns:] = dot(attention_ref[...], mix_ref[...], ((0,), (0,))).astype(BF)
    rest = rest_ref[...].astype(F32)
    lane = lax.broadcasted_iota(jnp.int32, rest.shape, 1)
    piece = (lane == EXPERTS) | (lane == EXPERTS + 2) | (lane == EXPERTS + 4)
    gain = jnp.sum(jnp.where(piece, rest, 0.0), axis=1, keepdims=True)
    gain_grad = jnp.sum(late * qkv_ref[...].astype(F32), axis=1, keepdims=True) / gain
    tail = tail_ref[...].astype(F32)
    tail_out_ref[...] = jnp.where(lane == EXPERTS + 1, gain_grad, tail).astype(BF)


def final_kernel(s_ref, rows_ref, qkv_ref, grad_mid_ref, x_ref, gains_ref, out_ref):
    grad_a = dot(rows_ref[0], qkv_ref[0], ((1,), (1,)))
    for t in range(1, rows_ref.shape[0]):
        grad_a += dot(rows_ref[t], qkv_ref[t], ((1,), (1,)))
    unit, inverse = normalize(x_ref[...].astype(F32))
    out_ref[...] = (
        grad_mid_ref[...] + norm_backward(grad_a * gains_ref[0:1], unit, inverse)
    ).astype(BF)


def body(
    ring,
    tensors,
    tokens,
    cotangent,
    routes,
    norm_gains,
    gains_moment,
    gains_second,
    query_weight,
    query_moment,
    query_second,
    keyval_weight,
    keyval_moment,
    keyval_second,
    output_weight,
    output_moment,
    output_second,
    router_weight,
    router_moment,
    router_second,
    gateup_weight,
    gateup_moment,
    gateup_second,
    down_weight,
    down_moment,
    down_second,
):
    length, width = tokens.shape
    rows = length // tensors
    experts = gateup_weight.shape[0]
    shape = jax.ShapeDtypeStruct
    lane_t = lax.axis_index("tensor").astype(jnp.int32).reshape(1)
    own_block = pl.BlockSpec((rows, width), lambda g, s: (s[0], 0))
    chips = tensors // 2

    gate_bf = gateup_weight[:, 0].astype(BF)
    up_bf = gateup_weight[:, 1].astype(BF)
    gate_pieces = tensor_gather(gate_bf, tensors)
    up_pieces = tensor_gather(up_bf, tensors)
    gate_low = jnp.concatenate(gate_pieces, axis=2)
    up_low = jnp.concatenate(up_pieces, axis=2)

    q_cols = query_weight.shape[1]
    k_cols = keyval_weight.shape[2]
    o_cols = output_weight.shape[0]
    heads_cols = q_cols + 2 * k_cols
    packed = jnp.concatenate(
        [
            query_weight.astype(BF),
            keyval_weight[0].astype(BF),
            keyval_weight[1].astype(BF),
            output_weight.T.astype(BF),
            router_weight.astype(BF),
        ]
        + split_pieces(norm_gains.T, 3)
        + [jnp.zeros((query_weight.shape[0], PAD - EXPERTS - 6), BF)],
        axis=1,
    )
    packed_blocks = ring_gather(hold(packed, [gate_bf, up_bf]), ring)
    offsets = sorted(packed_blocks)
    cosine_table, sine_table = rope_tables(length, HD)
    cosine_table = jnp.concatenate([cosine_table] * 4, axis=1)
    sine_table = jnp.concatenate([-sine_table, sine_table] * 2, axis=1)
    down_bf = down_weight.astype(BF)
    qkv_low, out_low, rest = place(
        [packed_blocks[o] for o in offsets],
        jnp.stack([ring_index(ring, o) for o in offsets]).astype(jnp.int32),
        cuts=[
            (0, heads_cols),
            (heads_cols, heads_cols + o_cols),
            (heads_cols + o_cols, heads_cols + o_cols + PAD),
        ],
        after=gate_pieces[1:chips] + up_pieces[1:chips] + [cosine_table, sine_table, down_bf],
    )
    gains_all = (
        rest[:, EXPERTS : EXPERTS + 2].astype(F32)
        + rest[:, EXPERTS + 2 : EXPERTS + 4].astype(F32)
        + rest[:, EXPERTS + 4 : EXPERTS + 6].astype(F32)
    ).T
    dy_own = lax.dynamic_slice_in_dim(cotangent, lane_t[0] * rows, rows, axis=0)
    dy_all = lax.all_gather(
        hold(dy_own, [packed_blocks[1 - ring // 2]]), "expert", axis=0, tiled=True
    )
    a, rotated, mixture = call_whole(
        functools.partial(front_kernel, q_cols, k_cols),
        [shape((length, width), BF), shape((length, heads_cols), BF), shape((length, q_cols), BF)],
        [tokens, gains_all, qkv_low, cosine_table, sine_table],
        "attention_forward",
        cost=10**10,
    )

    mixture_rows = lax.all_to_all(
        mixture.reshape(tensors, rows, o_cols), "tensor", split_axis=0, concat_axis=0, tiled=True
    )
    owners_t = tensor_index(tensors)
    out_pieces = tensor_gather(out_low, tensors, after=[mixture])
    out_all = place(out_pieces, owners_t, after=[mixture_rows]).reshape(tensors, width, o_cols)
    down_pieces = tensor_gather(hold(down_bf, [mixture]), tensors)
    down_low = jnp.concatenate(down_pieces, axis=1)
    message, x_mid = call_whole(
        middle_kernel,
        [shape((rows, width + PAD), BF), shape((rows, width), F32)],
        [mixture_rows, out_all, tokens, routes, gains_all, rest],
        "middle",
        scalars=lane_t,
        specs={2: own_block, 3: pl.BlockSpec((rows, routes.shape[1]), lambda g, s: (s[0], 0))},
        cost=10**9,
    )
    blocks = ring_gather(message, ring)

    half = ring // 2
    first = (lax.axis_index("expert") * experts).astype(jnp.int32)
    calls = [[0]] + [[-k, k] for k in range(1, half - 1)] + [[-half, half - 1], [1 - half]]
    back = {}
    forth = {}
    grads = []
    scaled = []
    order = []
    spots = []
    for number, call in enumerate(calls):
        hop = min(number + 1, half)
        after = [blocks[o] for o in (-hop, hop) if o in blocks and o not in call]
        after += scaled[-1:]
        owners = [ring_index(ring, o).astype(jnp.int32) * min(abs(o), 1) for o in call]
        result = expert_blocks(
            first,
            [blocks[o] for o in call],
            owners,
            [dy_own if o == 0 else dy_all for o in call],
            gate_low,
            up_low,
            down_low,
            after,
        )
        grads.append(result[0])
        scaled.append(result[1])
        for part, o in enumerate(call):
            forth[o], back[o] = result[2][part], result[3][part]
            order.append(o)
            spots.append((number, part, rows))

    still = jnp.zeros((ring,), jnp.int32)
    whose = jnp.stack([ring_index(ring, o) for o in order]).astype(jnp.int32)
    messages = [blocks[o] for o in order]
    weights = {}
    totals = {}

    def beside(hop, sent):
        kind = max(hop - 1, 0)
        if hop > 3 or kind in weights:
            return []
        if kind == 0:
            weights[0] = weight_grad([dy_all] * ring, whose, spots, scaled, 0, True, tensors, sent[:1])
        else:
            weights[kind] = weight_grad(
                messages, still, spots, grads, kind - 1, False, tensors, sent[:1]
            )
        early = [totals[done][-1] for done in totals]
        totals[kind] = core_sums(weights[kind], tensors)
        return [weights[kind][0]] + early

    returned, after = ring_reduce(lambda offset: back[offset], ring, beside)
    sums = place_far([forth[o] for o in order], whose, after=[returned[1]])
    moe_sum = lax.psum_scatter(sums, "expert", scatter_dimension=0, tiled=True)
    block_out = place(tensor_gather((x_mid + moe_sum.astype(F32)).astype(BF), tensors), owners_t)

    grad_mid, grad_attention, grad_mixture, tail = call_whole(
        functools.partial(middle_back_kernel, len(returned)),
        [
            shape((rows, width), F32),
            shape((rows, width), BF),
            shape((tensors, rows, o_cols), BF),
            shape((width, PAD), BF),
        ],
        returned + [x_mid, message, cotangent, gains_all, rest, out_all] + after,
        "middle_backward",
        scalars=lane_t,
        specs={
            len(returned) + 2: own_block,
            **{
                len(returned) + 6 + i: pl.BlockSpec(memory_space=pl.ANY) for i in range(len(after))
            },
        },
        cost=10**9,
    )
    grad_mixture = lax.all_to_all(
        grad_mixture, "tensor", split_axis=0, concat_axis=0, tiled=True
    ).reshape(length, o_cols)
    grad_attention_all = place(tensor_gather(grad_attention, tensors), owners_t)
    (grad_pre,) = call_whole(
        functools.partial(attention_back_kernel, q_cols, k_cols),
        [shape((length, heads_cols), BF)],
        [rotated, grad_mixture, cosine_table, sine_table, totals[0][-1]],
        "attention_backward",
        specs={4: pl.BlockSpec(memory_space=pl.ANY)},
        scratch=[pltpu.VMEM((length, heads_cols), F32)],
        cost=2 * 10**10,
    )
    grad_pre_rows = lax.all_to_all(
        grad_pre.reshape(tensors, rows, heads_cols), "tensor", split_axis=0, concat_axis=0, tiled=True
    )
    main, tail = call_whole(
        pack_kernel,
        [shape((width, heads_cols + o_cols), BF), shape((width, PAD), BF)],
        [a, grad_pre, grad_attention_all, mixture, qkv_low, rest, tail],
        "pack",
        cost=4 * 10**9,
    )
    tail = tensor_sum(tail, tensors)
    qkv_all = lax.all_gather(hold(qkv_low, [scaled[1]]), "tensor")
    (input_grad,) = call_whole(
        final_kernel,
        [shape((rows, width), BF)],
        [grad_pre_rows, qkv_all, grad_mid, tokens, gains_all],
        "input_gradient",
        scalars=lane_t,
        specs={3: own_block},
        cost=2 * 10**9,
    )
    pieces = cut(
        main,
        tail,
        jnp.stack([ring_index(ring, o) for o in offsets]).astype(jnp.int32),
        [input_grad],
    )
    pieces = dict(zip(offsets, pieces))
    summed, _ = ring_reduce(lambda offset: pieces[offset], ring)
    input_grad = place(tensor_gather(input_grad, tensors), owners_t)
    new_rest = adamw_rest(
        q_cols,
        k_cols,
        summed,
        [
            [norm_gains, gains_moment, gains_second],
            [query_weight, query_moment, query_second],
            [keyval_weight, keyval_moment, keyval_second],
            [output_weight, output_moment, output_second],
            [router_weight, router_moment, router_second],
        ],
    )

    new_gateup = adamw_blocks(
        gateup_weight,
        gateup_moment,
        gateup_second,
        [chip_sums(totals[1], tensors), chip_sums(totals[2], tensors)],
    )
    new_down = [
        array[:, 0]
        for array in adamw_blocks(
            down_weight[:, None],
            down_moment[:, None],
            down_second[:, None],
            [chip_sums(totals[0], tensors)],
        )
    ]
    return (block_out, input_grad) + tuple(new_rest) + tuple(new_gateup) + tuple(new_down)


def solution(mesh):
    rows = P("expert", None)
    gains = P(None, "expert")
    query = P("expert", "tensor")
    keyval = P(None, "expert", "tensor")
    output = P("tensor", "expert")
    gateup = P("expert", None, None, "tensor")
    down = P("expert", "tensor", None)
    weights = tuple(
        spec for spec in (gains, query, keyval, output, rows, gateup, down) for _ in range(3)
    )
    return jax.shard_map(
        functools.partial(body, mesh.shape["expert"], mesh.shape["tensor"]),
        mesh=mesh,
        in_specs=(rows, rows, rows) + weights,
        out_specs=(rows, rows) + weights,
        check_vma=False,
    )
```

```python
import functools

import jax
import jax.numpy as jnp
from jax import lax
from jax.experimental import pallas as pl
from jax.experimental.pallas import tpu as pltpu
from jax.sharding import PartitionSpec as P

HEADS = 16
KV_HEADS = 8
HD = 64
EXPERTS = 32
STEP = 10
PAD = 128

NORM_EPS = 1e-06
BETA_ONE = 0.9
BETA_TWO = 0.999
ADAM_EPS = 1e-08
MATRIX_RATE = 0.08
GAIN_RATE = 0.6
MATRIX_DECAY = 0.1
NEG_LARGE = -1e30
BF = jnp.bfloat16
F32 = jnp.float32


def dot(left, right, dims):
    return lax.dot_general(left, right, (dims, ((), ())), preferred_element_type=F32)


def normalize(values):
    inverse = lax.rsqrt(jnp.mean(values * values, axis=-1, keepdims=True) + NORM_EPS)
    return (values * inverse, inverse)


def norm_backward(grad_unit, unit, inverse):
    return inverse * (grad_unit - unit * jnp.mean(grad_unit * unit, axis=-1, keepdims=True))


def rope_tables(length, head_size):
    half_size = head_size // 2
    frequency = 10000.0 ** (-(jnp.arange(half_size, dtype=F32) * 2.0) / head_size)
    angles = jnp.arange(length, dtype=F32)[:, None] * frequency[None, :]
    return (jnp.cos(angles), jnp.sin(angles))


def adamw_update(weight, moment, second, gradient, rate, decay):
    moment_new = BETA_ONE * moment + (1.0 - BETA_ONE) * gradient
    second_new = BETA_TWO * second + (1.0 - BETA_TWO) * gradient * gradient
    fix_one = 1.0 - BETA_ONE**STEP
    fix_two = 1.0 - BETA_TWO**STEP
    update = moment_new / fix_one / (jnp.sqrt(second_new / fix_two) + ADAM_EPS)
    return (weight - rate * (update + decay * weight), moment_new, second_new)


def split_pieces(values, count):
    pieces = []
    for _ in range(count):
        high = lax.reduce_precision(values, 8, 7)
        pieces.append(high.astype(BF))
        values = values - high
    return pieces


def ring_order(size):
    return list(range(0, size, 2)) + list(range(1, size, 2))[::-1]


def ring_perm(size, step):
    order = ring_order(size)
    return [(order[i], order[(i + step) % size]) for i in range(size)]


def ring_index(size, offset):
    me = lax.axis_index("expert")
    place = jnp.where(me % 2 == 0, me // 2, size - 1 - me // 2)
    place = (place + offset) % size
    return jnp.where(place < (size + 1) // 2, 2 * place, 2 * (size - 1 - place) + 1)


def ring_gather(block, size):
    blocks = {0: block}
    ahead = behind = block
    for hop in range(1, size // 2 + 1):
        ahead = lax.ppermute(ahead, "expert", ring_perm(size, 1))
        blocks[-hop] = ahead
        if hop <= (size - 1) // 2:
            behind = lax.ppermute(behind, "expert", ring_perm(size, -1))
            blocks[hop] = behind
    return blocks


def ring_reduce(part, size, beside=None):
    down = up = None
    after = []
    move = lambda arrays, step: [lax.ppermute(x, "expert", ring_perm(size, step)) for x in arrays]
    for hop in range(size // 2, 0, -1):
        side = hop - 1
        lower = part(-hop)
        upper = part(side) if side > 0 else []
        if down is not None:
            pairs = list(zip(down, lower)) + (list(zip(up, upper)) if side > 0 else [])
            messages = add_pairs(pairs, after)
            lower, upper = messages[: len(lower)], messages[len(lower) :]
            after = beside(hop, messages) if beside else []
        down = move(lower, -1)
        if side > 0:
            up = move(upper, 1)
    return [list(terms) for terms in zip(part(0), down, up)], after


def tensor_perm(size, along, core):
    chips = size // 2
    return [(t, ((t // 2 + along) % chips) * 2 + ((t % 2) ^ core)) for t in range(size)]


def tensor_gather(shard, size, after=()):
    own = [shard] + [
        lax.ppermute(shard, "tensor", tensor_perm(size, -step, 0)) for step in range(1, size // 2)
    ]
    ready = [hold(piece, after) for piece in own] if after else own
    other = [lax.ppermute(piece, "tensor", tensor_perm(size, 0, 1)) for piece in ready]
    return own + other


def core_sums(parts, size):
    chips = size // 2
    came = [lax.ppermute(part, "tensor", tensor_perm(size, 0, 1)) for part in parts[chips:]]
    return [parts[0], came[0]] + [
        (part.astype(F32) + other.astype(F32)).astype(BF)
        for part, other in zip(parts[1:chips], came[1:])
    ]


def chip_sums(sums, size):
    return sums[:2] + [
        lax.ppermute(total, "tensor", tensor_perm(size, step + 1, 0))
        for step, total in enumerate(sums[2:])
    ]


def tensor_sum(values, size):
    values = values + lax.ppermute(values, "tensor", tensor_perm(size, 0, 1))
    moved = [
        lax.ppermute(values, "tensor", tensor_perm(size, step, 0)) for step in range(1, size // 2)
    ]
    return sum(moved, values)


def place_kernel(blocks, cuts, *refs):
    index_ref = refs[0]
    outs = refs[len(refs) - len(cuts) :]
    for block in range(blocks):
        source = refs[1 + block]
        size = source.shape[0]
        start = pl.multiple_of(index_ref[block] * size, size)
        for (low, high), out in zip(cuts, outs):
            out[pl.ds(start, size), :] = source[:, low:high]


def place(blocks, index, cuts=None, after=()):
    size, columns = blocks[0].shape
    cuts = cuts or [(0, columns)]
    count = len(blocks)
    vmem = pl.BlockSpec(memory_space=pltpu.VMEM)
    out = pl.pallas_call(
        functools.partial(place_kernel, count, cuts),
        in_specs=[pl.BlockSpec(memory_space=pltpu.SMEM)]
        + [vmem] * count
        + [pl.BlockSpec(memory_space=pl.ANY)] * len(after),
        out_specs=[vmem] * len(cuts),
        out_shape=[
            jax.ShapeDtypeStruct((count * size, high - low), blocks[0].dtype) for low, high in cuts
        ],
        compiler_params=pltpu.CompilerParams(vmem_limit_bytes=32 * 1024 * 1024),
        name="place",
    )(index, *blocks, *after)
    return out if len(cuts) > 1 else out[0]


def hold(array, after):
    flat = array.reshape(-1, array.shape[-1])
    return place([flat], jnp.zeros((1,), jnp.int32), after=after).reshape(array.shape)


def cut_kernel(blocks, s_ref, main_ref, tail_ref, *refs):
    outs = refs[len(refs) - blocks :]
    for i, out in enumerate(outs):
        size = out.shape[0]
        part = pl.ds(pl.multiple_of(s_ref[i] * size, size), size)
        out[:, : main_ref.shape[1]] = main_ref[part, :]
        out[:, main_ref.shape[1] :] = tail_ref[part, :]


def cut(main, tail, index, after):
    count = index.shape[0]
    vmem = pl.BlockSpec(memory_space=pltpu.VMEM)
    block = (main.shape[0] // count, main.shape[1] + tail.shape[1])
    return pl.pallas_call(
        functools.partial(cut_kernel, count),
        in_specs=[pl.BlockSpec(memory_space=pltpu.SMEM), vmem, vmem]
        + [pl.BlockSpec(memory_space=pl.ANY)] * len(after),
        out_specs=[vmem] * count,
        out_shape=[jax.ShapeDtypeStruct(block, main.dtype)] * count,
        compiler_params=pltpu.CompilerParams(vmem_limit_bytes=32 * 1024 * 1024),
        name="cut",
    )(index, main, tail, *after)


def add_kernel(count, *refs):
    outs = refs[len(refs) - count :]
    for i, out in enumerate(outs):
        out[...] = (refs[2 * i][...].astype(F32) + refs[2 * i + 1][...].astype(F32)).astype(BF)


def add_pairs(pairs, after):
    steps = 4 if pairs[0][0].shape[0] >= 256 else 1
    spec = lambda array: pl.BlockSpec((array.shape[0] // steps, array.shape[1]), lambda i: (i, 0))
    return pl.pallas_call(
        functools.partial(add_kernel, len(pairs)),
        grid=(steps,),
        in_specs=[spec(array) for pair in pairs for array in pair]
        + [pl.BlockSpec(memory_space=pl.ANY)] * len(after),
        out_specs=[spec(pair[0]) for pair in pairs],
        out_shape=[jax.ShapeDtypeStruct(pair[0].shape, BF) for pair in pairs],
        compiler_params=pltpu.CompilerParams(vmem_limit_bytes=60 * 1024 * 1024),
        name="add_pairs",
    )(*[array for pair in pairs for array in pair], *after)


def tensor_index(size):
    me = lax.axis_index("tensor")
    chips = size // 2
    chip, core = me // 2, me % 2
    own = [((chip + step) % chips) * 2 + core for step in range(chips)]
    other = [((chip + step) % chips) * 2 + (1 - core) for step in range(chips)]
    return jnp.stack(own + other).astype(jnp.int32)


def expert_kernel(count, afters, *refs):
    first_ref = refs[0]
    message_refs = refs[1 : 1 + count]
    cotangent_refs = refs[1 + count : 1 + 2 * count]
    weights_ref = refs[1 + 2 * count]
    outs = refs[2 + 2 * count + afters :]
    grads_ref, scaled_ref = outs[:2]
    y_refs = outs[2 : 2 + count]
    back_refs = outs[2 + count : 2 + 2 * count]
    rows_ref, dy_ref, y_acc, back_acc, tail_acc = outs[2 + 2 * count :]
    expert = pl.program_id(0)
    rows, width = cotangent_refs[0].shape

    @pl.when(expert == 0)
    def _():
        for i in range(count):
            rows_ref[i * rows : (i + 1) * rows] = message_refs[i][...]
            dy_ref[i * rows : (i + 1) * rows] = cotangent_refs[i][...]
        y_acc[...] = jnp.zeros_like(y_acc)
        back_acc[...] = jnp.zeros_like(back_acc)
        tail_acc[...] = jnp.zeros_like(tail_acc)

    gate_w = weights_ref[0, 0]
    up_w = weights_ref[1, 0]
    down_w = weights_ref[2, 0]
    column = first_ref[0] + expert
    b = rows_ref[:, :width]
    gate_pre = dot(b, gate_w, ((1,), (0,)))
    up_pre = dot(b, up_w, ((1,), (0,)))
    grad_act = dot(dy_ref[...], down_w, ((1,), (0,)))
    sig = 0.5 * jnp.tanh(0.5 * gate_pre) + 0.5
    silu = gate_pre * sig
    act = (silu * up_pre).astype(BF).astype(F32)
    grad_gating = jnp.sum(act * grad_act, axis=1, keepdims=True)
    lane = lax.broadcasted_iota(jnp.int32, (count * rows, PAD), 1)
    chosen = (lane == column) | (lane == column + EXPERTS)
    tail = rows_ref[:, width:].astype(F32)
    gating = jnp.sum(jnp.where(chosen, tail, 0.0), axis=1, keepdims=True)
    tail_acc[...] += jnp.where(chosen, grad_gating, 0.0)
    grad_act = grad_act * gating
    grad_gate = (grad_act * up_pre * (sig + silu * (1.0 - sig))).astype(BF)
    grad_up = (grad_act * silu).astype(BF)
    scaled = (act * gating).astype(BF)
    grads_ref[0, 0] = grad_gate
    grads_ref[1, 0] = grad_up
    scaled_ref[0] = scaled
    back_acc[...] += dot(grad_gate, gate_w, ((1,), (1,))) + dot(grad_up, up_w, ((1,), (1,)))
    y_acc[...] += dot(scaled, down_w, ((1,), (1,)))

    @pl.when(expert == pl.num_programs(0) - 1)
    def _():
        lane = lax.broadcasted_iota(jnp.int32, (rows, PAD), 1)
        for i in range(count):
            part = slice(i * rows, (i + 1) * rows)
            y_refs[i][...] = y_acc[part].astype(BF)
            total = tail_acc[part]
            high = total.astype(BF).astype(F32)
            back_refs[i][:, :width] = back_acc[part].astype(BF)
            back_refs[i][:, width:] = jnp.where(lane < EXPERTS, high, total - high).astype(BF)


def expert_blocks(first, messages, owners, cotangents, weights, after):
    _, experts, width, hidden = weights.shape
    rows, message = messages[0].shape
    count = len(messages)
    block = pl.BlockSpec((rows, message), lambda e, s: (0, 0))
    plain = pl.BlockSpec((rows, width), lambda e, s: (0, 0))
    owned = [pl.BlockSpec((rows, width), lambda e, s, i=i: (s[1 + i], 0)) for i in range(count)]
    shape = jax.ShapeDtypeStruct
    out = pl.pallas_call(
        functools.partial(expert_kernel, count, len(after)),
        grid_spec=pltpu.PrefetchScalarGridSpec(
            num_scalar_prefetch=1,
            grid=(experts,),
            in_specs=[block] * count
            + owned
            + [pl.BlockSpec((3, 1, width, hidden), lambda e, s: (0, e, 0, 0))]
            + [pl.BlockSpec(memory_space=pl.ANY)] * len(after),
            out_specs=[
                pl.BlockSpec((2, 1, count * rows, hidden), lambda e, s: (0, e, 0, 0)),
                pl.BlockSpec((1, count * rows, hidden), lambda e, s: (e, 0, 0)),
            ]
            + [plain] * count
            + [block] * count,
            scratch_shapes=[
                pltpu.VMEM((count * rows, message), BF),
                pltpu.VMEM((count * rows, width), BF),
                pltpu.VMEM((count * rows, width), F32),
                pltpu.VMEM((count * rows, width), F32),
                pltpu.VMEM((count * rows, PAD), F32),
            ],
        ),
        out_shape=[
            shape((2, experts, count * rows, hidden), BF),
            shape((experts, count * rows, hidden), BF),
        ]
        + [shape((rows, width), BF)] * count
        + [shape((rows, message), BF)] * count,
        compiler_params=pltpu.CompilerParams(vmem_limit_bytes=60 * 1024 * 1024),
        cost_estimate=pl.CostEstimate(
            flops=12 * count * rows * experts * width * hidden,
            bytes_accessed=6 * experts * width * hidden,
            transcendentals=count * rows * experts * hidden,
        ),
        name="expert_blocks",
    )(jnp.stack([first] + owners), *messages, *cotangents, weights, *after)
    return out[0], out[1], out[2 : 2 + count], out[2 + count :]


def weight_grad_kernel(spots, swap, shards, afters, *refs):
    blocks = len(spots)
    outs = refs[len(refs) - shards :]
    total = None
    for block, (call, part, rows) in enumerate(spots):
        grads_ref = refs[1 + blocks + call]
        lead = (0,) * (len(grads_ref.shape) - 2)
        grads = grads_ref[lead + (slice(part * rows, (part + 1) * rows),)]
        pair = (grads, refs[1 + block][...]) if swap else (refs[1 + block][...], grads)
        term = dot(*pair, ((0,), (0,)))
        total = term if total is None else total + term
    total = total.astype(BF)
    size = total.shape[0 if swap else 1] // shards
    for i, out in enumerate(outs):
        cut = slice(i * size, (i + 1) * size)
        out[0] = total[cut] if swap else total[:, cut]


def weight_grad(inputs, owners, spots, grads, pick, swap, shards, after):
    lead = grads[0].ndim == 4
    experts, _, hidden = grads[0].shape[-3:]
    rows = spots[0][2]
    width = inputs[0].shape[1] - (PAD if lead else 0)
    blocks = len(inputs)
    shape = (hidden // shards, width) if swap else (width, hidden // shards)
    in_specs = [pl.BlockSpec((rows, width), lambda e, s, i=i: (s[i], 0)) for i in range(blocks)]
    for array in grads:
        if lead:
            in_specs.append(pl.BlockSpec((1, 1) + array.shape[2:], lambda e, s: (pick, e, 0, 0)))
        else:
            in_specs.append(pl.BlockSpec((1,) + array.shape[1:], lambda e, s: (e, 0, 0)))
    in_specs += [pl.BlockSpec(memory_space=pl.ANY)] * len(after)
    return pl.pallas_call(
        functools.partial(weight_grad_kernel, spots, swap, shards, len(after)),
        grid_spec=pltpu.PrefetchScalarGridSpec(
            num_scalar_prefetch=1,
            grid=(experts,),
            in_specs=in_specs,
            out_specs=[pl.BlockSpec((1,) + shape, lambda e, s: (e, 0, 0))] * shards,
        ),
        out_shape=[jax.ShapeDtypeStruct((experts,) + shape, BF)] * shards,
        compiler_params=pltpu.CompilerParams(vmem_limit_bytes=60 * 1024 * 1024),
        cost_estimate=pl.CostEstimate(
            flops=2 * blocks * rows * experts * width * hidden,
            bytes_accessed=4 * blocks * rows * width,
            transcendentals=0,
        ),
        name="weight_grad",
    )(owners, *inputs, *grads, *after)


def adamw_kernel(kinds, parts, *refs):
    weight_ref, moment_ref, second_ref = refs[:3]
    outs = refs[len(refs) - 3 :]
    for kind in range(kinds):
        gradient = refs[3 + kind * parts][0].astype(F32)
        for i in range(1, parts):
            gradient += refs[3 + kind * parts + i][0].astype(F32)
        new = adamw_update(
            weight_ref[0, kind],
            moment_ref[0, kind],
            second_ref[0, kind],
            gradient,
            MATRIX_RATE,
            MATRIX_DECAY,
        )
        for out, value in zip(outs, new):
            out[0, kind] = value


def adamw_blocks(weight, moment, second, gradients):
    experts, kinds, high, wide = weight.shape
    parts = len(gradients[0])
    whole = pl.BlockSpec((1, kinds, high, wide), lambda e: (e, 0, 0, 0))
    return pl.pallas_call(
        functools.partial(adamw_kernel, kinds, parts),
        grid=(experts,),
        in_specs=[whole] * 3 + [pl.BlockSpec((1, high, wide), lambda e: (e, 0, 0))] * (kinds * parts),
        out_specs=[whole] * 3,
        out_shape=[jax.ShapeDtypeStruct(weight.shape, F32)] * 3,
        compiler_params=pltpu.CompilerParams(vmem_limit_bytes=60 * 1024 * 1024),
        cost_estimate=pl.CostEstimate(
            flops=20 * weight.size, bytes_accessed=28 * weight.size, transcendentals=weight.size
        ),
        name="adamw",
    )(weight, moment, second, *[part for kind in gradients for part in kind])


def adamw_rest_kernel(q_cols, k_cols, s_ref, *refs):
    total = refs[0][...].astype(F32) + refs[1][...].astype(F32) + refs[2][...].astype(F32)
    arrays, outs = refs[3:18], refs[18:]
    gains, query, keyval, output, router = (arrays[i : i + 3] for i in range(0, 15, 3))
    new_gains, new_query, new_keyval, new_output, new_router = (
        outs[i : i + 3] for i in range(0, 15, 3)
    )

    def update(refs, outs, where, gradient, rate, decay):
        new = adamw_update(*[ref[where] for ref in refs], gradient, rate, decay)
        for out, value in zip(outs, new):
            out[where] = value

    heads_cols = q_cols + 2 * k_cols
    o_cols = output[0].shape[0]
    every = (slice(None), slice(None))
    update(query, new_query, every, total[:, :q_cols], MATRIX_RATE, MATRIX_DECAY)
    for kind in range(2):
        low = q_cols + kind * k_cols
        update(
            keyval, new_keyval, (kind,) + every, total[:, low : low + k_cols], MATRIX_RATE, MATRIX_DECAY
        )
    turned = total[:, heads_cols : heads_cols + o_cols].T
    update(output, new_output, every, turned, MATRIX_RATE, MATRIX_DECAY)
    ends = total[:, heads_cols + o_cols :]
    update(router, new_router, every, ends[:, :EXPERTS], MATRIX_RATE, MATRIX_DECAY)
    turned = ends.T
    for kind in range(2):
        at = EXPERTS + 1 - kind
        where = (slice(kind, kind + 1), slice(None))
        update(gains, new_gains, where, turned[at : at + 1], GAIN_RATE, 0.0)


def adamw_rest(q_cols, k_cols, parts, groups):
    arrays = [array for group in groups for array in group]
    return call_whole(
        functools.partial(adamw_rest_kernel, q_cols, k_cols),
        [jax.ShapeDtypeStruct(array.shape, F32) for array in arrays],
        parts + arrays,
        "adamw_rest",
        cost=10**8,
    )


def call_whole(kernel, out_shape, operands, name, scalars=None, specs=None, scratch=(), cost=0):
    specs = specs or {}
    scalars = jnp.zeros((1,), jnp.int32) if scalars is None else scalars
    return pl.pallas_call(
        kernel,
        grid_spec=pltpu.PrefetchScalarGridSpec(
            num_scalar_prefetch=1,
            grid=(1,),
            in_specs=[
                specs.get(i, pl.BlockSpec(array.shape, lambda g, s, n=array.ndim: (0,) * n))
                for i, array in enumerate(operands)
            ],
            out_specs=[
                pl.BlockSpec(shape.shape, lambda g, s, n=len(shape.shape): (0,) * n)
                for shape in out_shape
            ],
            scratch_shapes=list(scratch),
        ),
        out_shape=out_shape,
        compiler_params=pltpu.CompilerParams(vmem_limit_bytes=60 * 1024 * 1024),
        cost_estimate=pl.CostEstimate(flops=cost, bytes_accessed=1 << 22, transcendentals=0),
        name=name,
    )(scalars, *operands)


def swap_halves(chunk):
    columns = chunk.shape[1]
    lane = lax.broadcasted_iota(jnp.int32, chunk.shape, 1)
    return jnp.where(
        lane % HD < HD // 2,
        pltpu.roll(chunk, columns - HD // 2, axis=1),
        pltpu.roll(chunk, HD // 2, axis=1),
    )


def turn(chunk, cosine, sine, begin, end):
    if begin >= end:
        return chunk
    turned = chunk * cosine + swap_halves(chunk) * sine
    if begin + chunk.shape[1] <= end:
        return turned
    lane = lax.broadcasted_iota(jnp.int32, chunk.shape, 1)
    return jnp.where(lane + begin < end, turned, chunk)


def soft(query, key, begin):
    scores = dot(query, key, ((1,), (1,))) * HD ** (-0.5)
    row = lax.broadcasted_iota(jnp.int32, scores.shape, 0) + begin
    scores = jnp.where(row >= lax.broadcasted_iota(jnp.int32, scores.shape, 1), scores, NEG_LARGE)
    exponent = jnp.exp(scores - jnp.max(scores, axis=1, keepdims=True))
    return exponent * (1.0 / jnp.sum(exponent, axis=1, keepdims=True))


def front_kernel(q_cols, k_cols, s_ref, x_ref, gains_ref, qkv_ref, cos_ref, sin_ref, a_ref, rot_ref, mix_ref):
    length = x_ref.shape[0]
    step = min(256, length)
    for begin in range(0, length, step):
        part = slice(begin, begin + step)
        x = x_ref[part].astype(F32)
        a = (normalize(x)[0] * gains_ref[0:1]).astype(BF)
        a_ref[part] = a
        pre = dot(a, qkv_ref[...], ((1,), (0,)))
        for low in range(0, pre.shape[1], 128):
            rot_ref[part, low : low + 128] = turn(
                pre[:, low : low + 128], cos_ref[part], sin_ref[part], low, q_cols + k_cols
            ).astype(BF)
    heads = q_cols // HD
    share = q_cols // k_cols
    for head in range(heads):
        at = head * HD
        key_at = q_cols + head // share * HD
        value_at = key_at + k_cols
        for begin in range(0, length, step):
            end = begin + step
            weights = soft(rot_ref[begin:end, at : at + HD], rot_ref[:end, key_at : key_at + HD], begin)
            mix_ref[begin:end, at : at + HD] = dot(
                weights.astype(BF), rot_ref[:end, value_at : value_at + HD], ((1,), (0,))
            ).astype(BF)


def attention_back_kernel(
    q_cols, k_cols, s_ref, rot_ref, grad_ref, cos_ref, sin_ref, after_ref, last_ref, out_ref, acc_ref
):
    length = rot_ref.shape[0]
    step = min(256, length)
    acc_ref[...] = jnp.zeros_like(acc_ref)
    heads = q_cols // HD
    share = q_cols // k_cols
    scale = HD ** (-0.5)
    for head in range(heads):
        at = head * HD
        key_at = q_cols + head // share * HD
        value_at = key_at + k_cols
        for begin in range(0, length, step):
            end = begin + step
            query = rot_ref[begin:end, at : at + HD]
            key = rot_ref[:end, key_at : key_at + HD]
            grad = grad_ref[begin:end, at : at + HD]
            weights = soft(query, key, begin)
            grad_weights = dot(grad, rot_ref[:end, value_at : value_at + HD], ((1,), (1,)))
            delta = jnp.sum(weights * grad_weights, axis=1, keepdims=True)
            grad_scores = (weights * (grad_weights - delta)).astype(BF)
            acc_ref[begin:end, at : at + HD] = dot(grad_scores, key, ((1,), (0,))) * scale
            acc_ref[:end, key_at : key_at + HD] += dot(grad_scores, query, ((0,), (0,))) * scale
            acc_ref[:end, value_at : value_at + HD] += dot(weights.astype(BF), grad, ((0,), (0,)))
    for begin in range(0, length, step):
        part = slice(begin, begin + step)
        for low in range(0, out_ref.shape[1], 128):
            out_ref[part, low : low + 128] = turn(
                acc_ref[part, low : low + 128], cos_ref[part], -sin_ref[part], low, q_cols + k_cols
            ).astype(BF)


def middle_kernel(s_ref, mix_ref, out_ref, x_ref, routes_ref, gains_ref, rest_ref, *more):
    message_ref, mid_ref = more[-2:]
    rows, width = x_ref.shape
    mid = x_ref[...].astype(F32)
    for t in range(mix_ref.shape[0]):
        mid += dot(mix_ref[t], out_ref[t], ((1,), (1,)))
    mid_ref[...] = mid
    b = (normalize(mid)[0] * gains_ref[1:2]).astype(BF)
    message_ref[:, :width] = b
    logits = dot(b, rest_ref[...], ((1,), (0,)))
    lane = lax.broadcasted_iota(jnp.int32, (rows, PAD), 1)
    routed = lane < 0
    for k in range(routes_ref.shape[1]):
        routed |= lane == routes_ref[:, k : k + 1]
    logits = jnp.where(routed, logits, NEG_LARGE)
    exponent = jnp.where(routed, jnp.exp(logits - jnp.max(logits, axis=1, keepdims=True)), 0.0)
    gating = exponent / jnp.sum(exponent, axis=1, keepdims=True)
    high = gating.astype(BF).astype(F32)
    low = pltpu.roll(gating - high, EXPERTS, axis=1)
    message_ref[:, width:] = jnp.where(lane < EXPERTS, high, low).astype(BF)


def join_tail(tail):
    lane = lax.broadcasted_iota(jnp.int32, tail.shape, 1)
    return jnp.where(lane < EXPERTS, tail + pltpu.roll(tail, PAD - EXPERTS, axis=1), 0.0)


def middle_back_kernel(parts, s_ref, *refs):
    sums = refs[:parts]
    mid_ref, message_ref, dy_ref, gains_ref, rest_ref, out_ref = refs[parts : parts + 6]
    grad_mid_ref, attention_ref, mix_ref, tail_ref = refs[len(refs) - 4 :]
    rows, width = mid_ref.shape
    total = sums[0][...].astype(F32)
    for ref in sums[1:]:
        total += ref[...].astype(F32)
    gating = join_tail(message_ref[:, width:].astype(F32))
    grad_gating = join_tail(total[:, width:])
    grad_logits = gating * (grad_gating - jnp.sum(gating * grad_gating, axis=1, keepdims=True))
    grad_logits = grad_logits.astype(BF)
    grad_b = total[:, :width] + dot(grad_logits, rest_ref[...], ((1,), (1,)))
    unit, inverse = normalize(mid_ref[...])
    grad_mid = dy_ref[...].astype(F32) + norm_backward(grad_b * gains_ref[1:2], unit, inverse)
    grad_mid_ref[...] = grad_mid
    attention = grad_mid.astype(BF)
    attention_ref[...] = attention
    for t in range(out_ref.shape[0]):
        mix_ref[t] = dot(attention, out_ref[t], ((1,), (0,))).astype(BF)
    lane = lax.broadcasted_iota(jnp.int32, (rows, PAD), 1)
    ones = jnp.where(lane == EXPERTS, 1.0, 0.0).astype(BF)
    tail_ref[...] = (
        dot(message_ref[:, :width], grad_logits, ((0,), (0,)))
        + dot((grad_b * unit).astype(BF), ones, ((0,), (0,)))
    ).astype(BF)


def pack_kernel(
    s_ref, a_ref, grad_ref, attention_ref, mix_ref, qkv_ref, rest_ref, tail_ref, *more
):
    main_ref, tail_out_ref = more[1:]
    late = dot(a_ref[...], grad_ref[...], ((0,), (0,)))
    columns = late.shape[1]
    main_ref[:, :columns] = late.astype(BF)
    main_ref[:, columns:] = dot(attention_ref[...], mix_ref[...], ((0,), (0,))).astype(BF)
    rest = rest_ref[...].astype(F32)
    lane = lax.broadcasted_iota(jnp.int32, rest.shape, 1)
    piece = (lane == EXPERTS) | (lane == EXPERTS + 2) | (lane == EXPERTS + 4)
    gain = jnp.sum(jnp.where(piece, rest, 0.0), axis=1, keepdims=True)
    gain_grad = jnp.sum(late * qkv_ref[...].astype(F32), axis=1, keepdims=True) / gain
    tail = tail_ref[...].astype(F32)
    tail_out_ref[...] = jnp.where(lane == EXPERTS + 1, gain_grad, tail).astype(BF)


def final_kernel(s_ref, rows_ref, qkv_ref, grad_mid_ref, x_ref, gains_ref, out_ref):
    grad_a = dot(rows_ref[0], qkv_ref[0], ((1,), (1,)))
    for t in range(1, rows_ref.shape[0]):
        grad_a += dot(rows_ref[t], qkv_ref[t], ((1,), (1,)))
    unit, inverse = normalize(x_ref[...].astype(F32))
    out_ref[...] = (
        grad_mid_ref[...] + norm_backward(grad_a * gains_ref[0:1], unit, inverse)
    ).astype(BF)


def body(
    ring,
    tensors,
    tokens,
    cotangent,
    routes,
    norm_gains,
    gains_moment,
    gains_second,
    query_weight,
    query_moment,
    query_second,
    keyval_weight,
    keyval_moment,
    keyval_second,
    output_weight,
    output_moment,
    output_second,
    router_weight,
    router_moment,
    router_second,
    gateup_weight,
    gateup_moment,
    gateup_second,
    down_weight,
    down_moment,
    down_second,
):
    length, width = tokens.shape
    rows = length // tensors
    experts = gateup_weight.shape[0]
    shape = jax.ShapeDtypeStruct
    lane_t = lax.axis_index("tensor").astype(jnp.int32).reshape(1)
    own_block = pl.BlockSpec((rows, width), lambda g, s: (s[0], 0))
    chips = tensors // 2

    shard = jnp.stack(
        [gateup_weight[:, 0], gateup_weight[:, 1], jnp.swapaxes(down_weight, 1, 2)]
    ).astype(BF)
    weight_pieces = [shard] + [
        lax.ppermute(shard, "tensor", tensor_perm(tensors, -step, 0)) for step in range(1, chips)
    ]

    q_cols = query_weight.shape[1]
    k_cols = keyval_weight.shape[2]
    o_cols = output_weight.shape[0]
    heads_cols = q_cols + 2 * k_cols
    packed = jnp.concatenate(
        [
            query_weight.astype(BF),
            keyval_weight[0].astype(BF),
            keyval_weight[1].astype(BF),
            output_weight.T.astype(BF),
            router_weight.astype(BF),
        ]
        + split_pieces(norm_gains.T, 3)
        + [jnp.zeros((query_weight.shape[0], PAD - EXPERTS - 6), BF)],
        axis=1,
    )
    packed_blocks = ring_gather(packed, ring)
    offsets = sorted(packed_blocks)
    cosine_table, sine_table = rope_tables(length, HD)
    cosine_table = jnp.concatenate([cosine_table] * 4, axis=1)
    sine_table = jnp.concatenate([-sine_table, sine_table] * 2, axis=1)
    qkv_low, out_low, rest = place(
        [packed_blocks[o] for o in offsets],
        jnp.stack([ring_index(ring, o) for o in offsets]).astype(jnp.int32),
        cuts=[
            (0, heads_cols),
            (heads_cols, heads_cols + o_cols),
            (heads_cols + o_cols, heads_cols + o_cols + PAD),
        ],
        after=[cosine_table, sine_table],
    )
    gains_all = (
        rest[:, EXPERTS : EXPERTS + 2].astype(F32)
        + rest[:, EXPERTS + 2 : EXPERTS + 4].astype(F32)
        + rest[:, EXPERTS + 4 : EXPERTS + 6].astype(F32)
    ).T
    dy_own = lax.dynamic_slice_in_dim(cotangent, lane_t[0] * rows, rows, axis=0)
    dy_all = lax.all_gather(dy_own, "expert", axis=0, tiled=True)
    a, rotated, mixture = call_whole(
        functools.partial(front_kernel, q_cols, k_cols),
        [shape((length, width), BF), shape((length, heads_cols), BF), shape((length, q_cols), BF)],
        [tokens, gains_all, qkv_low, cosine_table, sine_table],
        "attention_forward",
        cost=10**10,
    )

    mixture_rows = lax.all_to_all(
        mixture.reshape(tensors, rows, o_cols), "tensor", split_axis=0, concat_axis=0, tiled=True
    )
    owners_t = tensor_index(tensors)
    weight_pieces += [
        lax.ppermute(piece, "tensor", tensor_perm(tensors, 0, 1))
        for piece in [shard] + [hold(piece, [mixture_rows]) for piece in weight_pieces[1:]]
    ]
    expert_low = jnp.concatenate(weight_pieces, axis=3)
    out_pieces = tensor_gather(out_low, tensors, after=[mixture_rows])
    out_all = place(out_pieces, owners_t, after=[mixture_rows]).reshape(tensors, width, o_cols)
    message, x_mid = call_whole(
        middle_kernel,
        [shape((rows, width + PAD), BF), shape((rows, width), F32)],
        [mixture_rows, out_all, tokens, routes, gains_all, rest] + weight_pieces[1:chips],
        "middle",
        scalars=lane_t,
        specs={
            2: own_block,
            3: pl.BlockSpec((rows, routes.shape[1]), lambda g, s: (s[0], 0)),
            **{5 + i: pl.BlockSpec(memory_space=pl.ANY) for i in range(1, chips)},
        },
        cost=10**9,
    )
    blocks = {0: message}

    def next_hop(hop, after):
        for sign, last in ((-1, ring // 2), (1, (ring - 1) // 2)):
            if hop <= last:
                block = blocks[sign * (hop - 1)]
                block = hold(block, after) if after else block
                blocks[sign * hop] = lax.ppermute(block, "expert", ring_perm(ring, -sign))

    next_hop(1, [])
    next_hop(2, [])

    half = ring // 2
    first = (lax.axis_index("expert") * experts).astype(jnp.int32)
    calls = [[0]] + [[-k, k] for k in range(1, half - 1)] + [[-half, half - 1], [1 - half]]
    back = {}
    forth = {}
    grads = []
    scaled = []
    order = []
    spots = []
    for number, call in enumerate(calls):
        hop = min(number + 1, half)
        after = [blocks[o] for o in (-hop, hop) if o in blocks and o not in call]
        after += scaled[-1:]
        owners = [ring_index(ring, o).astype(jnp.int32) * min(abs(o), 1) for o in call]
        result = expert_blocks(
            first,
            [blocks[o] for o in call],
            owners,
            [dy_own if o == 0 else dy_all for o in call],
            expert_low,
            after,
        )
        grads.append(result[0])
        scaled.append(result[1])
        next_hop(number + 3, [result[1]])
        for part, o in enumerate(call):
            forth[o], back[o] = result[2][part], result[3][part]
            order.append(o)
            spots.append((number, part, rows))

    still = jnp.zeros((ring,), jnp.int32)
    whose = jnp.stack([ring_index(ring, o) for o in order]).astype(jnp.int32)
    messages = [blocks[o] for o in order]
    weights = {}
    totals = {}

    def beside(hop, sent):
        kind = max(hop - 1, 0)
        if hop > 3 or kind in weights:
            return []
        if kind == 0:
            weights[0] = weight_grad([dy_all] * ring, whose, spots, scaled, 0, True, tensors, sent[:1])
        else:
            weights[kind] = weight_grad(
                messages, still, spots, grads, kind - 1, False, tensors, sent[:1]
            )
        early = [totals[done][-1] for done in totals]
        totals[kind] = core_sums(weights[kind], tensors)
        return [weights[kind][0]] + early

    (returned, forward), after = ring_reduce(lambda offset: [back[offset], forth[offset]], ring, beside)
    moe_sum = sum(term.astype(F32) for term in forward)
    sums = {kind: chip_sums(total, tensors) for kind, total in totals.items()}
    after = after + [sums[2][-1]]
    block_out = place(tensor_gather((x_mid + moe_sum).astype(BF), tensors), owners_t)

    grad_mid, grad_attention, grad_mixture, tail = call_whole(
        functools.partial(middle_back_kernel, len(returned)),
        [
            shape((rows, width), F32),
            shape((rows, width), BF),
            shape((tensors, rows, o_cols), BF),
            shape((width, PAD), BF),
        ],
        returned + [x_mid, message, cotangent, gains_all, rest, out_all] + after,
        "middle_backward",
        scalars=lane_t,
        specs={
            len(returned) + 2: own_block,
            **{
                len(returned) + 6 + i: pl.BlockSpec(memory_space=pl.ANY) for i in range(len(after))
            },
        },
        cost=10**9,
    )
    grad_mixture = lax.all_to_all(
        grad_mixture, "tensor", split_axis=0, concat_axis=0, tiled=True
    ).reshape(length, o_cols)
    grad_attention_all = place(tensor_gather(grad_attention, tensors), owners_t)
    (grad_pre,) = call_whole(
        functools.partial(attention_back_kernel, q_cols, k_cols),
        [shape((length, heads_cols), BF)],
        [rotated, grad_mixture, cosine_table, sine_table, sums[1][-1], totals[0][-1]],
        "attention_backward",
        specs={i: pl.BlockSpec(memory_space=pl.ANY) for i in (4, 5)},
        scratch=[pltpu.VMEM((length, heads_cols), F32)],
        cost=2 * 10**10,
    )
    grad_pre_rows = lax.all_to_all(
        grad_pre.reshape(tensors, rows, heads_cols), "tensor", split_axis=0, concat_axis=0, tiled=True
    )
    main, tail = call_whole(
        pack_kernel,
        [shape((width, heads_cols + o_cols), BF), shape((width, PAD), BF)],
        [a, grad_pre, grad_attention_all, mixture, qkv_low, rest, tail, sums[0][-1]],
        "pack",
        specs={7: pl.BlockSpec(memory_space=pl.ANY)},
        cost=4 * 10**9,
    )
    tail = tensor_sum(tail, tensors)
    qkv_all = lax.all_gather(hold(qkv_low, [scaled[1]]), "tensor")
    (input_grad,) = call_whole(
        final_kernel,
        [shape((rows, width), BF)],
        [grad_pre_rows, qkv_all, grad_mid, tokens, gains_all],
        "input_gradient",
        scalars=lane_t,
        specs={3: own_block},
        cost=2 * 10**9,
    )
    pieces = cut(
        main,
        tail,
        jnp.stack([ring_index(ring, o) for o in offsets]).astype(jnp.int32),
        [input_grad],
    )
    pieces = dict(zip(offsets, pieces))
    new_gateup = adamw_blocks(
        gateup_weight,
        gateup_moment,
        gateup_second,
        [sums[1], sums[2]],
    )
    new_down = [
        array[:, 0]
        for array in adamw_blocks(
            down_weight[:, None],
            down_moment[:, None],
            down_second[:, None],
            [sums[0]],
        )
    ]
    fill = {half - 1: [new_gateup[0]], half - 2: [new_down[0]]}
    (summed,), _ = ring_reduce(
        lambda offset: [pieces[offset]], ring, lambda hop, sent: fill.get(hop, [])
    )
    input_grad = place(tensor_gather(input_grad, tensors), owners_t)
    new_rest = adamw_rest(
        q_cols,
        k_cols,
        summed,
        [
            [norm_gains, gains_moment, gains_second],
            [query_weight, query_moment, query_second],
            [keyval_weight, keyval_moment, keyval_second],
            [output_weight, output_moment, output_second],
            [router_weight, router_moment, router_second],
        ],
    )

    return (block_out, input_grad) + tuple(new_rest) + tuple(new_gateup) + tuple(new_down)


def solution(mesh):
    rows = P("expert", None)
    gains = P(None, "expert")
    query = P("expert", "tensor")
    keyval = P(None, "expert", "tensor")
    output = P("tensor", "expert")
    gateup = P("expert", None, None, "tensor")
    down = P("expert", "tensor", None)
    weights = tuple(
        spec for spec in (gains, query, keyval, output, rows, gateup, down) for _ in range(3)
    )
    return jax.shard_map(
        functools.partial(body, mesh.shape["expert"], mesh.shape["tensor"]),
        mesh=mesh,
        in_specs=(rows, rows, rows) + weights,
        out_specs=(rows, rows) + weights,
        check_vma=False,
    )
```
